128 devices in a mesh: ctx: 16 (over x, z), ffn: 8 (over y, core).
Axes of the slice: x: 4, y: 4, z: 4, core: 2. Of those that a mesh axis runs over, the one named last changes fastest.
Arguments:
- queries: bfloat16 [64, 8192], P('ffn'), may hold values from -12 to 12
- key_cache: bfloat16 [64, 2048, 512], P('ffn', 'ctx'), may hold values from -12 to 12
- value_cache: bfloat16 [64, 2048, 512], P('ffn', 'ctx'), may hold values from -6 to 6
- lengths: int32 [64], P('ffn'), may hold values from 1 to 2048, as said below
- residual: bfloat16 [64, 4096], P('ffn', 'ctx'), may hold values from -24 to 24
- o_weight: bfloat16 [8192, 4096], P('ctx'), may hold values from -0.59765625 to 0.59765625
- norm_gain: float32 [4096], P('ctx'), may hold values from 0.1 to 1.9
- gate_proj: bfloat16 [64, 4096, 1536], P('ffn', 'ctx'), may hold values from -0.09375 to 0.09375
- up_proj: bfloat16 [64, 4096, 1536], P('ffn', 'ctx'), may hold values from -0.09375 to 0.09375
- down_proj: bfloat16 [64, 1536, 4096], P('ffn', None, 'ctx'), may hold values from -0.15625 to 0.15625
- expert_ids: int32 [64, 8], P('ffn'), may hold values from 0 to 63, all different within a row; in each aligned block of 8 rows (0 to 7, 8 to 15, ...) at most 2 rows name the same one
- route_weight: float32 [64, 8], P('ffn'), may hold values from 0.05 to 0.3
Outputs:
- moe_out: bfloat16 [64, 4096], P('ffn', 'ctx')
The draws below stay inside these ranges and needn't reach their ends.
Inputs may be any that keep to these rules, and one draw needn't show every extreme that they name: `lengths`: some request has all 2048 positions filled. `expert_ids`: the 8 experts of a token differ; among the 8 tokens of one index of ffn, no expert is chosen more than 2 times, a bound that some block reaches.
All inputs are finite; a program needn't handle non-finite values.
Results may differ from the reference program's by a relative error of at most 0.035.
Values may be sent and summed in bfloat16 or wider, within the bound.
A program may use at most 128 MiB of HBM per device.

```python
import math
import jax
import jax.numpy as jnp
import numpy as np
from jax import lax

D = 4096
HQ = 64
KVH = 4
HD = 128
FFH = 1536
TOP = 8
MOST = 2
R_DEV = 8
REQUESTS = 64
CONTEXT = 2048
EXPERTS = 64


def draw_queries(key, part):
    key = jax.random.fold_in(key, 5)
    first = jax.random.fold_in(key, 0)
    group = HQ // KVH
    drawn = jax.random.normal(first, (REQUESTS, KVH, group, HD), jnp.float32)
    return drawn.reshape(REQUESTS, HQ * HD).astype(jnp.bfloat16)


def draw_key_cache(key, part):
    key = jax.random.fold_in(key, 7)
    first = jax.random.fold_in(key, 0)
    drawn = jax.random.normal(first, (REQUESTS, CONTEXT, KVH, HD), jnp.float32)
    return drawn.reshape(REQUESTS, CONTEXT, KVH * HD).astype(jnp.bfloat16)


def draw_lengths(key, part):
    key = jax.random.fold_in(key, 11)
    first, second = jax.random.split(key)
    base = jax.random.randint(first, (REQUESTS,), 1, CONTEXT + 1)
    picked = jax.random.randint(second, (), 0, REQUESTS)
    return jnp.where(jnp.arange(REQUESTS) == picked, CONTEXT, base).astype(jnp.int32)


def draw_residual(key, part):
    key = jax.random.fold_in(key, 13)
    first, second = jax.random.split(key)
    columns = jnp.arange(D, dtype=jnp.float32) / D
    base = jax.random.truncated_normal(first, -4.0, 4.0, (REQUESTS, D), jnp.float32)
    rows = jnp.exp(jax.random.uniform(second, (REQUESTS, 1), jnp.float32, math.log(0.2), math.log(2.0)))
    column_scale = 0.3 * jnp.exp(math.log(10.0) * columns)
    return (base * rows * column_scale[None, :]).astype(jnp.bfloat16)


def block_scale(stream_key, shape, shards, smallest, largest):
    def one(dim, shards_of):
        steps = jax.random.uniform(jax.random.fold_in(jax.random.fold_in(stream_key, 6), dim), (shards_of,), jnp.float32, smallest / len(shards), largest / len(shards))
        return jnp.repeat(jnp.exp(steps), shape[dim] // shards_of).reshape((-1,) + (1,) * (len(shape) - dim - 1))

    loudness = one(*shards[0])
    for cut in shards[1:]:
        loudness = loudness * one(*cut)
    return loudness


def shared_out(own_key, own, number, rows, number_of, top, limit, skew):
    sequence = jax.random.permutation(own_key, number_of)
    packed, usual = shares(number_of, rows * top, limit, skew, True), shares(number_of, rows * top, limit, skew, False)
    places = jnp.arange(number_of)

    def named(tallies, rotation):
        used = int((tallies > 0).sum())
        fixed = max(1, used // 4)
        shifted = fixed + (places - fixed + rotation * (used - fixed)) % max(1, number_of - fixed)
        return jnp.zeros((number_of,), jnp.int32).at[sequence[jnp.where(places < fixed, places, shifted)]].set(jnp.asarray(tallies, jnp.int32))

    tallies = jnp.where(number % 4 == 0, named(packed, number // 4), named(usual, number - number // 4 - 1))
    mixed = jax.random.permutation(jax.random.fold_in(own, 3), number_of)
    donor, taker = mixed[0:number_of // 2 * 2:2], mixed[1:number_of // 2 * 2:2]
    slack = jnp.minimum(tallies[donor] - 1, limit - tallies[taker]) // 2
    slack = jnp.where((donor == sequence[0]) | (taker == sequence[0]) | (tallies[taker] == 0), 0, jnp.maximum(slack, 0))
    shifted = jax.random.randint(jax.random.fold_in(own, 4), (number_of // 2,), 0, 1 << 20) % (slack + 1)
    tallies = tallies.at[donor].add(-shifted).at[taker].add(shifted)
    items = jnp.searchsorted(jnp.cumsum(tallies), jnp.arange(rows * top), side="right").astype(jnp.int32)
    table = items.reshape(top, rows).T
    table = table[jax.random.permutation(jax.random.fold_in(own, 1), rows)]
    rotation = jax.random.randint(jax.random.fold_in(own, 2), (rows, 1), 0, top)
    return jnp.take_along_axis(table, (jnp.arange(top)[None, :] + rotation) % top, axis=1)


def shares(count, total, most, skew, full):
    loads = [(1 << 20) // math.isqrt(grade ** skew) + 1 for grade in range(1, count + 1)]
    largest = most if full else min(most, max(-(-total // count), total * loads[0] // sum(loads)))
    least = 1 if total - largest >= count - 1 else 0
    holding, rest = [largest] + [least] * (count - 1), total - largest - least * (count - 1)
    while rest > 0:
        movable = [i for i in range(1, count) if holding[i] < largest] or [i for i in range(1, count) if holding[i] < most]
        pool, remaining = sum([loads[i] for i in movable]), rest
        for i in movable:
            addition = min(most - holding[i], max(1, remaining * loads[i] // pool), rest)
            holding[i] = holding[i] + addition
            rest = rest - addition
    return np.array(holding)


def scatter_about(rng, dims, scale, bound, cuts=(), held_as=jnp.bfloat16):
    entries = scale * jax.random.normal(rng, dims, jnp.float32)
    if cuts:
        entries = entries * block_scale(rng, dims, cuts, -0.22, 0.18)
    return jnp.clip(entries, -bound, bound).astype(held_as)


def setup_inputs(seed: int = 0) -> dict:
    keys = jax.random.split(jax.random.key(seed), 13)
    queries = draw_queries(jax.random.fold_in(keys[12], 71), 0)
    key_cache = draw_key_cache(jax.random.fold_in(keys[12], 71), 0)
    value_cache = scatter_about(keys[2], (REQUESTS, CONTEXT, KVH * HD), 1.0, 6.0, ((0, 8), (1, 16)))
    lengths = draw_lengths(jax.random.fold_in(keys[12], 71), 0)
    residual = draw_residual(jax.random.fold_in(keys[12], 71), 0)
    o_weight = scatter_about(keys[5], (HQ * HD, D), 0.1, 0.59765625, ((0, 16),))
    norm_gain = jnp.clip(1.0 + 0.18 * jax.random.normal(keys[6], (D,), jnp.float32), 0.1, 1.9)
    gate_proj = scatter_about(keys[7], (EXPERTS, D, FFH), D ** -0.5, 0.09375, ((0, 8), (1, 16)))
    up_proj = scatter_about(keys[8], (EXPERTS, D, FFH), D ** -0.5, 0.09375, ((0, 8), (1, 16)))
    down_proj = scatter_about(keys[9], (EXPERTS, FFH, D), FFH ** -0.5, 0.15625, ((0, 8), (2, 16)))
    expert_ids_keys = jax.random.split(jax.random.fold_in(keys[10], 1), REQUESTS // R_DEV)
    expert_ids_turns = jax.random.permutation(jax.random.fold_in(keys[10], 3), REQUESTS // R_DEV)
    expert_ids = jax.vmap(lambda own, number: shared_out(jax.random.fold_in(keys[10], 2), own, number, R_DEV, EXPERTS, TOP, MOST, 2))(expert_ids_keys, expert_ids_turns).reshape((REQUESTS, TOP))
    route_weight = jnp.clip(0.05 + 0.25 * jax.random.uniform(keys[11], (REQUESTS, TOP), jnp.float32) ** block_scale(keys[11], (REQUESTS, TOP), ((0, 8),), -0.2, 0.2), 0.05, 0.3)
    return {"queries": queries, "key_cache": key_cache, "value_cache": value_cache, "lengths": lengths, "residual": residual, "o_weight": o_weight, "norm_gain": norm_gain, "gate_proj": gate_proj, "up_proj": up_proj, "down_proj": down_proj, "expert_ids": expert_ids, "route_weight": route_weight}


def attention_out(queries, key_cache, value_cache, lengths):
    requests = queries.shape[0]
    group = HQ // KVH
    query_f = queries.astype(jnp.float32).reshape(requests, KVH, group, HD)
    key_f = key_cache.astype(jnp.float32).reshape(requests, CONTEXT, KVH, HD)
    value_f = value_cache.astype(jnp.float32).reshape(requests, CONTEXT, KVH, HD)
    scores = jnp.einsum('rkgd,rckd->rkgc', query_f, key_f) * HD ** (-0.5)
    position = jnp.arange(CONTEXT, dtype=jnp.int32)
    usable = (position[None, :] < lengths[:, None])[:, None, None, :]
    masked = jnp.where(usable, scores, -1e+30)
    peak_score = lax.optimization_barrier(jnp.max(masked, axis=-1, keepdims=True))
    probs = jnp.where(usable, jnp.exp(masked - peak_score), 0.0).astype(jnp.bfloat16)
    probs_f = probs.astype(jnp.float32)
    denominator = lax.optimization_barrier(jnp.sum(probs_f, axis=-1))
    numerator = jnp.einsum('rkgc,rckd->rkgd', probs_f, value_f)
    attended = (numerator / denominator[..., None]).astype(jnp.bfloat16)
    return attended.reshape(requests, HQ * HD)

def reference(queries, key_cache, value_cache, lengths, residual, o_weight, norm_gain, gate_proj, up_proj, down_proj, expert_ids, route_weight):
    attended = attention_out(queries, key_cache, value_cache, lengths)
    projected = jnp.dot(attended, o_weight, preferred_element_type=jnp.float32)
    hidden_state = (residual.astype(jnp.float32) + projected).astype(jnp.bfloat16)
    hidden_f = hidden_state.astype(jnp.float32)
    mean_square = lax.optimization_barrier(jnp.mean(hidden_f * hidden_f, axis=-1, keepdims=True))
    normed = (hidden_f * lax.rsqrt(mean_square + 1e-06) * norm_gain).astype(jnp.bfloat16)
    experts_all = gate_proj.shape[0]
    chosen = (expert_ids[:, :, None] == jnp.arange(experts_all, dtype=jnp.int32)[None, None, :]).astype(jnp.float32)
    combine_map = lax.optimization_barrier(jnp.sum(chosen * route_weight[:, :, None], axis=1))

    def expert_step(running, index):
        gate = jnp.dot(normed, gate_proj[index], preferred_element_type=jnp.float32)
        upward = jnp.dot(normed, up_proj[index], preferred_element_type=jnp.float32)
        inner = (jax.nn.silu(gate) * upward).astype(jnp.bfloat16)
        result = jnp.dot(inner, down_proj[index], preferred_element_type=jnp.float32).astype(jnp.bfloat16)
        coeff = lax.dynamic_index_in_dim(combine_map, index, 1, keepdims=True)
        return (running + coeff * result.astype(jnp.float32), None)
    start_sum = jnp.zeros((normed.shape[0], normed.shape[1]), jnp.float32)
    mixed, _ = lax.scan(expert_step, start_sum, jnp.arange(experts_all, dtype=jnp.int32))
    return mixed.astype(jnp.bfloat16)
```

```python
import jax
import jax.numpy as jnp
from jax import lax
from jax.experimental import pallas as pl
from jax.experimental.pallas import tpu as pltpu
from jax.sharding import PartitionSpec as P

D = 4096
HQ = 64
KVH = 4
HD = 128
FFH = 1536
MOST = 2
CTX = 16
SIDE = 4
FFN = 8
R = 8
E_LOC = 8
SLOTS = FFN * MOST
GROUPS = 2
PER = E_LOC // GROUPS
QUARTER = FFH // SIDE
COLS = D // CTX
LOGICAL = pl.DeviceIdType.LOGICAL
F32 = jnp.float32
BF16 = jnp.bfloat16


FAR_FIRST = sorted(
    ((dx, dz) for dx in range(SIDE) for dz in range(SIDE) if (dx, dz) != (0, 0)),
    key=lambda d: -(min(d[0], SIDE - d[0]) + min(d[1], SIDE - d[1])),
)
FFN_FIRST = (4, 5, 3, 2, 6, 7, 1)
OTHERS = (2, 1, 3)
BLOCKS = (2, 1, 3, 0)
HALVES = ((2, 1), (3, 0))


def kernel(
    len_hbm, res_hbm, gain_hbm, ids_hbm, route_hbm,
    q_hbm, k_hbm, v_hbm, o_hbm, g_hbm, u_hbm, d_hbm,
    out,
    lengths, residual, gain, ids, route,
    q_v, k_v, v_v, o_v, gu_v, d_v,
    send_a, recv_a, send_b, recv_b, recv_c, recv_r, recv_s,
    send_1, passing, behind, own_1, recv_1, send_2, recv_2, recv_e, send_f,
    pick, weigh, rows, results, partly,
    in_sem, kv_sem, o_sem, w_sem, send_sem, recv_sem, line_recv,
):
    cx = lax.axis_index("ctx")
    fx = lax.axis_index("ffn")
    sx = cx // SIDE
    sz = lax.rem(cx, SIDE)

    turn_x = [lax.rem(sx + step, SIDE) for step in range(SIDE)]
    turn_z = [lax.rem(sz + step, SIDE) for step in range(SIDE)]
    number_x = [x * (SIDE * FFN) for x in turn_x]
    number_z = [z * FFN + fx for z in turn_z]
    number_f = [cx * FFN + lax.rem(fx + step, FFN) for step in range(FFN)]

    def every_ffn(visit):
        for step in FFN_FIRST:
            visit(number_f[step])

    def place(g):
        return (sx, sz) if g == 0 else (sz, sx)

    def turn(g, step):
        return turn_x[step] if g == 0 else turn_z[step]

    def first_line(g, step):
        return number_x[step] + number_z[0] if g == 0 else number_x[0] + number_z[step]

    def second_line(g, step):
        return first_line(1 - g, step)

    def settle(ref, sem):
        pltpu.make_async_copy(ref, ref, sem).wait()

    def push(src, dst, phase, to, recv=None):
        pltpu.make_async_remote_copy(
            src_ref=src, dst_ref=dst, send_sem=send_sem.at[phase],
            recv_sem=recv_sem.at[phase] if recv is None else recv,
            device_id=to, device_id_type=LOGICAL,
        ).start()

    barrier = pltpu.get_barrier_semaphore()

    def greet(to):
        pl.semaphore_signal(barrier, inc=1, device_id=to, device_id_type=LOGICAL)

    pairs = [
        (q_hbm, q_v), (len_hbm, lengths),
        (ids_hbm, ids), (route_hbm, route), (res_hbm, residual), (gain_hbm, gain),
    ]
    first = [pltpu.make_async_copy(src, dst, in_sem.at[n]) for n, (src, dst) in enumerate(pairs)]
    for copy in first[:4]:
        copy.start()
    kv_copies = []
    for n, step in enumerate(BLOCKS):
        k = turn_x[step]
        span = pl.ds(pl.multiple_of(k * HD, HD), HD)
        kv_copies.append(
            (
                pltpu.make_async_copy(k_hbm.at[:, :, span], k_v.at[n], kv_sem.at[0, n]),
                pltpu.make_async_copy(v_hbm.at[:, :, span], v_v.at[n], kv_sem.at[1, n]),
            )
        )
        for copy in kv_copies[n]:
            copy.start()
    for copy in first[4:]:
        copy.start()
    for dx, dz in FAR_FIRST:
        greet(number_x[dx] + number_z[dz])
    every_ffn(greet)
    o_copies = [
        pltpu.make_async_copy(
            o_hbm.at[pl.ds(n * 128, 128)], o_v.at[pl.ds(n * 128, 128)], o_sem.at[n]
        )
        for n in range(4)
    ]

    for copy in o_copies:
        copy.start()

    def fetch(n, carry):
        for g in range(GROUPS):
            e = g * PER + lax.rem(place(g)[0] + SIDE - 1 - n, SIDE)
            pltpu.make_async_copy(g_hbm.at[e], gu_v.at[e, :, 0:FFH], w_sem.at[0, e]).start()
            pltpu.make_async_copy(u_hbm.at[e], gu_v.at[e, :, FFH:], w_sem.at[1, e]).start()
        return carry

    def fetch_down(e, carry):
        pltpu.make_async_copy(d_hbm.at[e], d_v.at[e], w_sem.at[2, e]).start()
        return carry


    lane8 = lax.broadcasted_iota(jnp.int32, (R, 128), 1)
    sub8 = lax.broadcasted_iota(jnp.int32, (R, 128), 0)
    filled = jnp.zeros((R, 128), jnp.int32)
    row_r = lax.broadcasted_iota(jnp.int32, (128, 128), 0) & 7
    lane_full = lax.broadcasted_iota(jnp.int32, (1, 4, R, 128), 3)
    head4 = lax.broadcasted_iota(jnp.int32, (1, 4, R, 128), 1)
    first[2].wait()
    first[3].wait()
    table = jnp.zeros((R, 128), F32)
    ids_f = ids[...].astype(F32)
    route_f = route[...]
    for k in range(8):
        table = jnp.where(lane8 == k, ids_f[:, k : k + 1], table)
        table = jnp.where(lane8 == 8 + k, route_f[:, k : k + 1], table)
    recv_r[fx] = table
    first[1].wait()
    for r in range(R):
        filled = jnp.where(sub8 == r, lengths[r], filled)
    usable = ((cx * 128 + lane8) < filled)[None]
    first[0].wait()

    def attend(n, k):
        part = q_v[:, pl.ds(pl.multiple_of(k * 16 * HD, 16 * HD), 16 * HD)].astype(F32)
        queries = jnp.concatenate(
            [part[:, g * HD : (g + 1) * HD] for g in range(16)], axis=0
        ).astype(BF16)
        every = lax.dot_general(
            queries, k_v[n].reshape(R * 128, HD), (((1,), (1,)), ((), ())),
            preferred_element_type=F32,
        )
        scores = every[:, 0:128]
        for r in range(1, R):
            scores = jnp.where(row_r == r, every[:, r * 128 : (r + 1) * 128], scores)
        scores = (scores * HD ** (-0.5)).reshape(16, R, 128)
        peak = jnp.max(jnp.where(usable, scores, -1e30), axis=-1, keepdims=True)
        peak = peak.astype(BF16).astype(F32)
        probs = jnp.where(usable, jnp.exp(scores - peak), 0.0)
        probs = probs.astype(BF16).astype(F32)
        total = jnp.sum(probs, axis=-1, keepdims=True)
        flat = probs.reshape(128, 128)
        spread = jnp.concatenate(
            [jnp.where(row_r == r, flat, 0.0).astype(BF16) for r in range(R)], axis=1
        )
        numerator = jnp.dot(spread, v_v[n].reshape(R * 128, HD), preferred_element_type=F32)
        send_a[pl.ds(k * 4, 4), 0:4] = numerator.reshape(4, 4, R, HD).astype(BF16)
        peak4 = jnp.broadcast_to(peak, (16, R, 128)).reshape(4, 4, R, 128)
        total4 = jnp.broadcast_to(total, (16, R, 128)).reshape(4, 4, R, 128)
        high = total4.astype(BF16).astype(F32)
        marks = jnp.sum(
            jnp.where(lane_full == head4, peak4, 0.0)
            + jnp.where(lane_full == head4 + 4, high, 0.0)
            + jnp.where(lane_full == head4 + 8, total4 - high, 0.0),
            axis=1,
        )
        send_a[pl.ds(k * 4, 4), 4] = marks.astype(BF16)

    for n, half in enumerate(HALVES):
        for copy in kv_copies[2 * n] + kv_copies[2 * n + 1]:
            copy.wait()
        for m, step in enumerate(half):
            attend(2 * n + m, turn_x[step])
        if n == 0:
            pl.semaphore_wait(barrier, CTX - 1 + FFN - 1)
            every_ffn(lambda to: push(recv_r.at[fx], recv_r.at[fx], 1, to))
        for step in half:
            for z in OTHERS + ((0,) if step else ()):
                to = turn_x[step] * SIDE + turn_z[z]
                push(send_a.at[to], recv_a.at[cx], 0, number_x[step] + number_z[z])
    recv_a[cx] = send_a[cx]
    lax.fori_loop(0, PER, fetch, 0)
    lax.fori_loop(0, E_LOC, fetch_down, 0)

    settle(recv_r.at[pl.ds(0, FFN - 1)], recv_sem.at[1])
    tables = recv_r[...].reshape(FFN * R, 128)
    lane = lax.broadcasted_iota(jnp.int32, (FFN * R, 128), 1)
    token = lax.broadcasted_iota(jnp.int32, (FFN * R, 128), 0)
    expert = (fx * E_LOC + (lane >> 4)).astype(F32)
    chosen = jnp.zeros((FFN * R, 128), F32)
    weight = jnp.zeros((FFN * R, 128), F32)
    for k in range(8):
        hit = tables[:, k : k + 1] == expert
        chosen = jnp.where(hit, 1.0, chosen)
        weight = jnp.where(hit, tables[:, 8 + k : 9 + k], weight)
    row = lax.broadcasted_iota(jnp.int32, (64, 64), 0)
    col = lax.broadcasted_iota(jnp.int32, (64, 64), 1)
    before = jnp.where((col < row) & ((col >> 3) == (row >> 3)), 1.0, 0.0).astype(BF16)
    rank = jnp.dot(before, chosen.astype(BF16), preferred_element_type=F32)
    here = (
        (chosen > 0.5)
        & (rank == (lane & 1).astype(F32))
        & ((token >> 3) == ((lane & 15) >> 1))
    )
    here_f = jnp.where(here, 1.0, 0.0)
    padded = jnp.concatenate([here_f, jnp.zeros((64, 128), F32)], axis=0)
    pick[...] = jnp.transpose(padded).astype(BF16)
    weight = jnp.where(here, weight, 0.0)
    high = weight.astype(BF16)
    weigh[0:64] = high
    weigh[64:128] = (weight - high.astype(F32)).astype(BF16)

    settle(recv_a.at[pl.ds(0, CTX - 1)], recv_sem.at[0])
    got = recv_a[...].astype(F32)
    marks = got[:, 4]
    factor = jnp.exp(marks - jnp.max(marks, axis=0, keepdims=True))
    share = pltpu.roll(marks, 124, 2) + pltpu.roll(marks, 120, 2)
    below = jnp.sum(factor * share, axis=0)
    heads = []
    for h in range(4):
        top = jnp.zeros((R, HD), F32)
        for c in range(CTX):
            top = top + factor[c, :, h : h + 1] * got[c, h]
        heads.append(top / below[:, h : h + 1])
    attended = jnp.concatenate(heads, axis=1).astype(BF16)

    for copy in o_copies:
        copy.wait()
    for half in HALVES:
        for step in half:
            block = turn_x[step]
            span = pl.ds(pl.multiple_of(block * 1024, 1024), 1024)
            projected = jnp.dot(attended, o_v[:, span], preferred_element_type=F32)
            for z in range(SIDE):
                left, right = projected[:, z * 256 : z * 256 + 128], projected[:, z * 256 + 128 : z * 256 + 256]
                send_b[block * SIDE + z] = jnp.concatenate([left, right], axis=0).astype(BF16)
        for step in half:
            for z in OTHERS + ((0,) if step else ()):
                to = turn_x[step] * SIDE + turn_z[z]
                push(send_b.at[to], recv_b.at[cx], 2, number_x[step] + number_z[z])
    recv_b[cx] = send_b[cx]

    def weights_here(e, carry):
        pltpu.make_async_copy(g_hbm.at[e], gu_v.at[e, :, 0:FFH], w_sem.at[0, e]).wait()
        pltpu.make_async_copy(u_hbm.at[e], gu_v.at[e, :, FFH:], w_sem.at[1, e]).wait()
        return carry

    first[4].wait()
    first[5].wait()
    res = residual[...].astype(F32)
    res = jnp.concatenate([res[:, 0:128], res[:, 128:256]], axis=0)
    settle(recv_b.at[pl.ds(0, CTX - 1)], recv_sem.at[2])
    hidden = res + jnp.sum(recv_b[...].astype(F32), axis=0)
    recv_c[fx] = hidden.astype(BF16)
    every_ffn(lambda to: push(recv_c.at[fx], recv_c.at[fx], 3, to))
    lax.fori_loop(0, E_LOC, weights_here, 0)
    settle(recv_c.at[pl.ds(0, FFN - 1)], recv_sem.at[3])
    tokens = recv_c[...].astype(F32)
    left = tokens[:, 0:8, :].reshape(64, 128)
    right = tokens[:, 8:16, :].reshape(64, 128)
    gained = jnp.concatenate([left * gain[:, 0:128], right * gain[:, 128:256]], axis=1)
    gained = jnp.concatenate([gained, jnp.zeros((64, 256), F32)], axis=0).astype(BF16)
    rows[...] = (
        jnp.dot(pick[...], gained, preferred_element_type=F32)
        .astype(BF16)
        .reshape(E_LOC, SLOTS, COLS)
    )

    def share_squares():
        squares = jnp.sum(left * left + right * right, axis=1, keepdims=True).reshape(FFN, R, 1)
        squares = jnp.broadcast_to(squares, (FFN, R, 128))
        block = lax.broadcasted_iota(jnp.int32, (FFN, R, 128), 0)
        lanes = lax.broadcasted_iota(jnp.int32, (FFN, R, 128), 2)
        recv_s[0, sx] = jnp.sum(jnp.where(lanes == block, squares, 0.0), axis=0)
        for step in OTHERS:
            push(recv_s.at[0, sx], recv_s.at[0, sx], 6, first_line(0, step))

    def gate_up(g, step):
        e = g * PER + turn(g, step)
        both = jnp.dot(rows[e], gu_v[e], preferred_element_type=F32)
        return both[:, 0:FFH], both[:, FFH:]

    for g in range(GROUPS):
        gate, upward = gate_up(g, 2)
        send_1[g, 4] = gate.astype(BF16)
        send_1[g, 5] = upward.astype(BF16)
    for g in range(GROUPS):
        push(send_1.at[g, 5], passing.at[g], 9 + g, first_line(g, 3))
        push(send_1.at[g, 4], recv_1.at[g, 4], 4 + g, first_line(g, 2))
    share_squares()
    for g in range(GROUPS):
        gate, upward = gate_up(g, 1)
        send_1[g, 0] = gate.astype(BF16)
        send_1[g, 1] = upward.astype(BF16)
    for g in range(GROUPS):
        push(send_1.at[g, pl.ds(0, 2)], recv_1.at[g, pl.ds(0, 2)], 4 + g, first_line(g, 1))
    for g in range(GROUPS):
        gate, behind[g] = gate_up(g, 3)
        send_1[g, 2] = gate.astype(BF16)
    for g in range(GROUPS):
        push(send_1.at[g, 2], recv_1.at[g, 2], 4 + g, first_line(g, 3))
    for g in range(GROUPS):
        own_1[g, 0], own_1[g, 1] = gate_up(g, 0)
    for g in range(GROUPS):
        settle(passing.at[g], recv_sem.at[9 + g])
        send_1[g, 3] = (behind[g] + passing[g].astype(F32)).astype(BF16)
        push(send_1.at[g, 3], recv_1.at[g, 3], 4 + g, first_line(g, 3))
    settle(recv_s.at[0, pl.ds(0, SIDE - 1)], recv_sem.at[6])
    recv_s[1, sz] = jnp.sum(recv_s[0], axis=0)
    for step in OTHERS:
        push(recv_s.at[1, sz], recv_s.at[1, sz], 12, second_line(0, step))

    for g in range(GROUPS):
        after = place(g)[1]
        settle(recv_1.at[g], recv_sem.at[4 + g])
        gate = own_1[g, 0]
        upward = own_1[g, 1]
        for c in (0, 2, 4):
            gate = gate + recv_1[g, c].astype(F32)
        for c in (1, 3):
            upward = upward + recv_1[g, c].astype(F32)
        for n in range(SIDE):
            span = slice(n * QUARTER, (n + 1) * QUARTER)
            send_2[g, n, 0:SLOTS] = gate[:, span].astype(BF16)
            send_2[g, n, SLOTS:] = upward[:, span].astype(BF16)
        for step in OTHERS:
            to = turn(1 - g, step)
            push(send_2.at[g, to], recv_2.at[g, after], 7 + g, second_line(g, step))
        recv_2[g, after] = send_2[g, after]

    settle(recv_s.at[1, pl.ds(0, SIDE - 1)], recv_sem.at[12])
    scale = lax.rsqrt(jnp.sum(recv_s[1], axis=0) * (1.0 / D) + 1e-06)
    scale = jnp.concatenate(
        [jnp.broadcast_to(scale[:, b : b + 1], (R, 128)) for b in range(FFN)]
        + [jnp.zeros((64, 128), F32)],
        axis=0,
    )
    high = scale.astype(BF16)
    split = jnp.concatenate([high, (scale - high.astype(F32)).astype(BF16)], axis=1)
    owned = [
        pick[pl.ds(pl.multiple_of((g * PER + place(g)[0]) * SLOTS, SLOTS), SLOTS), :]
        for g in range(GROUPS)
    ]
    scales = jnp.dot(jnp.concatenate(owned, axis=0), split, preferred_element_type=F32)
    scales = scales[:, 0:128] + scales[:, 128:256]
    own_scales = [
        jnp.concatenate([scales[g * SLOTS : (g + 1) * SLOTS]] * (QUARTER // 128), axis=1)
        for g in range(GROUPS)
    ]

    for g in range(GROUPS):
        settle(recv_2.at[g, pl.ds(0, SIDE - 1)], recv_sem.at[7 + g])
        both = recv_2[g, 0].astype(F32)
        for c in range(1, SIDE):
            both = both + recv_2[g, c].astype(F32)
        gate = both[0:SLOTS] * own_scales[g]
        upward = both[SLOTS:] * own_scales[g]
        inner = gate / (1.0 + jnp.exp(-gate)) * upward
        recv_e[sx, sz, g] = inner.astype(BF16)
    for dx, dz in FAR_FIRST:
        push(
            recv_e.at[sx, sz], recv_e.at[sx, sz], 13, number_x[dx] + number_z[dz], line_recv.at[sx]
        )

    def down_here(e, carry):
        pltpu.make_async_copy(d_hbm.at[e], d_v.at[e], w_sem.at[2, e]).wait()
        return carry

    lax.fori_loop(0, E_LOC, down_here, 0)
    for step in (0, 1, 3, 2):
        x = turn_x[step]
        settle(recv_e.at[0, pl.ds(0, SIDE if step else SIDE - 1)], line_recv.at[x])
        inner = jnp.concatenate([recv_e[x, q, 0] for q in range(SIDE)], axis=1)
        results[x] = jnp.dot(inner, d_v[x], preferred_element_type=F32).astype(BF16)
        span = pl.ds(pl.multiple_of(x * QUARTER, QUARTER), QUARTER)
        for n in range(PER):
            term = jnp.dot(recv_e[x, n, 1], d_v[PER + n, span, :], preferred_element_type=F32)
            if step:
                term = term + partly[n]
            if step != 2:
                partly[n] = term
            else:
                results[PER + n] = term.astype(BF16)

    found = results[...].reshape(E_LOC * SLOTS, COLS)
    mixed = jnp.dot(weigh[...], found, preferred_element_type=F32)
    mixed = mixed[0:64] + mixed[64:128]
    for b in range(FFN):
        piece = mixed[b * R : (b + 1) * R]
        send_f[b] = piece.astype(BF16)
    for step in FFN_FIRST:
        push(send_f.at[lax.rem(fx + step, FFN)], out.at[fx], 11, number_f[step])
    kept = pltpu.make_async_copy(send_f.at[fx], out.at[fx], o_sem.at[0])
    kept.start()

    settle(send_a.at[pl.ds(0, CTX - 1)], send_sem.at[0])
    settle(recv_r.at[pl.ds(0, FFN - 1)], send_sem.at[1])
    settle(send_b.at[pl.ds(0, CTX - 1)], send_sem.at[2])
    settle(recv_c.at[pl.ds(0, FFN - 1)], send_sem.at[3])
    settle(recv_s.at[0, pl.ds(0, SIDE - 1)], send_sem.at[6])
    settle(recv_s.at[1, pl.ds(0, SIDE - 1)], send_sem.at[12])
    for g in range(GROUPS):
        settle(recv_1.at[g], send_sem.at[4 + g])
        settle(passing.at[g], send_sem.at[9 + g])
        settle(send_2.at[g, pl.ds(0, SIDE - 1)], send_sem.at[7 + g])
    settle(recv_e.at[pl.ds(0, SIDE - 1)], send_sem.at[13])
    settle(recv_e.at[0, pl.ds(0, SIDE - 1)], send_sem.at[13])
    settle(send_f.at[pl.ds(0, FFN - 1)], send_sem.at[11])

    kept.wait()
    settle(out.at[pl.ds(0, FFN - 1)], recv_sem.at[11])


def local(
    queries, key_cache, value_cache, lengths, residual, o_weight, norm_gain,
    gate_proj, up_proj, down_proj, expert_ids, route_weight,
):
    anywhere = pl.BlockSpec(memory_space=pl.ANY)
    parts = pl.pallas_call(
        kernel,
        out_shape=pltpu.VMEM((FFN, R, COLS), BF16),
        in_specs=[anywhere] * 12,
        out_specs=pl.BlockSpec(memory_space=pltpu.VMEM),
        scratch_shapes=[
            pltpu.SMEM((R,), jnp.int32),
            pltpu.VMEM((R, COLS), BF16),
            pltpu.VMEM((1, COLS), F32),
            pltpu.VMEM((R, 8), jnp.int32),
            pltpu.VMEM((R, 8), F32),
            pltpu.VMEM((R, HQ * HD), BF16),
            pltpu.VMEM((KVH, R, 128, HD), BF16),
            pltpu.VMEM((KVH, R, 128, HD), BF16),
            pltpu.VMEM((HQ * HD // CTX, D), BF16),
            pltpu.VMEM((E_LOC, COLS, 2 * FFH), BF16),
            pltpu.VMEM((E_LOC, FFH, COLS), BF16),
            pltpu.VMEM((CTX, 5, R, 128), BF16),
            pltpu.VMEM((CTX, 5, R, 128), BF16),
            pltpu.VMEM((CTX, 16, 128), BF16),
            pltpu.VMEM((CTX, 16, 128), BF16),
            pltpu.VMEM((FFN, 16, 128), BF16),
            pltpu.VMEM((FFN, R, 128), F32),
            pltpu.VMEM((2, SIDE, R, 128), F32),
            pltpu.VMEM((GROUPS, 6, SLOTS, FFH), BF16),
            pltpu.VMEM((GROUPS, SLOTS, FFH), BF16),
            pltpu.VMEM((GROUPS, SLOTS, FFH), F32),
            pltpu.VMEM((GROUPS, 2, SLOTS, FFH), F32),
            pltpu.VMEM((GROUPS, 5, SLOTS, FFH), BF16),
            pltpu.VMEM((GROUPS, SIDE, 2 * SLOTS, QUARTER), BF16),
            pltpu.VMEM((GROUPS, SIDE, 2 * SLOTS, QUARTER), BF16),
            pltpu.VMEM((SIDE, SIDE, GROUPS, SLOTS, QUARTER), BF16),
            pltpu.VMEM((FFN, R, COLS), BF16),
            pltpu.VMEM((128, 128), BF16),
            pltpu.VMEM((128, 128), BF16),
            pltpu.VMEM((E_LOC, SLOTS, COLS), BF16),
            pltpu.VMEM((E_LOC, SLOTS, COLS), BF16),
            pltpu.VMEM((PER, SLOTS, COLS), F32),
            pltpu.SemaphoreType.DMA((6,)),
            pltpu.SemaphoreType.DMA((2, KVH)),
            pltpu.SemaphoreType.DMA((4,)),
            pltpu.SemaphoreType.DMA((3, E_LOC)),
            pltpu.SemaphoreType.DMA((14,)),
            pltpu.SemaphoreType.DMA((14,)),
            pltpu.SemaphoreType.DMA((SIDE,)),
        ],
        compiler_params=pltpu.CompilerParams(
            collective_id=0, has_side_effects=True, vmem_limit_bytes=56 * 2**20
        ),
        cost_estimate=pl.CostEstimate(
            flops=1_000_000_000, bytes_accessed=26_000_000, transcendentals=100_000
        ),
    )(
        lengths, residual, norm_gain.reshape(1, COLS), expert_ids, route_weight,
        queries, key_cache, value_cache, o_weight, gate_proj, up_proj, down_proj,
    )
    return jnp.sum(parts.astype(F32), axis=0).astype(BF16)


def solution(mesh):
    placed = (
        P("ffn", None),
        P("ffn", "ctx", None),
        P("ffn", "ctx", None),
        P("ffn"),
        P("ffn", "ctx"),
        P("ctx", None),
        P("ctx"),
        P("ffn", "ctx", None),
        P("ffn", "ctx", None),
        P("ffn", None, "ctx"),
        P("ffn", None),
        P("ffn", None),
    )
    return jax.shard_map(
        local, mesh=mesh, in_specs=placed, out_specs=P("ffn", "ctx"), check_vma=False
    )
```

```python
import jax
import jax.numpy as jnp
from jax import lax
from jax.experimental import pallas as pl
from jax.experimental.pallas import tpu as pltpu
from jax.sharding import PartitionSpec as P

D = 4096
HQ = 64
KVH = 4
HD = 128
FFH = 1536
MOST = 2
CTX = 16
SIDE = 4
FFN = 8
R = 8
E_LOC = 8
SLOTS = FFN * MOST
GROUPS = 2
PER = E_LOC // GROUPS
QUARTER = FFH // SIDE
COLS = D // CTX
LOGICAL = pl.DeviceIdType.LOGICAL
F32 = jnp.float32
BF16 = jnp.bfloat16


FAR_FIRST = sorted(
    ((dx, dz) for dx in range(SIDE) for dz in range(SIDE) if (dx, dz) != (0, 0)),
    key=lambda d: -(min(d[0], SIDE - d[0]) + min(d[1], SIDE - d[1])),
)
FFN_FIRST = (4, 5, 3, 2, 6, 7, 1)
OTHERS = (2, 1, 3)
BLOCKS = (2, 1, 3, 0)
HALVES = ((2, 1), (3, 0))


def kernel(
    len_hbm, res_hbm, gain_hbm, ids_hbm, route_hbm,
    q_hbm, k_hbm, v_hbm, o_hbm, g_hbm, u_hbm, d_hbm,
    out,
    lengths, residual, gain, ids, route,
    q_v, k_v, v_v, o_v, gu_v, d_v,
    send_a, recv_a, send_b, recv_b, recv_c, recv_r, recv_s,
    send_1, passing, behind, own_1, recv_1, send_2, recv_2, recv_e, send_f,
    pick, weigh, rows, results, partly,
    in_sem, kv_sem, o_sem, w_sem, send_sem, recv_sem, line_recv,
):
    cx = lax.axis_index("ctx")
    fx = lax.axis_index("ffn")
    sx = cx // SIDE
    sz = lax.rem(cx, SIDE)

    turn_x = [lax.rem(sx + step, SIDE) for step in range(SIDE)]
    turn_z = [lax.rem(sz + step, SIDE) for step in range(SIDE)]
    number_x = [x * (SIDE * FFN) for x in turn_x]
    number_z = [z * FFN + fx for z in turn_z]
    number_f = [cx * FFN + lax.rem(fx + step, FFN) for step in range(FFN)]

    def every_ffn(visit):
        for step in FFN_FIRST:
            visit(number_f[step])

    def place(g):
        return (sx, sz) if g == 0 else (sz, sx)

    def turn(g, step):
        return turn_x[step] if g == 0 else turn_z[step]

    def first_line(g, step):
        return number_x[step] + number_z[0] if g == 0 else number_x[0] + number_z[step]

    def second_line(g, step):
        return first_line(1 - g, step)

    def settle(ref, sem):
        pltpu.make_async_copy(ref, ref, sem).wait()

    def push(src, dst, phase, to, recv=None):
        pltpu.make_async_remote_copy(
            src_ref=src, dst_ref=dst, send_sem=send_sem.at[phase],
            recv_sem=recv_sem.at[phase] if recv is None else recv,
            device_id=to, device_id_type=LOGICAL,
        ).start()

    with jax.named_scope("entry"):
        barrier = pltpu.get_barrier_semaphore()

        def greet(to):
            pl.semaphore_signal(barrier, inc=1, device_id=to, device_id_type=LOGICAL)

        pairs = [
            (q_hbm, q_v), (len_hbm, lengths),
            (ids_hbm, ids), (route_hbm, route), (res_hbm, residual), (gain_hbm, gain),
        ]
        first = [pltpu.make_async_copy(src, dst, in_sem.at[n]) for n, (src, dst) in enumerate(pairs)]
        for copy in first[:4]:
            copy.start()
        kv_copies = []
        for n, step in enumerate(BLOCKS):
            k = turn_x[step]
            span = pl.ds(pl.multiple_of(k * HD, HD), HD)
            kv_copies.append(
                (
                    pltpu.make_async_copy(k_hbm.at[:, :, span], k_v.at[n], kv_sem.at[0, n]),
                    pltpu.make_async_copy(v_hbm.at[:, :, span], v_v.at[n], kv_sem.at[1, n]),
                )
            )
            for copy in kv_copies[n]:
                copy.start()
        for copy in first[4:]:
            copy.start()
        for dx, dz in FAR_FIRST:
            greet(number_x[dx] + number_z[dz])
        every_ffn(greet)
        o_copies = [
            pltpu.make_async_copy(
                o_hbm.at[pl.ds(n * 128, 128)], o_v.at[pl.ds(n * 128, 128)], o_sem.at[n]
            )
            for n in range(4)
        ]

        for copy in o_copies:
            copy.start()

        def fetch(n, carry):
            for g in range(GROUPS):
                e = g * PER + lax.rem(place(g)[0] + SIDE - 1 - n, SIDE)
                pltpu.make_async_copy(g_hbm.at[e], gu_v.at[e, :, 0:FFH], w_sem.at[0, e]).start()
                pltpu.make_async_copy(u_hbm.at[e], gu_v.at[e, :, FFH:], w_sem.at[1, e]).start()
            return carry

        def fetch_down(e, carry):
            pltpu.make_async_copy(d_hbm.at[e], d_v.at[e], w_sem.at[2, e]).start()
            return carry


        lane8 = lax.broadcasted_iota(jnp.int32, (R, 128), 1)
        sub8 = lax.broadcasted_iota(jnp.int32, (R, 128), 0)
        filled = jnp.zeros((R, 128), jnp.int32)
        row_r = lax.broadcasted_iota(jnp.int32, (128, 128), 0) & 7
        lane_full = lax.broadcasted_iota(jnp.int32, (1, 4, R, 128), 3)
        head4 = lax.broadcasted_iota(jnp.int32, (1, 4, R, 128), 1)
        first[2].wait()
        first[3].wait()
        table = jnp.zeros((R, 128), F32)
        ids_f = ids[...].astype(F32)
        route_f = route[...]
        for k in range(8):
            table = jnp.where(lane8 == k, ids_f[:, k : k + 1], table)
            table = jnp.where(lane8 == 8 + k, route_f[:, k : k + 1], table)
        recv_r[fx] = table
        first[1].wait()
        for r in range(R):
            filled = jnp.where(sub8 == r, lengths[r], filled)
        usable = ((cx * 128 + lane8) < filled)[None]
        first[0].wait()

        def attend(n, k):
            part = q_v[:, pl.ds(pl.multiple_of(k * 16 * HD, 16 * HD), 16 * HD)].astype(F32)
            queries = jnp.concatenate(
                [part[:, g * HD : (g + 1) * HD] for g in range(16)], axis=0
            ).astype(BF16)
            every = lax.dot_general(
                queries, k_v[n].reshape(R * 128, HD), (((1,), (1,)), ((), ())),
                preferred_element_type=F32,
            )
            scores = every[:, 0:128]
            for r in range(1, R):
                scores = jnp.where(row_r == r, every[:, r * 128 : (r + 1) * 128], scores)
            scores = (scores * HD ** (-0.5)).reshape(16, R, 128)
            peak = jnp.max(jnp.where(usable, scores, -1e30), axis=-1, keepdims=True)
            peak = peak.astype(BF16).astype(F32)
            probs = jnp.where(usable, jnp.exp(scores - peak), 0.0)
            probs = probs.astype(BF16).astype(F32)
            total = jnp.sum(probs, axis=-1, keepdims=True)
            flat = probs.reshape(128, 128)
            spread = jnp.concatenate(
                [jnp.where(row_r == r, flat, 0.0).astype(BF16) for r in range(R)], axis=1
            )
            numerator = jnp.dot(spread, v_v[n].reshape(R * 128, HD), preferred_element_type=F32)
            send_a[pl.ds(k * 4, 4), 0:4] = numerator.reshape(4, 4, R, HD).astype(BF16)
            peak4 = jnp.broadcast_to(peak, (16, R, 128)).reshape(4, 4, R, 128)
            total4 = jnp.broadcast_to(total, (16, R, 128)).reshape(4, 4, R, 128)
            high = total4.astype(BF16).astype(F32)
            marks = jnp.sum(
                jnp.where(lane_full == head4, peak4, 0.0)
                + jnp.where(lane_full == head4 + 4, high, 0.0)
                + jnp.where(lane_full == head4 + 8, total4 - high, 0.0),
                axis=1,
            )
            send_a[pl.ds(k * 4, 4), 4] = marks.astype(BF16)

    with jax.named_scope("attention"):
        for pair in kv_copies:
            for copy in pair:
                copy.wait()
        for n, step in enumerate(BLOCKS):
            attend(n, turn_x[step])

    with jax.named_scope("attention_sends"):
        pl.semaphore_wait(barrier, CTX - 1 + FFN - 1)
        for step in BLOCKS:
            for z in OTHERS + ((0,) if step else ()):
                to = turn_x[step] * SIDE + turn_z[z]
                push(send_a.at[to], recv_a.at[cx], 0, number_x[step] + number_z[z])
        every_ffn(lambda to: push(recv_r.at[fx], recv_r.at[fx], 1, to))
        recv_a[cx] = send_a[cx]
        lax.fori_loop(0, PER, fetch, 0)
        lax.fori_loop(0, E_LOC, fetch_down, 0)

    with jax.named_scope("routing"):
        settle(recv_r.at[pl.ds(0, FFN - 1)], recv_sem.at[1])
        tables = recv_r[...].reshape(FFN * R, 128)
        lane = lax.broadcasted_iota(jnp.int32, (FFN * R, 128), 1)
        token = lax.broadcasted_iota(jnp.int32, (FFN * R, 128), 0)
        expert = (fx * E_LOC + (lane >> 4)).astype(F32)
        chosen = jnp.zeros((FFN * R, 128), F32)
        weight = jnp.zeros((FFN * R, 128), F32)
        for k in range(8):
            hit = tables[:, k : k + 1] == expert
            chosen = jnp.where(hit, 1.0, chosen)
            weight = jnp.where(hit, tables[:, 8 + k : 9 + k], weight)
        row = lax.broadcasted_iota(jnp.int32, (64, 64), 0)
        col = lax.broadcasted_iota(jnp.int32, (64, 64), 1)
        before = jnp.where((col < row) & ((col >> 3) == (row >> 3)), 1.0, 0.0).astype(BF16)
        rank = jnp.dot(before, chosen.astype(BF16), preferred_element_type=F32)
        here = (
            (chosen > 0.5)
            & (rank == (lane & 1).astype(F32))
            & ((token >> 3) == ((lane & 15) >> 1))
        )
        here_f = jnp.where(here, 1.0, 0.0)
        padded = jnp.concatenate([here_f, jnp.zeros((64, 128), F32)], axis=0)
        pick[...] = jnp.transpose(padded).astype(BF16)
        weight = jnp.where(here, weight, 0.0)
        high = weight.astype(BF16)
        weigh[0:64] = high
        weigh[64:128] = (weight - high.astype(F32)).astype(BF16)

    with jax.named_scope("attention_wait"):
        settle(recv_a.at[pl.ds(0, CTX - 1)], recv_sem.at[0])

    with jax.named_scope("attention_combine"):
        got = recv_a[...].astype(F32)
        marks = got[:, 4]
        factor = jnp.exp(marks - jnp.max(marks, axis=0, keepdims=True))
        share = pltpu.roll(marks, 124, 2) + pltpu.roll(marks, 120, 2)
        below = jnp.sum(factor * share, axis=0)
        heads = []
        for h in range(4):
            top = jnp.zeros((R, HD), F32)
            for c in range(CTX):
                top = top + factor[c, :, h : h + 1] * got[c, h]
            heads.append(top / below[:, h : h + 1])
        attended = jnp.concatenate(heads, axis=1).astype(BF16)

        for copy in o_copies:
            copy.wait()

    with jax.named_scope("projection"):
        for half in HALVES:
            for step in half:
                block = turn_x[step]
                span = pl.ds(pl.multiple_of(block * 1024, 1024), 1024)
                projected = jnp.dot(attended, o_v[:, span], preferred_element_type=F32)
                for z in range(SIDE):
                    left, right = projected[:, z * 256 : z * 256 + 128], projected[:, z * 256 + 128 : z * 256 + 256]
                    send_b[block * SIDE + z] = jnp.concatenate([left, right], axis=0).astype(BF16)
            for step in half:
                for z in OTHERS + ((0,) if step else ()):
                    to = turn_x[step] * SIDE + turn_z[z]
                    push(send_b.at[to], recv_b.at[cx], 2, number_x[step] + number_z[z])
        recv_b[cx] = send_b[cx]

        def weights_here(e, carry):
            pltpu.make_async_copy(g_hbm.at[e], gu_v.at[e, :, 0:FFH], w_sem.at[0, e]).wait()
            pltpu.make_async_copy(u_hbm.at[e], gu_v.at[e, :, FFH:], w_sem.at[1, e]).wait()
            return carry

        first[4].wait()
        first[5].wait()
        res = residual[...].astype(F32)
        res = jnp.concatenate([res[:, 0:128], res[:, 128:256]], axis=0)

    with jax.named_scope("projection_wait"):
        settle(recv_b.at[pl.ds(0, CTX - 1)], recv_sem.at[2])

    with jax.named_scope("hidden_sends"):
        hidden = res + jnp.sum(recv_b[...].astype(F32), axis=0)
        recv_c[fx] = hidden.astype(BF16)
        every_ffn(lambda to: push(recv_c.at[fx], recv_c.at[fx], 3, to))
        lax.fori_loop(0, E_LOC, weights_here, 0)

    with jax.named_scope("hidden_wait"):
        settle(recv_c.at[pl.ds(0, FFN - 1)], recv_sem.at[3])

    with jax.named_scope("rows"):
        tokens = recv_c[...].astype(F32)
        left = tokens[:, 0:8, :].reshape(64, 128)
        right = tokens[:, 8:16, :].reshape(64, 128)
        gained = jnp.concatenate([left * gain[:, 0:128], right * gain[:, 128:256]], axis=1)
        gained = jnp.concatenate([gained, jnp.zeros((64, 256), F32)], axis=0).astype(BF16)
        rows[...] = (
            jnp.dot(pick[...], gained, preferred_element_type=F32)
            .astype(BF16)
            .reshape(E_LOC, SLOTS, COLS)
        )

        def share_squares():
            squares = jnp.sum(left * left + right * right, axis=1, keepdims=True).reshape(FFN, R, 1)
            squares = jnp.broadcast_to(squares, (FFN, R, 128))
            block = lax.broadcasted_iota(jnp.int32, (FFN, R, 128), 0)
            lanes = lax.broadcasted_iota(jnp.int32, (FFN, R, 128), 2)
            recv_s[0, sx] = jnp.sum(jnp.where(lanes == block, squares, 0.0), axis=0)
            for step in OTHERS:
                push(recv_s.at[0, sx], recv_s.at[0, sx], 6, first_line(0, step))

        def gate_up(g, step):
            e = g * PER + turn(g, step)
            both = jnp.dot(rows[e], gu_v[e], preferred_element_type=F32)
            return both[:, 0:FFH], both[:, FFH:]

    with jax.named_scope("gate_up"):
        for g in range(GROUPS):
            gate, upward = gate_up(g, 2)
            send_1[g, 4] = gate.astype(BF16)
            send_1[g, 5] = upward.astype(BF16)
        for g in range(GROUPS):
            push(send_1.at[g, 5], passing.at[g], 9 + g, first_line(g, 3))
            push(send_1.at[g, 4], recv_1.at[g, 4], 4 + g, first_line(g, 2))
        share_squares()
        for g in range(GROUPS):
            gate, upward = gate_up(g, 1)
            send_1[g, 0] = gate.astype(BF16)
            send_1[g, 1] = upward.astype(BF16)
        for g in range(GROUPS):
            push(send_1.at[g, pl.ds(0, 2)], recv_1.at[g, pl.ds(0, 2)], 4 + g, first_line(g, 1))
        for g in range(GROUPS):
            gate, behind[g] = gate_up(g, 3)
            send_1[g, 2] = gate.astype(BF16)
        for g in range(GROUPS):
            push(send_1.at[g, 2], recv_1.at[g, 2], 4 + g, first_line(g, 3))
        for g in range(GROUPS):
            own_1[g, 0], own_1[g, 1] = gate_up(g, 0)
        for g in range(GROUPS):
            settle(passing.at[g], recv_sem.at[9 + g])
            send_1[g, 3] = (behind[g] + passing[g].astype(F32)).astype(BF16)
            push(send_1.at[g, 3], recv_1.at[g, 3], 4 + g, first_line(g, 3))

    with jax.named_scope("square_sums"):
        settle(recv_s.at[0, pl.ds(0, SIDE - 1)], recv_sem.at[6])
        recv_s[1, sz] = jnp.sum(recv_s[0], axis=0)
        for step in OTHERS:
            push(recv_s.at[1, sz], recv_s.at[1, sz], 12, second_line(0, step))

    with jax.named_scope("first_sums"):
        for g in range(GROUPS):
            after = place(g)[1]
            settle(recv_1.at[g], recv_sem.at[4 + g])
            gate = own_1[g, 0]
            upward = own_1[g, 1]
            for c in (0, 2, 4):
                gate = gate + recv_1[g, c].astype(F32)
            for c in (1, 3):
                upward = upward + recv_1[g, c].astype(F32)
            for n in range(SIDE):
                span = slice(n * QUARTER, (n + 1) * QUARTER)
                send_2[g, n, 0:SLOTS] = gate[:, span].astype(BF16)
                send_2[g, n, SLOTS:] = upward[:, span].astype(BF16)
            for step in OTHERS:
                to = turn(1 - g, step)
                push(send_2.at[g, to], recv_2.at[g, after], 7 + g, second_line(g, step))
            recv_2[g, after] = send_2[g, after]

    with jax.named_scope("scales"):
        settle(recv_s.at[1, pl.ds(0, SIDE - 1)], recv_sem.at[12])
        scale = lax.rsqrt(jnp.sum(recv_s[1], axis=0) * (1.0 / D) + 1e-06)
        scale = jnp.concatenate(
            [jnp.broadcast_to(scale[:, b : b + 1], (R, 128)) for b in range(FFN)]
            + [jnp.zeros((64, 128), F32)],
            axis=0,
        )
        high = scale.astype(BF16)
        split = jnp.concatenate([high, (scale - high.astype(F32)).astype(BF16)], axis=1)
        owned = [
            pick[pl.ds(pl.multiple_of((g * PER + place(g)[0]) * SLOTS, SLOTS), SLOTS), :]
            for g in range(GROUPS)
        ]
        scales = jnp.dot(jnp.concatenate(owned, axis=0), split, preferred_element_type=F32)
        scales = scales[:, 0:128] + scales[:, 128:256]
        own_scales = [
            jnp.concatenate([scales[g * SLOTS : (g + 1) * SLOTS]] * (QUARTER // 128), axis=1)
            for g in range(GROUPS)
        ]

    with jax.named_scope("inner"):
        for g in range(GROUPS):
            settle(recv_2.at[g, pl.ds(0, SIDE - 1)], recv_sem.at[7 + g])
            both = recv_2[g, 0].astype(F32)
            for c in range(1, SIDE):
                both = both + recv_2[g, c].astype(F32)
            gate = both[0:SLOTS] * own_scales[g]
            upward = both[SLOTS:] * own_scales[g]
            inner = gate / (1.0 + jnp.exp(-gate)) * upward
            recv_e[sx, sz, g] = inner.astype(BF16)

    with jax.named_scope("inner_sends"):
        for dx, dz in FAR_FIRST:
            push(
                recv_e.at[sx, sz], recv_e.at[sx, sz], 13, number_x[dx] + number_z[dz], line_recv.at[sx]
            )

        def down_here(e, carry):
            pltpu.make_async_copy(d_hbm.at[e], d_v.at[e], w_sem.at[2, e]).wait()
            return carry

        lax.fori_loop(0, E_LOC, down_here, 0)

    with jax.named_scope("down"):
        for step in (0, 1, 3, 2):
            x = turn_x[step]
            settle(recv_e.at[0, pl.ds(0, SIDE if step else SIDE - 1)], line_recv.at[x])
            inner = jnp.concatenate([recv_e[x, q, 0] for q in range(SIDE)], axis=1)
            results[x] = jnp.dot(inner, d_v[x], preferred_element_type=F32).astype(BF16)
            span = pl.ds(pl.multiple_of(x * QUARTER, QUARTER), QUARTER)
            for n in range(PER):
                term = jnp.dot(recv_e[x, n, 1], d_v[PER + n, span, :], preferred_element_type=F32)
                if step:
                    term = term + partly[n]
                if step != 2:
                    partly[n] = term
                else:
                    results[PER + n] = term.astype(BF16)

    with jax.named_scope("mix"):
        found = results[...].reshape(E_LOC * SLOTS, COLS)
        mixed = jnp.dot(weigh[...], found, preferred_element_type=F32)
        mixed = mixed[0:64] + mixed[64:128]
        for b in range(FFN):
            piece = mixed[b * R : (b + 1) * R]
            send_f[b] = piece.astype(BF16)
        for step in FFN_FIRST:
            push(send_f.at[lax.rem(fx + step, FFN)], out.at[fx], 11, number_f[step])
        kept = pltpu.make_async_copy(send_f.at[fx], out.at[fx], o_sem.at[0])
        kept.start()

    with jax.named_scope("last_wait"):
        settle(send_a.at[pl.ds(0, CTX - 1)], send_sem.at[0])
        settle(recv_r.at[pl.ds(0, FFN - 1)], send_sem.at[1])
        settle(send_b.at[pl.ds(0, CTX - 1)], send_sem.at[2])
        settle(recv_c.at[pl.ds(0, FFN - 1)], send_sem.at[3])
        settle(recv_s.at[0, pl.ds(0, SIDE - 1)], send_sem.at[6])
        settle(recv_s.at[1, pl.ds(0, SIDE - 1)], send_sem.at[12])
        for g in range(GROUPS):
            settle(recv_1.at[g], send_sem.at[4 + g])
            settle(passing.at[g], send_sem.at[9 + g])
            settle(send_2.at[g, pl.ds(0, SIDE - 1)], send_sem.at[7 + g])
        settle(recv_e.at[pl.ds(0, SIDE - 1)], send_sem.at[13])
        settle(recv_e.at[0, pl.ds(0, SIDE - 1)], send_sem.at[13])
        settle(send_f.at[pl.ds(0, FFN - 1)], send_sem.at[11])

        kept.wait()
        settle(out.at[pl.ds(0, FFN - 1)], recv_sem.at[11])


def local(
    queries, key_cache, value_cache, lengths, residual, o_weight, norm_gain,
    gate_proj, up_proj, down_proj, expert_ids, route_weight,
):
    anywhere = pl.BlockSpec(memory_space=pl.ANY)
    parts = pl.pallas_call(
        kernel,
        out_shape=pltpu.VMEM((FFN, R, COLS), BF16),
        in_specs=[anywhere] * 12,
        out_specs=pl.BlockSpec(memory_space=pltpu.VMEM),
        scratch_shapes=[
            pltpu.SMEM((R,), jnp.int32),
            pltpu.VMEM((R, COLS), BF16),
            pltpu.VMEM((1, COLS), F32),
            pltpu.VMEM((R, 8), jnp.int32),
            pltpu.VMEM((R, 8), F32),
            pltpu.VMEM((R, HQ * HD), BF16),
            pltpu.VMEM((KVH, R, 128, HD), BF16),
            pltpu.VMEM((KVH, R, 128, HD), BF16),
            pltpu.VMEM((HQ * HD // CTX, D), BF16),
            pltpu.VMEM((E_LOC, COLS, 2 * FFH), BF16),
            pltpu.VMEM((E_LOC, FFH, COLS), BF16),
            pltpu.VMEM((CTX, 5, R, 128), BF16),
            pltpu.VMEM((CTX, 5, R, 128), BF16),
            pltpu.VMEM((CTX, 16, 128), BF16),
            pltpu.VMEM((CTX, 16, 128), BF16),
            pltpu.VMEM((FFN, 16, 128), BF16),
            pltpu.VMEM((FFN, R, 128), F32),
            pltpu.VMEM((2, SIDE, R, 128), F32),
            pltpu.VMEM((GROUPS, 6, SLOTS, FFH), BF16),
            pltpu.VMEM((GROUPS, SLOTS, FFH), BF16),
            pltpu.VMEM((GROUPS, SLOTS, FFH), F32),
            pltpu.VMEM((GROUPS, 2, SLOTS, FFH), F32),
            pltpu.VMEM((GROUPS, 5, SLOTS, FFH), BF16),
            pltpu.VMEM((GROUPS, SIDE, 2 * SLOTS, QUARTER), BF16),
            pltpu.VMEM((GROUPS, SIDE, 2 * SLOTS, QUARTER), BF16),
            pltpu.VMEM((SIDE, SIDE, GROUPS, SLOTS, QUARTER), BF16),
            pltpu.VMEM((FFN, R, COLS), BF16),
            pltpu.VMEM((128, 128), BF16),
            pltpu.VMEM((128, 128), BF16),
            pltpu.VMEM((E_LOC, SLOTS, COLS), BF16),
            pltpu.VMEM((E_LOC, SLOTS, COLS), BF16),
            pltpu.VMEM((PER, SLOTS, COLS), F32),
            pltpu.SemaphoreType.DMA((6,)),
            pltpu.SemaphoreType.DMA((2, KVH)),
            pltpu.SemaphoreType.DMA((4,)),
            pltpu.SemaphoreType.DMA((3, E_LOC)),
            pltpu.SemaphoreType.DMA((14,)),
            pltpu.SemaphoreType.DMA((14,)),
            pltpu.SemaphoreType.DMA((SIDE,)),
        ],
        compiler_params=pltpu.CompilerParams(
            collective_id=0, has_side_effects=True, vmem_limit_bytes=56 * 2**20
        ),
        cost_estimate=pl.CostEstimate(
            flops=1_000_000_000, bytes_accessed=26_000_000, transcendentals=100_000
        ),
    )(
        lengths, residual, norm_gain.reshape(1, COLS), expert_ids, route_weight,
        queries, key_cache, value_cache, o_weight, gate_proj, up_proj, down_proj,
    )
    return jnp.sum(parts.astype(F32), axis=0).astype(BF16)


def solution(mesh):
    placed = (
        P("ffn", None),
        P("ffn", "ctx", None),
        P("ffn", "ctx", None),
        P("ffn"),
        P("ffn", "ctx"),
        P("ctx", None),
        P("ctx"),
        P("ffn", "ctx", None),
        P("ffn", "ctx", None),
        P("ffn", None, "ctx"),
        P("ffn", None),
        P("ffn", None),
    )
    return jax.shard_map(
        local, mesh=mesh, in_specs=placed, out_specs=P("ffn", "ctx"), check_vma=False
    )
```

```python
import jax
import jax.numpy as jnp
from jax import lax
from jax.experimental import pallas as pl
from jax.experimental.pallas import tpu as pltpu
from jax.sharding import PartitionSpec as P

D = 4096
HQ = 64
KVH = 4
HD = 128
FFH = 1536
MOST = 2
CTX = 16
SIDE = 4
FFN = 8
R = 8
E_LOC = 8
SLOTS = FFN * MOST
GROUPS = 2
PER = E_LOC // GROUPS
QUARTER = FFH // SIDE
COLS = D // CTX
LOGICAL = pl.DeviceIdType.LOGICAL
F32 = jnp.float32
BF16 = jnp.bfloat16


FAR_FIRST = sorted(
    ((dx, dz) for dx in range(SIDE) for dz in range(SIDE) if (dx, dz) != (0, 0)),
    key=lambda d: -(min(d[0], SIDE - d[0]) + min(d[1], SIDE - d[1])),
)
FFN_FIRST = (4, 5, 3, 2, 6, 7, 1)
OTHERS = (2, 1, 3)
BLOCKS = (2, 1, 3, 0)


def kernel(
    len_hbm, res_hbm, gain_hbm, ids_hbm, route_hbm,
    q_hbm, k_hbm, v_hbm, o_hbm, g_hbm, u_hbm, d_hbm,
    out,
    lengths, residual, gain, ids, route,
    q_v, k_v, v_v, o_v, gu_v, d_v,
    send_a, recv_a, send_b, recv_b, recv_c, recv_r, recv_s,
    send_1, passing, behind, own_1, recv_1, send_2, recv_2, recv_e, send_f,
    pick, weigh, rows, results, partly,
    in_sem, kv_sem, o_sem, w_sem, send_sem, recv_sem, line_recv,
):
    cx = lax.axis_index("ctx")
    fx = lax.axis_index("ffn")
    sx = cx // SIDE
    sz = lax.rem(cx, SIDE)

    turn_x = [lax.rem(sx + step, SIDE) for step in range(SIDE)]
    turn_z = [lax.rem(sz + step, SIDE) for step in range(SIDE)]
    number_x = [x * (SIDE * FFN) for x in turn_x]
    number_z = [z * FFN + fx for z in turn_z]
    number_f = [cx * FFN + lax.rem(fx + step, FFN) for step in range(FFN)]

    def every_ffn(visit):
        for step in FFN_FIRST:
            visit(number_f[step])

    def place(g):
        return (sx, sz) if g == 0 else (sz, sx)

    def turn(g, step):
        return turn_x[step] if g == 0 else turn_z[step]

    def first_line(g, step):
        return number_x[step] + number_z[0] if g == 0 else number_x[0] + number_z[step]

    def second_line(g, step):
        return first_line(1 - g, step)

    def settle(ref, sem):
        pltpu.make_async_copy(ref, ref, sem).wait()

    def push(src, dst, phase, to, recv=None):
        pltpu.make_async_remote_copy(
            src_ref=src, dst_ref=dst, send_sem=send_sem.at[phase],
            recv_sem=recv_sem.at[phase] if recv is None else recv,
            device_id=to, device_id_type=LOGICAL,
        ).start()

    with jax.named_scope("entry"):
        barrier = pltpu.get_barrier_semaphore()

        def greet(to):
            pl.semaphore_signal(barrier, inc=1, device_id=to, device_id_type=LOGICAL)

        pairs = [
            (q_hbm, q_v), (len_hbm, lengths),
            (ids_hbm, ids), (route_hbm, route), (res_hbm, residual), (gain_hbm, gain),
        ]
        first = [pltpu.make_async_copy(src, dst, in_sem.at[n]) for n, (src, dst) in enumerate(pairs)]
        for copy in first[:4]:
            copy.start()
        kv_copies = []
        for n in range(2):
            for m, (src, dst) in enumerate(((k_hbm, k_v), (v_hbm, v_v))):
                span = pl.ds(n * (R // 2), R // 2)
                kv_copies.append(
                    pltpu.make_async_copy(src.at[span], dst.at[span], kv_sem.at[m, n])
                )
        for copy in kv_copies:
            copy.start()
        for copy in first[4:]:
            copy.start()
        for dx, dz in FAR_FIRST:
            greet(number_x[dx] + number_z[dz])
        every_ffn(greet)
        o_copies = [
            pltpu.make_async_copy(
                o_hbm.at[pl.ds(n * 128, 128)], o_v.at[pl.ds(n * 128, 128)], o_sem.at[n]
            )
            for n in range(4)
        ]

        for copy in o_copies:
            copy.start()

        def fetch(n, carry):
            for g in range(GROUPS):
                e = g * PER + lax.rem(place(g)[0] + SIDE - 1 - n, SIDE)
                pltpu.make_async_copy(g_hbm.at[e], gu_v.at[e, :, 0:FFH], w_sem.at[0, e]).start()
                pltpu.make_async_copy(u_hbm.at[e], gu_v.at[e, :, FFH:], w_sem.at[1, e]).start()
            return carry

        def fetch_down(e, carry):
            pltpu.make_async_copy(d_hbm.at[e], d_v.at[e], w_sem.at[2, e]).start()
            return carry


        lane8 = lax.broadcasted_iota(jnp.int32, (R, 128), 1)
        sub8 = lax.broadcasted_iota(jnp.int32, (R, 128), 0)
        filled = jnp.zeros((R, 128), jnp.int32)
        row_r = lax.broadcasted_iota(jnp.int32, (128, 128), 0) & 7
        lane_full = lax.broadcasted_iota(jnp.int32, (1, 4, R, 128), 3)
        head4 = lax.broadcasted_iota(jnp.int32, (1, 4, R, 128), 1)
        first[2].wait()
        first[3].wait()
        table = jnp.zeros((R, 128), F32)
        ids_f = ids[...].astype(F32)
        route_f = route[...]
        for k in range(8):
            table = jnp.where(lane8 == k, ids_f[:, k : k + 1], table)
            table = jnp.where(lane8 == 8 + k, route_f[:, k : k + 1], table)
        recv_r[fx] = table
        first[1].wait()
        for r in range(R):
            filled = jnp.where(sub8 == r, lengths[r], filled)
        usable = ((cx * 128 + lane8) < filled)[None]
        first[0].wait()

        def attend(k):
            part = q_v[:, k * 16 * HD : (k + 1) * 16 * HD].astype(F32)
            queries = jnp.concatenate(
                [part[:, g * HD : (g + 1) * HD] for g in range(16)], axis=0
            ).astype(BF16)
            every = lax.dot_general(
                queries, k_v[:, :, k * HD : (k + 1) * HD].reshape(R * 128, HD),
                (((1,), (1,)), ((), ())), preferred_element_type=F32,
            )
            scores = every[:, 0:128]
            for r in range(1, R):
                scores = jnp.where(row_r == r, every[:, r * 128 : (r + 1) * 128], scores)
            scores = (scores * HD ** (-0.5)).reshape(16, R, 128)
            peak = jnp.max(jnp.where(usable, scores, -1e30), axis=-1, keepdims=True)
            peak = peak.astype(BF16).astype(F32)
            probs = jnp.where(usable, jnp.exp(scores - peak), 0.0)
            probs = probs.astype(BF16).astype(F32)
            total = jnp.sum(probs, axis=-1, keepdims=True)
            flat = probs.reshape(128, 128)
            spread = jnp.concatenate(
                [jnp.where(row_r == r, flat, 0.0).astype(BF16) for r in range(R)], axis=1
            )
            values = v_v[:, :, k * HD : (k + 1) * HD].reshape(R * 128, HD)
            numerator = jnp.dot(spread, values, preferred_element_type=F32)
            send_a[k * 4 : (k + 1) * 4, 0:4] = numerator.reshape(4, 4, R, HD).astype(BF16)
            peak4 = jnp.broadcast_to(peak, (16, R, 128)).reshape(4, 4, R, 128)
            total4 = jnp.broadcast_to(total, (16, R, 128)).reshape(4, 4, R, 128)
            high = total4.astype(BF16).astype(F32)
            marks = jnp.sum(
                jnp.where(lane_full == head4, peak4, 0.0)
                + jnp.where(lane_full == head4 + 4, high, 0.0)
                + jnp.where(lane_full == head4 + 8, total4 - high, 0.0),
                axis=1,
            )
            send_a[k * 4 : (k + 1) * 4, 4] = marks.astype(BF16)

    with jax.named_scope("attention"):
        for copy in kv_copies:
            copy.wait()
        for k in range(KVH):
            attend(k)

    with jax.named_scope("attention_sends"):
        pl.semaphore_wait(barrier, CTX - 1 + FFN - 1)
        for step in BLOCKS:
            for z in OTHERS + ((0,) if step else ()):
                to = turn_x[step] * SIDE + turn_z[z]
                push(send_a.at[to], recv_a.at[cx], 0, number_x[step] + number_z[z])
        every_ffn(lambda to: push(recv_r.at[fx], recv_r.at[fx], 1, to))
        recv_a[cx] = send_a[cx]
        lax.fori_loop(0, PER, fetch, 0)
        lax.fori_loop(0, E_LOC, fetch_down, 0)

    with jax.named_scope("routing"):
        settle(recv_r.at[pl.ds(0, FFN - 1)], recv_sem.at[1])
        tables = recv_r[...].reshape(FFN * R, 128)
        lane = lax.broadcasted_iota(jnp.int32, (FFN * R, 128), 1)
        token = lax.broadcasted_iota(jnp.int32, (FFN * R, 128), 0)
        expert = (fx * E_LOC + (lane >> 4)).astype(F32)
        chosen = jnp.zeros((FFN * R, 128), F32)
        weight = jnp.zeros((FFN * R, 128), F32)
        for k in range(8):
            hit = tables[:, k : k + 1] == expert
            chosen = jnp.where(hit, 1.0, chosen)
            weight = jnp.where(hit, tables[:, 8 + k : 9 + k], weight)
        row = lax.broadcasted_iota(jnp.int32, (64, 64), 0)
        col = lax.broadcasted_iota(jnp.int32, (64, 64), 1)
        before = jnp.where((col < row) & ((col >> 3) == (row >> 3)), 1.0, 0.0).astype(BF16)
        rank = jnp.dot(before, chosen.astype(BF16), preferred_element_type=F32)
        here = (
            (chosen > 0.5)
            & (rank == (lane & 1).astype(F32))
            & ((token >> 3) == ((lane & 15) >> 1))
        )
        here_f = jnp.where(here, 1.0, 0.0)
        padded = jnp.concatenate([here_f, jnp.zeros((64, 128), F32)], axis=0)
        pick[...] = jnp.transpose(padded).astype(BF16)
        weight = jnp.where(here, weight, 0.0)
        high = weight.astype(BF16)
        weigh[0:64] = high
        weigh[64:128] = (weight - high.astype(F32)).astype(BF16)

    with jax.named_scope("attention_wait"):
        settle(recv_a.at[pl.ds(0, CTX - 1)], recv_sem.at[0])

    with jax.named_scope("attention_combine"):
        got = recv_a[...].astype(F32)
        marks = got[:, 4]
        factor = jnp.exp(marks - jnp.max(marks, axis=0, keepdims=True))
        share = pltpu.roll(marks, 124, 2) + pltpu.roll(marks, 120, 2)
        below = jnp.sum(factor * share, axis=0)
        heads = []
        for h in range(4):
            top = jnp.zeros((R, HD), F32)
            for c in range(CTX):
                top = top + factor[c, :, h : h + 1] * got[c, h]
            heads.append(top / below[:, h : h + 1])
        attended = jnp.concatenate(heads, axis=1).astype(BF16)

        for copy in o_copies:
            copy.wait()

    with jax.named_scope("projection"):
        projected = jnp.dot(attended, o_v[...], preferred_element_type=F32)
        for c in range(CTX):
            ahead, rest = projected[:, c * 256 : c * 256 + 128], projected[:, c * 256 + 128 : c * 256 + 256]
            send_b[c] = jnp.concatenate([ahead, rest], axis=0).astype(BF16)
        for step in BLOCKS:
            for z in OTHERS + ((0,) if step else ()):
                to = turn_x[step] * SIDE + turn_z[z]
                push(send_b.at[to], recv_b.at[cx], 2, number_x[step] + number_z[z])
        recv_b[cx] = send_b[cx]

        def weights_here(e, carry):
            pltpu.make_async_copy(g_hbm.at[e], gu_v.at[e, :, 0:FFH], w_sem.at[0, e]).wait()
            pltpu.make_async_copy(u_hbm.at[e], gu_v.at[e, :, FFH:], w_sem.at[1, e]).wait()
            return carry

        first[4].wait()
        first[5].wait()
        res = residual[...].astype(F32)
        res = jnp.concatenate([res[:, 0:128], res[:, 128:256]], axis=0)

    with jax.named_scope("projection_wait"):
        settle(recv_b.at[pl.ds(0, CTX - 1)], recv_sem.at[2])

    with jax.named_scope("hidden_sends"):
        hidden = res + jnp.sum(recv_b[...].astype(F32), axis=0)
        recv_c[fx] = hidden.astype(BF16)
        every_ffn(lambda to: push(recv_c.at[fx], recv_c.at[fx], 3, to))
        lax.fori_loop(0, E_LOC, weights_here, 0)

    with jax.named_scope("hidden_wait"):
        settle(recv_c.at[pl.ds(0, FFN - 1)], recv_sem.at[3])

    with jax.named_scope("rows"):
        tokens = recv_c[...].astype(F32)
        left = tokens[:, 0:8, :].reshape(64, 128)
        right = tokens[:, 8:16, :].reshape(64, 128)
        gained = jnp.concatenate([left * gain[:, 0:128], right * gain[:, 128:256]], axis=1)
        gained = jnp.concatenate([gained, jnp.zeros((64, 256), F32)], axis=0).astype(BF16)
        rows[...] = (
            jnp.dot(pick[...], gained, preferred_element_type=F32)
            .astype(BF16)
            .reshape(E_LOC, SLOTS, COLS)
        )

        def share_squares():
            squares = jnp.sum(left * left + right * right, axis=1, keepdims=True).reshape(FFN, R, 1)
            squares = jnp.broadcast_to(squares, (FFN, R, 128))
            block = lax.broadcasted_iota(jnp.int32, (FFN, R, 128), 0)
            lanes = lax.broadcasted_iota(jnp.int32, (FFN, R, 128), 2)
            recv_s[0, sx] = jnp.sum(jnp.where(lanes == block, squares, 0.0), axis=0)
            for step in OTHERS:
                push(recv_s.at[0, sx], recv_s.at[0, sx], 6, first_line(0, step))

        def gate_up(g, step):
            e = g * PER + turn(g, step)
            both = jnp.dot(rows[e], gu_v[e], preferred_element_type=F32)
            return both[:, 0:FFH], both[:, FFH:]

    with jax.named_scope("gate_up"):
        for g in range(GROUPS):
            gate, upward = gate_up(g, 2)
            send_1[g, 4] = gate.astype(BF16)
            send_1[g, 5] = upward.astype(BF16)
        for g in range(GROUPS):
            push(send_1.at[g, 5], passing.at[g], 9 + g, first_line(g, 3))
            push(send_1.at[g, 4], recv_1.at[g, 4], 4 + g, first_line(g, 2))
        for g in range(GROUPS):
            gate, upward = gate_up(g, 1)
            send_1[g, 0] = gate.astype(BF16)
            send_1[g, 1] = upward.astype(BF16)
            gate, behind[g] = gate_up(g, 3)
            send_1[g, 2] = gate.astype(BF16)
        for g in range(GROUPS):
            push(send_1.at[g, pl.ds(0, 2)], recv_1.at[g, pl.ds(0, 2)], 4 + g, first_line(g, 1))
            push(send_1.at[g, 2], recv_1.at[g, 2], 4 + g, first_line(g, 3))
        for g in range(GROUPS):
            own_1[g, 0], own_1[g, 1] = gate_up(g, 0)
        share_squares()
        for g in range(GROUPS):
            settle(passing.at[g], recv_sem.at[9 + g])
            send_1[g, 3] = (behind[g] + passing[g].astype(F32)).astype(BF16)
            push(send_1.at[g, 3], recv_1.at[g, 3], 4 + g, first_line(g, 3))

    with jax.named_scope("square_sums"):
        settle(recv_s.at[0, pl.ds(0, SIDE - 1)], recv_sem.at[6])
        recv_s[1, sz] = jnp.sum(recv_s[0], axis=0)
        for step in OTHERS:
            push(recv_s.at[1, sz], recv_s.at[1, sz], 12, second_line(0, step))

    with jax.named_scope("first_sums"):
        for g in range(GROUPS):
            after = place(g)[1]
            settle(recv_1.at[g], recv_sem.at[4 + g])
            gate = own_1[g, 0]
            upward = own_1[g, 1]
            for c in (0, 2, 4):
                gate = gate + recv_1[g, c].astype(F32)
            for c in (1, 3):
                upward = upward + recv_1[g, c].astype(F32)
            for n in range(SIDE):
                span = slice(n * QUARTER, (n + 1) * QUARTER)
                send_2[g, n, 0:SLOTS] = gate[:, span].astype(BF16)
                send_2[g, n, SLOTS:] = upward[:, span].astype(BF16)
            for step in OTHERS:
                to = turn(1 - g, step)
                push(send_2.at[g, to], recv_2.at[g, after], 7 + g, second_line(g, step))
            recv_2[g, after] = send_2[g, after]

    with jax.named_scope("scales"):
        settle(recv_s.at[1, pl.ds(0, SIDE - 1)], recv_sem.at[12])
        scale = lax.rsqrt(jnp.sum(recv_s[1], axis=0) * (1.0 / D) + 1e-06)
        scale = jnp.concatenate(
            [jnp.broadcast_to(scale[:, b : b + 1], (R, 128)) for b in range(FFN)]
            + [jnp.zeros((64, 128), F32)],
            axis=0,
        )
        high = scale.astype(BF16)
        split = jnp.concatenate([high, (scale - high.astype(F32)).astype(BF16)], axis=1)
        owned = [
            pick[pl.ds(pl.multiple_of((g * PER + place(g)[0]) * SLOTS, SLOTS), SLOTS), :]
            for g in range(GROUPS)
        ]
        scales = jnp.dot(jnp.concatenate(owned, axis=0), split, preferred_element_type=F32)
        scales = scales[:, 0:128] + scales[:, 128:256]
        own_scales = [
            jnp.concatenate([scales[g * SLOTS : (g + 1) * SLOTS]] * (QUARTER // 128), axis=1)
            for g in range(GROUPS)
        ]

    with jax.named_scope("inner"):
        for g in range(GROUPS):
            settle(recv_2.at[g, pl.ds(0, SIDE - 1)], recv_sem.at[7 + g])
            both = recv_2[g, 0].astype(F32)
            for c in range(1, SIDE):
                both = both + recv_2[g, c].astype(F32)
            gate = both[0:SLOTS] * own_scales[g]
            upward = both[SLOTS:] * own_scales[g]
            inner = gate / (1.0 + jnp.exp(-gate)) * upward
            recv_e[sx, sz, g] = inner.astype(BF16)

    with jax.named_scope("inner_sends"):
        for dx, dz in FAR_FIRST:
            push(
                recv_e.at[sx, sz], recv_e.at[sx, sz], 13, number_x[dx] + number_z[dz], line_recv.at[sx]
            )

        def down_here(e, carry):
            pltpu.make_async_copy(d_hbm.at[e], d_v.at[e], w_sem.at[2, e]).wait()
            return carry

        lax.fori_loop(0, E_LOC, down_here, 0)

    with jax.named_scope("down"):
        for step in (0, 1, 3, 2):
            x = turn_x[step]
            settle(recv_e.at[0, pl.ds(0, SIDE if step else SIDE - 1)], line_recv.at[x])
            inner = jnp.concatenate([recv_e[x, q, 0] for q in range(SIDE)], axis=1)
            results[x] = jnp.dot(inner, d_v[x], preferred_element_type=F32).astype(BF16)
            span = pl.ds(pl.multiple_of(x * QUARTER, QUARTER), QUARTER)
            for n in range(PER):
                term = jnp.dot(recv_e[x, n, 1], d_v[PER + n, span, :], preferred_element_type=F32)
                if step:
                    term = term + partly[n]
                if step != 2:
                    partly[n] = term
                else:
                    results[PER + n] = term.astype(BF16)

    with jax.named_scope("mix"):
        found = results[...].reshape(E_LOC * SLOTS, COLS)
        mixed = jnp.dot(weigh[...], found, preferred_element_type=F32)
        mixed = mixed[0:64] + mixed[64:128]
        for b in range(FFN):
            piece = mixed[b * R : (b + 1) * R]
            send_f[b] = piece.astype(BF16)
        for step in FFN_FIRST:
            push(send_f.at[lax.rem(fx + step, FFN)], out.at[fx], 11, number_f[step])
        kept = pltpu.make_async_copy(send_f.at[fx], out.at[fx], o_sem.at[0])
        kept.start()

    with jax.named_scope("last_wait"):
        settle(send_a.at[pl.ds(0, CTX - 1)], send_sem.at[0])
        settle(recv_r.at[pl.ds(0, FFN - 1)], send_sem.at[1])
        settle(send_b.at[pl.ds(0, CTX - 1)], send_sem.at[2])
        settle(recv_c.at[pl.ds(0, FFN - 1)], send_sem.at[3])
        settle(recv_s.at[0, pl.ds(0, SIDE - 1)], send_sem.at[6])
        settle(recv_s.at[1, pl.ds(0, SIDE - 1)], send_sem.at[12])
        for g in range(GROUPS):
            settle(recv_1.at[g], send_sem.at[4 + g])
            settle(passing.at[g], send_sem.at[9 + g])
            settle(send_2.at[g, pl.ds(0, SIDE - 1)], send_sem.at[7 + g])
        settle(recv_e.at[pl.ds(0, SIDE - 1)], send_sem.at[13])
        settle(recv_e.at[0, pl.ds(0, SIDE - 1)], send_sem.at[13])
        settle(send_f.at[pl.ds(0, FFN - 1)], send_sem.at[11])

        kept.wait()
        settle(out.at[pl.ds(0, FFN - 1)], recv_sem.at[11])


def local(
    queries, key_cache, value_cache, lengths, residual, o_weight, norm_gain,
    gate_proj, up_proj, down_proj, expert_ids, route_weight,
):
    anywhere = pl.BlockSpec(memory_space=pl.ANY)
    parts = pl.pallas_call(
        kernel,
        out_shape=pltpu.VMEM((FFN, R, COLS), BF16),
        in_specs=[anywhere] * 12,
        out_specs=pl.BlockSpec(memory_space=pltpu.VMEM),
        scratch_shapes=[
            pltpu.SMEM((R,), jnp.int32),
            pltpu.VMEM((R, COLS), BF16),
            pltpu.VMEM((1, COLS), F32),
            pltpu.VMEM((R, 8), jnp.int32),
            pltpu.VMEM((R, 8), F32),
            pltpu.VMEM((R, HQ * HD), BF16),
            pltpu.VMEM((R, 128, KVH * HD), BF16),
            pltpu.VMEM((R, 128, KVH * HD), BF16),
            pltpu.VMEM((HQ * HD // CTX, D), BF16),
            pltpu.VMEM((E_LOC, COLS, 2 * FFH), BF16),
            pltpu.VMEM((E_LOC, FFH, COLS), BF16),
            pltpu.VMEM((CTX, 5, R, 128), BF16),
            pltpu.VMEM((CTX, 5, R, 128), BF16),
            pltpu.VMEM((CTX, 16, 128), BF16),
            pltpu.VMEM((CTX, 16, 128), BF16),
            pltpu.VMEM((FFN, 16, 128), BF16),
            pltpu.VMEM((FFN, R, 128), F32),
            pltpu.VMEM((2, SIDE, R, 128), F32),
            pltpu.VMEM((GROUPS, 6, SLOTS, FFH), BF16),
            pltpu.VMEM((GROUPS, SLOTS, FFH), BF16),
            pltpu.VMEM((GROUPS, SLOTS, FFH), F32),
            pltpu.VMEM((GROUPS, 2, SLOTS, FFH), F32),
            pltpu.VMEM((GROUPS, 5, SLOTS, FFH), BF16),
            pltpu.VMEM((GROUPS, SIDE, 2 * SLOTS, QUARTER), BF16),
            pltpu.VMEM((GROUPS, SIDE, 2 * SLOTS, QUARTER), BF16),
            pltpu.VMEM((SIDE, SIDE, GROUPS, SLOTS, QUARTER), BF16),
            pltpu.VMEM((FFN, R, COLS), BF16),
            pltpu.VMEM((128, 128), BF16),
            pltpu.VMEM((128, 128), BF16),
            pltpu.VMEM((E_LOC, SLOTS, COLS), BF16),
            pltpu.VMEM((E_LOC, SLOTS, COLS), BF16),
            pltpu.VMEM((PER, SLOTS, COLS), F32),
            pltpu.SemaphoreType.DMA((6,)),
            pltpu.SemaphoreType.DMA((2, 2)),
            pltpu.SemaphoreType.DMA((4,)),
            pltpu.SemaphoreType.DMA((3, E_LOC)),
            pltpu.SemaphoreType.DMA((14,)),
            pltpu.SemaphoreType.DMA((14,)),
            pltpu.SemaphoreType.DMA((SIDE,)),
        ],
        compiler_params=pltpu.CompilerParams(
            collective_id=0, has_side_effects=True, vmem_limit_bytes=56 * 2**20
        ),
        cost_estimate=pl.CostEstimate(
            flops=1_000_000_000, bytes_accessed=26_000_000, transcendentals=100_000
        ),
    )(
        lengths, residual, norm_gain.reshape(1, COLS), expert_ids, route_weight,
        queries, key_cache, value_cache, o_weight, gate_proj, up_proj, down_proj,
    )
    return jnp.sum(parts.astype(F32), axis=0).astype(BF16)


def solution(mesh):
    placed = (
        P("ffn", None),
        P("ffn", "ctx", None),
        P("ffn", "ctx", None),
        P("ffn"),
        P("ffn", "ctx"),
        P("ctx", None),
        P("ctx"),
        P("ffn", "ctx", None),
        P("ffn", "ctx", None),
        P("ffn", None, "ctx"),
        P("ffn", None),
        P("ffn", None),
    )
    return jax.shard_map(
        local, mesh=mesh, in_specs=placed, out_specs=P("ffn", "ctx"), check_vma=False
    )
```

```python
import jax
import jax.numpy as jnp
from jax import lax
from jax.experimental import pallas as pl
from jax.experimental.pallas import tpu as pltpu
from jax.sharding import PartitionSpec as P

D = 4096
HQ = 64
KVH = 4
HD = 128
FFH = 1536
MOST = 2
CTX = 16
SIDE = 4
FFN = 8
R = 8
E_LOC = 8
SLOTS = FFN * MOST
GROUPS = 2
PER = E_LOC // GROUPS
QUARTER = FFH // SIDE
COLS = D // CTX
LOGICAL = pl.DeviceIdType.LOGICAL
F32 = jnp.float32
BF16 = jnp.bfloat16


FAR_FIRST = sorted(
    ((dx, dz) for dx in range(SIDE) for dz in range(SIDE) if (dx, dz) != (0, 0)),
    key=lambda d: -(min(d[0], SIDE - d[0]) + min(d[1], SIDE - d[1])),
)
FFN_FIRST = (4, 5, 3, 2, 6, 7, 1)
OTHERS = (2, 1, 3)
BLOCKS = (2, 1, 3, 0)


def kernel(
    len_hbm, res_hbm, gain_hbm, ids_hbm, route_hbm,
    q_hbm, k_hbm, v_hbm, o_hbm, g_hbm, u_hbm, d_hbm,
    out,
    lengths, residual, gain, ids, route,
    q_v, k_v, v_v, o_v, gu_v, d_v,
    send_a, recv_a, send_b, recv_b, recv_c, recv_r, recv_s,
    send_1, passing, behind, own_1, recv_1, send_2, recv_2, recv_e, send_f,
    pick, weigh, rows, results, partly,
    in_sem, kv_sem, o_sem, w_sem, send_sem, recv_sem, line_recv,
):
    cx = lax.axis_index("ctx")
    fx = lax.axis_index("ffn")
    sx = cx // SIDE
    sz = lax.rem(cx, SIDE)

    way = 1 - 2 * lax.rem(fx, 2)
    turn_x = [lax.rem(sx + SIDE + way * step, SIDE) for step in range(SIDE)]
    turn_z = [lax.rem(sz + SIDE + way * step, SIDE) for step in range(SIDE)]
    number_x = [x * (SIDE * FFN) for x in turn_x]
    number_z = [z * FFN + fx for z in turn_z]
    number_f = [cx * FFN + lax.rem(fx + step, FFN) for step in range(FFN)]

    def every_ffn(visit):
        for step in FFN_FIRST:
            visit(number_f[step])

    def place(g):
        return (sx, sz) if g == 0 else (sz, sx)

    def turn(g, step):
        return turn_x[step] if g == 0 else turn_z[step]

    def first_line(g, step):
        return number_x[step] + number_z[0] if g == 0 else number_x[0] + number_z[step]

    def second_line(g, step):
        return first_line(1 - g, step)

    def settle(ref, sem):
        pltpu.make_async_copy(ref, ref, sem).wait()

    def push(src, dst, phase, to, recv=None):
        pltpu.make_async_remote_copy(
            src_ref=src, dst_ref=dst, send_sem=send_sem.at[phase],
            recv_sem=recv_sem.at[phase] if recv is None else recv,
            device_id=to, device_id_type=LOGICAL,
        ).start()

    with jax.named_scope("entry"):
        barrier = pltpu.get_barrier_semaphore()

        def greet(to):
            pl.semaphore_signal(barrier, inc=1, device_id=to, device_id_type=LOGICAL)

        pairs = [
            (q_hbm, q_v), (len_hbm, lengths),
            (ids_hbm, ids), (route_hbm, route), (res_hbm, residual), (gain_hbm, gain),
        ]
        first = [pltpu.make_async_copy(src, dst, in_sem.at[n]) for n, (src, dst) in enumerate(pairs)]
        for copy in first[:4]:
            copy.start()
        kv_copies = []
        for m, (src, dst) in enumerate(((k_hbm, k_v), (v_hbm, v_v))):
            for n in range(2):
                span = pl.ds(n * (R // 2), R // 2)
                kv_copies.append(
                    pltpu.make_async_copy(src.at[span], dst.at[span], kv_sem.at[m, n])
                )
        for copy in kv_copies:
            copy.start()
        for copy in first[4:]:
            copy.start()
        for dx, dz in FAR_FIRST:
            greet(number_x[dx] + number_z[dz])
        every_ffn(greet)
        o_copies = [
            pltpu.make_async_copy(
                o_hbm.at[pl.ds(n * 128, 128)], o_v.at[pl.ds(n * 128, 128)], o_sem.at[n]
            )
            for n in range(4)
        ]


        def fetch(step):
            for g in range(GROUPS):
                e = g * PER + turn(g, step)
                pltpu.make_async_copy(g_hbm.at[e], gu_v.at[e, :, 0:FFH], w_sem.at[0, e]).start()
                pltpu.make_async_copy(u_hbm.at[e], gu_v.at[e, :, FFH:], w_sem.at[1, e]).start()

        def fetch_down(e, carry):
            pltpu.make_async_copy(d_hbm.at[e], d_v.at[e], w_sem.at[2, e]).start()
            return carry


        lane8 = lax.broadcasted_iota(jnp.int32, (R, 128), 1)
        sub8 = lax.broadcasted_iota(jnp.int32, (R, 128), 0)
        filled = jnp.zeros((R, 128), jnp.int32)
        row_r = lax.broadcasted_iota(jnp.int32, (128, 128), 0) & 7
        lane_full = lax.broadcasted_iota(jnp.int32, (1, 4, R, 128), 3)
        head4 = lax.broadcasted_iota(jnp.int32, (1, 4, R, 128), 1)
        first[2].wait()
        first[3].wait()
        table = jnp.zeros((R, 128), F32)
        ids_f = ids[...].astype(F32)
        route_f = route[...]
        for k in range(8):
            table = jnp.where(lane8 == k, ids_f[:, k : k + 1], table)
            table = jnp.where(lane8 == 8 + k, route_f[:, k : k + 1], table)
        recv_r[fx] = table
        first[1].wait()
        for r in range(R):
            filled = jnp.where(sub8 == r, lengths[r], filled)
        usable = ((cx * 128 + lane8) < filled)[None]
        first[0].wait()

        def weigh_up(k):
            part = q_v[:, k * 16 * HD : (k + 1) * 16 * HD].astype(F32)
            queries = jnp.concatenate(
                [part[:, g * HD : (g + 1) * HD] for g in range(16)], axis=0
            ).astype(BF16)
            every = lax.dot_general(
                queries, k_v[:, :, k * HD : (k + 1) * HD].reshape(R * 128, HD),
                (((1,), (1,)), ((), ())), preferred_element_type=F32,
            )
            scores = every[:, 0:128]
            for r in range(1, R):
                scores = jnp.where(row_r == r, every[:, r * 128 : (r + 1) * 128], scores)
            scores = (scores * HD ** (-0.5)).reshape(16, R, 128)
            peak = jnp.max(jnp.where(usable, scores, -1e30), axis=-1, keepdims=True)
            peak = peak.astype(BF16).astype(F32)
            probs = jnp.where(usable, jnp.exp(scores - peak), 0.0)
            probs = probs.astype(BF16).astype(F32)
            total = jnp.sum(probs, axis=-1, keepdims=True)
            peak4 = jnp.broadcast_to(peak, (16, R, 128)).reshape(4, 4, R, 128)
            total4 = jnp.broadcast_to(total, (16, R, 128)).reshape(4, 4, R, 128)
            high = total4.astype(BF16).astype(F32)
            marks = jnp.sum(
                jnp.where(lane_full == head4, peak4, 0.0)
                + jnp.where(lane_full == head4 + 4, high, 0.0)
                + jnp.where(lane_full == head4 + 8, total4 - high, 0.0),
                axis=1,
            )
            send_a[k * 4 : (k + 1) * 4, 4] = marks.astype(BF16)
            return probs.reshape(128, 128)

        def sum_up(k, flat):
            spread = jnp.concatenate(
                [jnp.where(row_r == r, flat, 0.0).astype(BF16) for r in range(R)], axis=1
            )
            values = v_v[:, :, k * HD : (k + 1) * HD].reshape(R * 128, HD)
            numerator = jnp.dot(spread, values, preferred_element_type=F32)
            send_a[k * 4 : (k + 1) * 4, 0:4] = numerator.reshape(4, 4, R, HD).astype(BF16)

    with jax.named_scope("attention"):
        kv_copies[0].wait()
        kv_copies[1].wait()
        flats = [weigh_up(k) for k in range(KVH)]
        kv_copies[2].wait()
        kv_copies[3].wait()
        for copy in o_copies:
            copy.start()
        for k in range(KVH):
            sum_up(k, flats[k])

    with jax.named_scope("attention_sends"):
        pl.semaphore_wait(barrier, CTX - 1 + FFN - 1)
        for step in BLOCKS:
            for z in OTHERS + ((0,) if step else ()):
                to = turn_x[step] * SIDE + turn_z[z]
                push(send_a.at[to], recv_a.at[cx], 0, number_x[step] + number_z[z])
        every_ffn(lambda to: push(recv_r.at[fx], recv_r.at[fx], 1, to))
        recv_a[cx] = send_a[cx]
        fetch(2)
        fetch(1)

    with jax.named_scope("routing"):
        settle(recv_r.at[pl.ds(0, FFN - 1)], recv_sem.at[1])
        tables = recv_r[...].reshape(FFN * R, 128)
        lane = lax.broadcasted_iota(jnp.int32, (FFN * R, 128), 1)
        token = lax.broadcasted_iota(jnp.int32, (FFN * R, 128), 0)
        expert = (fx * E_LOC + (lane >> 4)).astype(F32)
        chosen = jnp.zeros((FFN * R, 128), F32)
        weight = jnp.zeros((FFN * R, 128), F32)
        for k in range(8):
            hit = tables[:, k : k + 1] == expert
            chosen = jnp.where(hit, 1.0, chosen)
            weight = jnp.where(hit, tables[:, 8 + k : 9 + k], weight)
        row = lax.broadcasted_iota(jnp.int32, (64, 64), 0)
        col = lax.broadcasted_iota(jnp.int32, (64, 64), 1)
        before = jnp.where((col < row) & ((col >> 3) == (row >> 3)), 1.0, 0.0).astype(BF16)
        rank = jnp.dot(before, chosen.astype(BF16), preferred_element_type=F32)
        here = (
            (chosen > 0.5)
            & (rank == (lane & 1).astype(F32))
            & ((token >> 3) == ((lane & 15) >> 1))
        )
        here_f = jnp.where(here, 1.0, 0.0)
        padded = jnp.concatenate([here_f, jnp.zeros((64, 128), F32)], axis=0)
        pick[...] = jnp.transpose(padded).astype(BF16)
        weight = jnp.where(here, weight, 0.0)
        high = weight.astype(BF16)
        weigh[0:64] = high
        weigh[64:128] = (weight - high.astype(F32)).astype(BF16)

    with jax.named_scope("attention_wait"):
        settle(recv_a.at[pl.ds(0, CTX - 1)], recv_sem.at[0])

    with jax.named_scope("attention_combine"):
        got = recv_a[...].astype(F32)
        marks = got[:, 4]
        factor = jnp.exp(marks - jnp.max(marks, axis=0, keepdims=True))
        share = pltpu.roll(marks, 124, 2) + pltpu.roll(marks, 120, 2)
        below = jnp.sum(factor * share, axis=0)
        heads = []
        for h in range(4):
            top = jnp.zeros((R, HD), F32)
            for c in range(CTX):
                top = top + factor[c, :, h : h + 1] * got[c, h]
            heads.append(top / below[:, h : h + 1])
        attended = jnp.concatenate(heads, axis=1).astype(BF16)

        for copy in o_copies:
            copy.wait()

    with jax.named_scope("projection"):
        projected = jnp.dot(attended, o_v[...], preferred_element_type=F32)
        for c in range(CTX):
            ahead, rest = projected[:, c * 256 : c * 256 + 128], projected[:, c * 256 + 128 : c * 256 + 256]
            send_b[c] = jnp.concatenate([ahead, rest], axis=0).astype(BF16)
        for step in BLOCKS:
            for z in OTHERS + ((0,) if step else ()):
                to = turn_x[step] * SIDE + turn_z[z]
                push(send_b.at[to], recv_b.at[cx], 2, number_x[step] + number_z[z])
        recv_b[cx] = send_b[cx]
        fetch(3)
        fetch(0)

        def weights_here(e, carry):
            pltpu.make_async_copy(g_hbm.at[e], gu_v.at[e, :, 0:FFH], w_sem.at[0, e]).wait()
            pltpu.make_async_copy(u_hbm.at[e], gu_v.at[e, :, FFH:], w_sem.at[1, e]).wait()
            return carry

        first[4].wait()
        first[5].wait()
        res = residual[...].astype(F32)
        res = jnp.concatenate([res[:, 0:128], res[:, 128:256]], axis=0)

    with jax.named_scope("projection_wait"):
        settle(recv_b.at[pl.ds(0, CTX - 1)], recv_sem.at[2])

    with jax.named_scope("hidden_sends"):
        hidden = res + jnp.sum(recv_b[...].astype(F32), axis=0)
        recv_c[fx] = hidden.astype(BF16)
        every_ffn(lambda to: push(recv_c.at[fx], recv_c.at[fx], 3, to))
        lax.fori_loop(0, E_LOC, fetch_down, 0)
        lax.fori_loop(0, E_LOC, weights_here, 0)

    with jax.named_scope("hidden_wait"):
        settle(recv_c.at[pl.ds(0, FFN - 1)], recv_sem.at[3])

    with jax.named_scope("rows"):
        tokens = recv_c[...].astype(F32)
        left = tokens[:, 0:8, :].reshape(64, 128)
        right = tokens[:, 8:16, :].reshape(64, 128)
        gained = jnp.concatenate([left * gain[:, 0:128], right * gain[:, 128:256]], axis=1)
        gained = jnp.concatenate([gained, jnp.zeros((64, 256), F32)], axis=0).astype(BF16)
        rows[...] = (
            jnp.dot(pick[...], gained, preferred_element_type=F32)
            .astype(BF16)
            .reshape(E_LOC, SLOTS, COLS)
        )

        def share_squares():
            squares = jnp.sum(left * left + right * right, axis=1, keepdims=True).reshape(FFN, R, 1)
            squares = jnp.broadcast_to(squares, (FFN, R, 128))
            block = lax.broadcasted_iota(jnp.int32, (FFN, R, 128), 0)
            lanes = lax.broadcasted_iota(jnp.int32, (FFN, R, 128), 2)
            recv_s[0, sx] = jnp.sum(jnp.where(lanes == block, squares, 0.0), axis=0)
            for step in OTHERS:
                push(recv_s.at[0, sx], recv_s.at[0, sx], 6, first_line(0, step))

        def gate_up(g, step):
            e = g * PER + turn(g, step)
            both = jnp.dot(rows[e], gu_v[e], preferred_element_type=F32)
            return both[:, 0:FFH], both[:, FFH:]

    with jax.named_scope("gate_up"):
        for g in range(GROUPS):
            gate, upward = gate_up(g, 2)
            send_1[g, 4] = gate.astype(BF16)
            send_1[g, 5] = upward.astype(BF16)
        for g in range(GROUPS):
            push(send_1.at[g, 5], passing.at[g], 9 + g, first_line(g, 3))
            push(send_1.at[g, 4], recv_1.at[g, 4], 4 + g, first_line(g, 2))
        for g in range(GROUPS):
            gate, upward = gate_up(g, 1)
            send_1[g, 0] = gate.astype(BF16)
            send_1[g, 1] = upward.astype(BF16)
            gate, behind[g] = gate_up(g, 3)
            send_1[g, 2] = gate.astype(BF16)
        for g in range(GROUPS):
            push(send_1.at[g, pl.ds(0, 2)], recv_1.at[g, pl.ds(0, 2)], 4 + g, first_line(g, 1))
            push(send_1.at[g, 2], recv_1.at[g, 2], 4 + g, first_line(g, 3))
        for g in range(GROUPS):
            own_1[g, 0], own_1[g, 1] = gate_up(g, 0)
        share_squares()
        for g in range(GROUPS):
            settle(passing.at[g], recv_sem.at[9 + g])
            send_1[g, 3] = (behind[g] + passing[g].astype(F32)).astype(BF16)
            push(send_1.at[g, 3], recv_1.at[g, 3], 4 + g, first_line(g, 3))

    with jax.named_scope("square_sums"):
        settle(recv_s.at[0, pl.ds(0, SIDE - 1)], recv_sem.at[6])
        recv_s[1, sz] = jnp.sum(recv_s[0], axis=0)
        for step in OTHERS:
            push(recv_s.at[1, sz], recv_s.at[1, sz], 12, second_line(0, step))

    with jax.named_scope("first_sums"):
        for g in range(GROUPS):
            after = place(g)[1]
            settle(recv_1.at[g], recv_sem.at[4 + g])
            gate = own_1[g, 0]
            upward = own_1[g, 1]
            for c in (0, 2, 4):
                gate = gate + recv_1[g, c].astype(F32)
            for c in (1, 3):
                upward = upward + recv_1[g, c].astype(F32)
            for n in range(SIDE):
                span = slice(n * QUARTER, (n + 1) * QUARTER)
                send_2[g, n, 0:SLOTS] = gate[:, span].astype(BF16)
                send_2[g, n, SLOTS:] = upward[:, span].astype(BF16)
            for step in OTHERS:
                to = turn(1 - g, step)
                push(send_2.at[g, to], recv_2.at[g, after], 7 + g, second_line(g, step))
            recv_2[g, after] = send_2[g, after]

    with jax.named_scope("scales"):
        settle(recv_s.at[1, pl.ds(0, SIDE - 1)], recv_sem.at[12])
        scale = lax.rsqrt(jnp.sum(recv_s[1], axis=0) * (1.0 / D) + 1e-06)
        scale = jnp.concatenate(
            [jnp.broadcast_to(scale[:, b : b + 1], (R, 128)) for b in range(FFN)]
            + [jnp.zeros((64, 128), F32)],
            axis=0,
        )
        high = scale.astype(BF16)
        split = jnp.concatenate([high, (scale - high.astype(F32)).astype(BF16)], axis=1)
        owned = [
            pick[pl.ds(pl.multiple_of((g * PER + place(g)[0]) * SLOTS, SLOTS), SLOTS), :]
            for g in range(GROUPS)
        ]
        scales = jnp.dot(jnp.concatenate(owned, axis=0), split, preferred_element_type=F32)
        scales = scales[:, 0:128] + scales[:, 128:256]
        own_scales = [
            jnp.concatenate([scales[g * SLOTS : (g + 1) * SLOTS]] * (QUARTER // 128), axis=1)
            for g in range(GROUPS)
        ]

    with jax.named_scope("inner"):
        for g in range(GROUPS):
            settle(recv_2.at[g, pl.ds(0, SIDE - 1)], recv_sem.at[7 + g])
            both = recv_2[g, 0].astype(F32)
            for c in range(1, SIDE):
                both = both + recv_2[g, c].astype(F32)
            gate = both[0:SLOTS] * own_scales[g]
            upward = both[SLOTS:] * own_scales[g]
            inner = gate / (1.0 + jnp.exp(-gate)) * upward
            recv_e[sx, sz, g] = inner.astype(BF16)

    with jax.named_scope("inner_sends"):
        for dx, dz in FAR_FIRST:
            push(
                recv_e.at[sx, sz], recv_e.at[sx, sz], 13, number_x[dx] + number_z[dz], line_recv.at[sx]
            )

        def down_here(e, carry):
            pltpu.make_async_copy(d_hbm.at[e], d_v.at[e], w_sem.at[2, e]).wait()
            return carry

        lax.fori_loop(0, E_LOC, down_here, 0)

    with jax.named_scope("down"):
        for step in (0, 1, 3, 2):
            x = turn_x[step]
            settle(recv_e.at[0, pl.ds(0, SIDE if step else SIDE - 1)], line_recv.at[x])
            inner = jnp.concatenate([recv_e[x, q, 0] for q in range(SIDE)], axis=1)
            results[x] = jnp.dot(inner, d_v[x], preferred_element_type=F32).astype(BF16)
            span = pl.ds(pl.multiple_of(x * QUARTER, QUARTER), QUARTER)
            for n in range(PER):
                term = jnp.dot(recv_e[x, n, 1], d_v[PER + n, span, :], preferred_element_type=F32)
                if step:
                    term = term + partly[n]
                if step != 2:
                    partly[n] = term
                else:
                    results[PER + n] = term.astype(BF16)

    with jax.named_scope("mix"):
        found = results[...].reshape(E_LOC * SLOTS, COLS)
        mixed = jnp.dot(weigh[...], found, preferred_element_type=F32)
        mixed = mixed[0:64] + mixed[64:128]
        for b in range(FFN):
            piece = mixed[b * R : (b + 1) * R]
            send_f[b] = piece.astype(BF16)
        for step in FFN_FIRST:
            push(send_f.at[lax.rem(fx + step, FFN)], out.at[fx], 11, number_f[step])
        kept = pltpu.make_async_copy(send_f.at[fx], out.at[fx], o_sem.at[0])
        kept.start()

    with jax.named_scope("last_wait"):
        settle(send_a.at[pl.ds(0, CTX - 1)], send_sem.at[0])
        settle(recv_r.at[pl.ds(0, FFN - 1)], send_sem.at[1])
        settle(send_b.at[pl.ds(0, CTX - 1)], send_sem.at[2])
        settle(recv_c.at[pl.ds(0, FFN - 1)], send_sem.at[3])
        settle(recv_s.at[0, pl.ds(0, SIDE - 1)], send_sem.at[6])
        settle(recv_s.at[1, pl.ds(0, SIDE - 1)], send_sem.at[12])
        for g in range(GROUPS):
            settle(recv_1.at[g], send_sem.at[4 + g])
            settle(passing.at[g], send_sem.at[9 + g])
            settle(send_2.at[g, pl.ds(0, SIDE - 1)], send_sem.at[7 + g])
        settle(recv_e.at[pl.ds(0, SIDE - 1)], send_sem.at[13])
        settle(recv_e.at[0, pl.ds(0, SIDE - 1)], send_sem.at[13])
        settle(send_f.at[pl.ds(0, FFN - 1)], send_sem.at[11])

        kept.wait()
        settle(out.at[pl.ds(0, FFN - 1)], recv_sem.at[11])


def local(
    queries, key_cache, value_cache, lengths, residual, o_weight, norm_gain,
    gate_proj, up_proj, down_proj, expert_ids, route_weight,
):
    anywhere = pl.BlockSpec(memory_space=pl.ANY)
    parts = pl.pallas_call(
        kernel,
        out_shape=pltpu.VMEM((FFN, R, COLS), BF16),
        in_specs=[anywhere] * 12,
        out_specs=pl.BlockSpec(memory_space=pltpu.VMEM),
        scratch_shapes=[
            pltpu.SMEM((R,), jnp.int32),
            pltpu.VMEM((R, COLS), BF16),
            pltpu.VMEM((1, COLS), F32),
            pltpu.VMEM((R, 8), jnp.int32),
            pltpu.VMEM((R, 8), F32),
            pltpu.VMEM((R, HQ * HD), BF16),
            pltpu.VMEM((R, 128, KVH * HD), BF16),
            pltpu.VMEM((R, 128, KVH * HD), BF16),
            pltpu.VMEM((HQ * HD // CTX, D), BF16),
            pltpu.VMEM((E_LOC, COLS, 2 * FFH), BF16),
            pltpu.VMEM((E_LOC, FFH, COLS), BF16),
            pltpu.VMEM((CTX, 5, R, 128), BF16),
            pltpu.VMEM((CTX, 5, R, 128), BF16),
            pltpu.VMEM((CTX, 16, 128), BF16),
            pltpu.VMEM((CTX, 16, 128), BF16),
            pltpu.VMEM((FFN, 16, 128), BF16),
            pltpu.VMEM((FFN, R, 128), F32),
            pltpu.VMEM((2, SIDE, R, 128), F32),
            pltpu.VMEM((GROUPS, 6, SLOTS, FFH), BF16),
            pltpu.VMEM((GROUPS, SLOTS, FFH), BF16),
            pltpu.VMEM((GROUPS, SLOTS, FFH), F32),
            pltpu.VMEM((GROUPS, 2, SLOTS, FFH), F32),
            pltpu.VMEM((GROUPS, 5, SLOTS, FFH), BF16),
            pltpu.VMEM((GROUPS, SIDE, 2 * SLOTS, QUARTER), BF16),
            pltpu.VMEM((GROUPS, SIDE, 2 * SLOTS, QUARTER), BF16),
            pltpu.VMEM((SIDE, SIDE, GROUPS, SLOTS, QUARTER), BF16),
            pltpu.VMEM((FFN, R, COLS), BF16),
            pltpu.VMEM((128, 128), BF16),
            pltpu.VMEM((128, 128), BF16),
            pltpu.VMEM((E_LOC, SLOTS, COLS), BF16),
            pltpu.VMEM((E_LOC, SLOTS, COLS), BF16),
            pltpu.VMEM((PER, SLOTS, COLS), F32),
            pltpu.SemaphoreType.DMA((6,)),
            pltpu.SemaphoreType.DMA((2, 2)),
            pltpu.SemaphoreType.DMA((4,)),
            pltpu.SemaphoreType.DMA((3, E_LOC)),
            pltpu.SemaphoreType.DMA((14,)),
            pltpu.SemaphoreType.DMA((14,)),
            pltpu.SemaphoreType.DMA((SIDE,)),
        ],
        compiler_params=pltpu.CompilerParams(
            collective_id=0, has_side_effects=True, vmem_limit_bytes=56 * 2**20
        ),
        cost_estimate=pl.CostEstimate(
            flops=1_000_000_000, bytes_accessed=26_000_000, transcendentals=100_000
        ),
    )(
        lengths, residual, norm_gain.reshape(1, COLS), expert_ids, route_weight,
        queries, key_cache, value_cache, o_weight, gate_proj, up_proj, down_proj,
    )
    return jnp.sum(parts.astype(F32), axis=0).astype(BF16)


def solution(mesh):
    placed = (
        P("ffn", None),
        P("ffn", "ctx", None),
        P("ffn", "ctx", None),
        P("ffn"),
        P("ffn", "ctx"),
        P("ctx", None),
        P("ctx"),
        P("ffn", "ctx", None),
        P("ffn", "ctx", None),
        P("ffn", None, "ctx"),
        P("ffn", None),
        P("ffn", None),
    )
    return jax.shard_map(
        local, mesh=mesh, in_specs=placed, out_specs=P("ffn", "ctx"), check_vma=False
    )
```

```python
import jax
import jax.numpy as jnp
from jax import lax
from jax.experimental import pallas as pl
from jax.experimental.pallas import tpu as pltpu
from jax.sharding import PartitionSpec as P

D = 4096
HQ = 64
KVH = 4
HD = 128
FFH = 1536
MOST = 2
CTX = 16
SIDE = 4
FFN = 8
R = 8
E_LOC = 8
SLOTS = FFN * MOST
GROUPS = 2
PER = E_LOC // GROUPS
QUARTER = FFH // SIDE
COLS = D // CTX
LOGICAL = pl.DeviceIdType.LOGICAL
F32 = jnp.float32
BF16 = jnp.bfloat16


FAR_FIRST = sorted(
    ((dx, dz) for dx in range(SIDE) for dz in range(SIDE) if (dx, dz) != (0, 0)),
    key=lambda d: -(min(d[0], SIDE - d[0]) + min(d[1], SIDE - d[1])),
)
FFN_FIRST = (4, 5, 3, 2, 6, 7, 1)
OTHERS = (2, 1, 3)
BLOCKS = (2, 1, 3, 0)


def kernel(
    len_hbm, res_hbm, gain_hbm, ids_hbm, route_hbm,
    q_hbm, k_hbm, v_hbm, o_hbm, g_hbm, u_hbm, d_hbm,
    out,
    lengths, residual, gain, ids, route,
    q_v, k_v, v_v, o_v, gu_v, d_v,
    send_a, recv_a, send_b, recv_b, recv_c, recv_r, recv_s,
    send_1, passing, behind, own_1, recv_1, send_2, recv_2, recv_e, send_f, recv_f,
    pick, weigh, rows, results, partly,
    in_sem, kv_sem, o_sem, w_sem, send_sem, recv_sem, line_recv,
):
    cx = lax.axis_index("ctx")
    fx = lax.axis_index("ffn")
    sx = cx // SIDE
    sz = lax.rem(cx, SIDE)

    way = 1 - 2 * lax.rem(fx, 2)
    turn_x = [lax.rem(sx + SIDE + way * step, SIDE) for step in range(SIDE)]
    turn_z = [lax.rem(sz + SIDE + way * step, SIDE) for step in range(SIDE)]
    number_x = [x * (SIDE * FFN) for x in turn_x]
    number_z = [z * FFN + fx for z in turn_z]
    odd = lax.rem(fx, 2)
    outer_number = [x + odd * (z - x) for x, z in zip(number_x, number_z)]
    inner_number = [z + odd * (x - z) for x, z in zip(number_x, number_z)]
    outer_place = [x * SIDE + odd * (z - x * SIDE) for x, z in zip(turn_x, turn_z)]
    inner_place = [z + odd * (x * SIDE - z) for x, z in zip(turn_x, turn_z)]
    number_f = [cx * FFN + lax.rem(fx + step, FFN) for step in range(FFN)]

    def every_ffn(visit):
        for step in FFN_FIRST:
            visit(number_f[step])

    def place(g):
        return (sx, sz) if g == 0 else (sz, sx)

    def turn(g, step):
        return turn_x[step] if g == 0 else turn_z[step]

    def first_line(g, step):
        return number_x[step] + number_z[0] if g == 0 else number_x[0] + number_z[step]

    def second_line(g, step):
        return first_line(1 - g, step)

    def settle(ref, sem):
        pltpu.make_async_copy(ref, ref, sem).wait()

    def push(src, dst, phase, to, recv=None):
        pltpu.make_async_remote_copy(
            src_ref=src, dst_ref=dst, send_sem=send_sem.at[phase],
            recv_sem=recv_sem.at[phase] if recv is None else recv,
            device_id=to, device_id_type=LOGICAL,
        ).start()

    with jax.named_scope("entry"):
        barrier = pltpu.get_barrier_semaphore()

        def greet(to):
            pl.semaphore_signal(barrier, inc=1, device_id=to, device_id_type=LOGICAL)

        pairs = [
            (q_hbm, q_v), (len_hbm, lengths),
            (ids_hbm, ids), (route_hbm, route), (res_hbm, residual), (gain_hbm, gain),
        ]
        first = [pltpu.make_async_copy(src, dst, in_sem.at[n]) for n, (src, dst) in enumerate(pairs)]
        for copy in first[:4]:
            copy.start()
        kv_copies = []
        for m, (src, dst) in enumerate(((k_hbm, k_v), (v_hbm, v_v))):
            for n in range(2):
                span = pl.ds(n * (R // 2), R // 2)
                kv_copies.append(
                    pltpu.make_async_copy(src.at[span], dst.at[span], kv_sem.at[m, n])
                )
        for copy in kv_copies:
            copy.start()
        for copy in first[4:]:
            copy.start()
        for dx, dz in FAR_FIRST:
            greet(number_x[dx] + number_z[dz])
        every_ffn(greet)
        o_copies = [
            pltpu.make_async_copy(
                o_hbm.at[pl.ds(n * 128, 128)], o_v.at[pl.ds(n * 128, 128)], o_sem.at[n]
            )
            for n in range(4)
        ]


        def fetch(step):
            for g in range(GROUPS):
                e = g * PER + turn(g, step)
                pltpu.make_async_copy(g_hbm.at[e], gu_v.at[e, :, 0:FFH], w_sem.at[0, e]).start()
                pltpu.make_async_copy(u_hbm.at[e], gu_v.at[e, :, FFH:], w_sem.at[1, e]).start()

        def fetch_down(e, carry):
            pltpu.make_async_copy(d_hbm.at[e], d_v.at[e], w_sem.at[2, e]).start()
            return carry


        lane8 = lax.broadcasted_iota(jnp.int32, (R, 128), 1)
        sub8 = lax.broadcasted_iota(jnp.int32, (R, 128), 0)
        filled = jnp.zeros((R, 128), jnp.int32)
        row_r = lax.broadcasted_iota(jnp.int32, (128, 128), 0) & 7
        lane_full = lax.broadcasted_iota(jnp.int32, (1, 4, R, 128), 3)
        head4 = lax.broadcasted_iota(jnp.int32, (1, 4, R, 128), 1)
        first[2].wait()
        first[3].wait()
        table = jnp.zeros((R, 128), F32)
        ids_f = ids[...].astype(F32)
        route_f = route[...]
        for k in range(8):
            table = jnp.where(lane8 == k, ids_f[:, k : k + 1], table)
            table = jnp.where(lane8 == 8 + k, route_f[:, k : k + 1], table)
        recv_r[fx] = table
        first[1].wait()
        for r in range(R):
            filled = jnp.where(sub8 == r, lengths[r], filled)
        usable = ((cx * 128 + lane8) < filled)[None]
        first[0].wait()

        def weigh_up(k):
            part = q_v[:, k * 16 * HD : (k + 1) * 16 * HD].astype(F32)
            queries = jnp.concatenate(
                [part[:, g * HD : (g + 1) * HD] for g in range(16)], axis=0
            ).astype(BF16)
            every = lax.dot_general(
                queries, k_v[:, :, k * HD : (k + 1) * HD].reshape(R * 128, HD),
                (((1,), (1,)), ((), ())), preferred_element_type=F32,
            )
            scores = every[:, 0:128]
            for r in range(1, R):
                scores = jnp.where(row_r == r, every[:, r * 128 : (r + 1) * 128], scores)
            scores = (scores * HD ** (-0.5)).reshape(16, R, 128)
            peak = jnp.max(jnp.where(usable, scores, -1e30), axis=-1, keepdims=True)
            peak = peak.astype(BF16).astype(F32)
            probs = jnp.where(usable, jnp.exp(scores - peak), 0.0)
            probs = probs.astype(BF16).astype(F32)
            total = jnp.sum(probs, axis=-1, keepdims=True)
            peak4 = jnp.broadcast_to(peak, (16, R, 128)).reshape(4, 4, R, 128)
            total4 = jnp.broadcast_to(total, (16, R, 128)).reshape(4, 4, R, 128)
            high = total4.astype(BF16).astype(F32)
            marks = jnp.sum(
                jnp.where(lane_full == head4, peak4, 0.0)
                + jnp.where(lane_full == head4 + 4, high, 0.0)
                + jnp.where(lane_full == head4 + 8, total4 - high, 0.0),
                axis=1,
            )
            send_a[k * 4 : (k + 1) * 4, 4] = marks.astype(BF16)
            return probs.reshape(128, 128)

        def sum_up(k, flat):
            spread = jnp.concatenate(
                [jnp.where(row_r == r, flat, 0.0).astype(BF16) for r in range(R)], axis=1
            )
            values = v_v[:, :, k * HD : (k + 1) * HD].reshape(R * 128, HD)
            numerator = jnp.dot(spread, values, preferred_element_type=F32)
            send_a[k * 4 : (k + 1) * 4, 0:4] = numerator.reshape(4, 4, R, HD).astype(BF16)

    with jax.named_scope("attention"):
        kv_copies[0].wait()
        kv_copies[1].wait()
        flats = [weigh_up(k) for k in range(KVH)]
        kv_copies[2].wait()
        kv_copies[3].wait()
        for copy in o_copies:
            copy.start()
        for k in range(KVH):
            sum_up(k, flats[k])

    with jax.named_scope("attention_sends"):
        pl.semaphore_wait(barrier, CTX - 1 + FFN - 1)
        for step in BLOCKS:
            for z in OTHERS + ((0,) if step else ()):
                to = outer_place[step] + inner_place[z]
                push(send_a.at[to], recv_a.at[cx], 0, outer_number[step] + inner_number[z])
        every_ffn(lambda to: push(recv_r.at[fx], recv_r.at[fx], 1, to))
        recv_a[cx] = send_a[cx]
        fetch(2)
        fetch(1)

    with jax.named_scope("routing"):
        settle(recv_r.at[pl.ds(0, FFN - 1)], recv_sem.at[1])
        tables = recv_r[...].reshape(FFN * R, 128)
        lane = lax.broadcasted_iota(jnp.int32, (FFN * R, 128), 1)
        token = lax.broadcasted_iota(jnp.int32, (FFN * R, 128), 0)
        expert = (fx * E_LOC + (lane >> 4)).astype(F32)
        chosen = jnp.zeros((FFN * R, 128), F32)
        weight = jnp.zeros((FFN * R, 128), F32)
        for k in range(8):
            hit = tables[:, k : k + 1] == expert
            chosen = jnp.where(hit, 1.0, chosen)
            weight = jnp.where(hit, tables[:, 8 + k : 9 + k], weight)
        row = lax.broadcasted_iota(jnp.int32, (64, 64), 0)
        col = lax.broadcasted_iota(jnp.int32, (64, 64), 1)
        before = jnp.where((col < row) & ((col >> 3) == (row >> 3)), 1.0, 0.0).astype(BF16)
        rank = jnp.dot(before, chosen.astype(BF16), preferred_element_type=F32)
        here = (
            (chosen > 0.5)
            & (rank == (lane & 1).astype(F32))
            & ((token >> 3) == ((lane & 15) >> 1))
        )
        here_f = jnp.where(here, 1.0, 0.0)
        padded = jnp.concatenate([here_f, jnp.zeros((64, 128), F32)], axis=0)
        pick[...] = jnp.transpose(padded).astype(BF16)
        weight = jnp.where(here, weight, 0.0)
        high = weight.astype(BF16)
        weigh[0:64] = high
        weigh[64:128] = (weight - high.astype(F32)).astype(BF16)

    with jax.named_scope("attention_wait"):
        settle(recv_a.at[pl.ds(0, CTX - 1)], recv_sem.at[0])

    with jax.named_scope("attention_combine"):
        got = recv_a[...].astype(F32)
        marks = got[:, 4]
        factor = jnp.exp(marks - jnp.max(marks, axis=0, keepdims=True))
        share = pltpu.roll(marks, 124, 2) + pltpu.roll(marks, 120, 2)
        below = jnp.sum(factor * share, axis=0)
        heads = []
        for h in range(4):
            top = jnp.zeros((R, HD), F32)
            for c in range(CTX):
                top = top + factor[c, :, h : h + 1] * got[c, h]
            heads.append(top / below[:, h : h + 1])
        attended = jnp.concatenate(heads, axis=1).astype(BF16)

        for copy in o_copies:
            copy.wait()

    with jax.named_scope("projection"):
        projected = jnp.dot(attended, o_v[...], preferred_element_type=F32)
        for c in range(CTX):
            ahead, rest = projected[:, c * 256 : c * 256 + 128], projected[:, c * 256 + 128 : c * 256 + 256]
            send_b[c] = jnp.concatenate([ahead, rest], axis=0).astype(BF16)
        for step in BLOCKS:
            for z in OTHERS + ((0,) if step else ()):
                to = outer_place[step] + inner_place[z]
                push(send_b.at[to], recv_b.at[cx], 2, outer_number[step] + inner_number[z])
        recv_b[cx] = send_b[cx]
        fetch(3)
        fetch(0)

        def weights_here(e, carry):
            pltpu.make_async_copy(g_hbm.at[e], gu_v.at[e, :, 0:FFH], w_sem.at[0, e]).wait()
            pltpu.make_async_copy(u_hbm.at[e], gu_v.at[e, :, FFH:], w_sem.at[1, e]).wait()
            return carry

        first[4].wait()
        first[5].wait()
        res = residual[...].astype(F32)
        res = jnp.concatenate([res[:, 0:128], res[:, 128:256]], axis=0)

    with jax.named_scope("projection_wait"):
        settle(recv_b.at[pl.ds(0, CTX - 1)], recv_sem.at[2])

    with jax.named_scope("hidden_sends"):
        hidden = res + jnp.sum(recv_b[...].astype(F32), axis=0)
        recv_c[fx] = hidden.astype(BF16)
        every_ffn(lambda to: push(recv_c.at[fx], recv_c.at[fx], 3, to))
        lax.fori_loop(0, E_LOC, fetch_down, 0)
        lax.fori_loop(0, E_LOC, weights_here, 0)

    with jax.named_scope("hidden_wait"):
        settle(recv_c.at[pl.ds(0, FFN - 1)], recv_sem.at[3])

    with jax.named_scope("rows"):
        tokens = recv_c[...].astype(F32)
        left = tokens[:, 0:8, :].reshape(64, 128)
        right = tokens[:, 8:16, :].reshape(64, 128)
        gained = jnp.concatenate([left * gain[:, 0:128], right * gain[:, 128:256]], axis=1)
        gained = jnp.concatenate([gained, jnp.zeros((64, 256), F32)], axis=0).astype(BF16)
        rows[...] = (
            jnp.dot(pick[...], gained, preferred_element_type=F32)
            .astype(BF16)
            .reshape(E_LOC, SLOTS, COLS)
        )

        def share_squares():
            squares = jnp.sum(left * left + right * right, axis=1, keepdims=True).reshape(FFN, R, 1)
            squares = jnp.broadcast_to(squares, (FFN, R, 128))
            block = lax.broadcasted_iota(jnp.int32, (FFN, R, 128), 0)
            lanes = lax.broadcasted_iota(jnp.int32, (FFN, R, 128), 2)
            recv_s[0, sx] = jnp.sum(jnp.where(lanes == block, squares, 0.0), axis=0)
            for step in OTHERS:
                push(recv_s.at[0, sx], recv_s.at[0, sx], 6, first_line(0, step))

        def gate_up(g, step):
            e = g * PER + turn(g, step)
            both = jnp.dot(rows[e], gu_v[e], preferred_element_type=F32)
            return both[:, 0:FFH], both[:, FFH:]

    with jax.named_scope("gate_up"):
        for g in range(GROUPS):
            gate, upward = gate_up(g, 2)
            send_1[g, 4] = gate.astype(BF16)
            send_1[g, 5] = upward.astype(BF16)
        for g in range(GROUPS):
            push(send_1.at[g, 5], passing.at[g], 9 + g, first_line(g, 3))
            push(send_1.at[g, 4], recv_1.at[g, 4], 4 + g, first_line(g, 2))
        for g in range(GROUPS):
            gate, upward = gate_up(g, 1)
            send_1[g, 0] = gate.astype(BF16)
            send_1[g, 1] = upward.astype(BF16)
            gate, behind[g] = gate_up(g, 3)
            send_1[g, 2] = gate.astype(BF16)
        for g in range(GROUPS):
            push(send_1.at[g, pl.ds(0, 2)], recv_1.at[g, pl.ds(0, 2)], 4 + g, first_line(g, 1))
            push(send_1.at[g, 2], recv_1.at[g, 2], 4 + g, first_line(g, 3))
        for g in range(GROUPS):
            own_1[g, 0], own_1[g, 1] = gate_up(g, 0)
        share_squares()
        for g in range(GROUPS):
            settle(passing.at[g], recv_sem.at[9 + g])
            send_1[g, 3] = (behind[g] + passing[g].astype(F32)).astype(BF16)
            push(send_1.at[g, 3], recv_1.at[g, 3], 4 + g, first_line(g, 3))

    with jax.named_scope("square_sums"):
        settle(recv_s.at[0, pl.ds(0, SIDE - 1)], recv_sem.at[6])
        recv_s[1, sz] = jnp.sum(recv_s[0], axis=0)
        for step in OTHERS:
            push(recv_s.at[1, sz], recv_s.at[1, sz], 12, second_line(0, step))

    with jax.named_scope("first_sums"):
        for g in range(GROUPS):
            after = place(g)[1]
            settle(recv_1.at[g], recv_sem.at[4 + g])
            gate = own_1[g, 0]
            upward = own_1[g, 1]
            for c in (0, 2, 4):
                gate = gate + recv_1[g, c].astype(F32)
            for c in (1, 3):
                upward = upward + recv_1[g, c].astype(F32)
            for n in range(SIDE):
                span = slice(n * QUARTER, (n + 1) * QUARTER)
                send_2[g, n, 0:SLOTS] = gate[:, span].astype(BF16)
                send_2[g, n, SLOTS:] = upward[:, span].astype(BF16)
            for step in OTHERS:
                to = turn(1 - g, step)
                push(send_2.at[g, to], recv_2.at[g, after], 7 + g, second_line(g, step))
            recv_2[g, after] = send_2[g, after]

    with jax.named_scope("scales"):
        settle(recv_s.at[1, pl.ds(0, SIDE - 1)], recv_sem.at[12])
        scale = lax.rsqrt(jnp.sum(recv_s[1], axis=0) * (1.0 / D) + 1e-06)
        scale = jnp.concatenate(
            [jnp.broadcast_to(scale[:, b : b + 1], (R, 128)) for b in range(FFN)]
            + [jnp.zeros((64, 128), F32)],
            axis=0,
        )
        high = scale.astype(BF16)
        split = jnp.concatenate([high, (scale - high.astype(F32)).astype(BF16)], axis=1)
        owned = [
            pick[pl.ds(pl.multiple_of((g * PER + place(g)[0]) * SLOTS, SLOTS), SLOTS), :]
            for g in range(GROUPS)
        ]
        scales = jnp.dot(jnp.concatenate(owned, axis=0), split, preferred_element_type=F32)
        scales = scales[:, 0:128] + scales[:, 128:256]
        own_scales = [
            jnp.concatenate([scales[g * SLOTS : (g + 1) * SLOTS]] * (QUARTER // 128), axis=1)
            for g in range(GROUPS)
        ]

    with jax.named_scope("inner"):
        for g in range(GROUPS):
            settle(recv_2.at[g, pl.ds(0, SIDE - 1)], recv_sem.at[7 + g])
            both = recv_2[g, 0].astype(F32)
            for c in range(1, SIDE):
                both = both + recv_2[g, c].astype(F32)
            gate = both[0:SLOTS] * own_scales[g]
            upward = both[SLOTS:] * own_scales[g]
            inner = gate / (1.0 + jnp.exp(-gate)) * upward
            recv_e[sx, sz, g] = inner.astype(BF16)

    with jax.named_scope("inner_sends"):
        for dx, dz in FAR_FIRST:
            push(
                recv_e.at[sx, sz], recv_e.at[sx, sz], 13, outer_number[dx] + inner_number[dz],
                line_recv.at[sx],
            )

        def down_here(e, carry):
            pltpu.make_async_copy(d_hbm.at[e], d_v.at[e], w_sem.at[2, e]).wait()
            return carry

        lax.fori_loop(0, E_LOC, down_here, 0)

    with jax.named_scope("down"):
        for step in (0, 1, 3, 2):
            x = turn_x[step]
            settle(recv_e.at[0, pl.ds(0, SIDE if step else SIDE - 1)], line_recv.at[x])
            inner = jnp.concatenate([recv_e[x, q, 0] for q in range(SIDE)], axis=1)
            results[x] = jnp.dot(inner, d_v[x], preferred_element_type=F32).astype(BF16)
            span = pl.ds(pl.multiple_of(x * QUARTER, QUARTER), QUARTER)
            for n in range(PER):
                term = jnp.dot(recv_e[x, n, 1], d_v[PER + n, span, :], preferred_element_type=F32)
                if step:
                    term = term + partly[n]
                if step != 2:
                    partly[n] = term
                else:
                    results[PER + n] = term.astype(BF16)

    with jax.named_scope("mix"):
        found = results[...].reshape(E_LOC * SLOTS, COLS)
        mixed = jnp.dot(weigh[...], found, preferred_element_type=F32)
        mixed = mixed[0:64] + mixed[64:128]
        for b in range(FFN):
            piece = mixed[b * R : (b + 1) * R]
            send_f[b] = piece.astype(BF16)
        for step in FFN_FIRST:
            push(send_f.at[lax.rem(fx + step, FFN)], recv_f.at[fx], 11, number_f[step])
        recv_f[fx] = send_f[fx]

    with jax.named_scope("last_wait"):
        settle(send_a.at[pl.ds(0, CTX - 1)], send_sem.at[0])
        settle(recv_r.at[pl.ds(0, FFN - 1)], send_sem.at[1])
        settle(send_b.at[pl.ds(0, CTX - 1)], send_sem.at[2])
        settle(recv_c.at[pl.ds(0, FFN - 1)], send_sem.at[3])
        settle(recv_s.at[0, pl.ds(0, SIDE - 1)], send_sem.at[6])
        settle(recv_s.at[1, pl.ds(0, SIDE - 1)], send_sem.at[12])
        for g in range(GROUPS):
            settle(recv_1.at[g], send_sem.at[4 + g])
            settle(passing.at[g], send_sem.at[9 + g])
            settle(send_2.at[g, pl.ds(0, SIDE - 1)], send_sem.at[7 + g])
        settle(recv_e.at[pl.ds(0, SIDE - 1)], send_sem.at[13])
        settle(recv_e.at[0, pl.ds(0, SIDE - 1)], send_sem.at[13])
        settle(send_f.at[pl.ds(0, FFN - 1)], send_sem.at[11])

        settle(recv_f.at[pl.ds(0, FFN - 1)], recv_sem.at[11])
        out[...] = jnp.sum(recv_f[...].astype(F32), axis=0).astype(BF16)


def local(
    queries, key_cache, value_cache, lengths, residual, o_weight, norm_gain,
    gate_proj, up_proj, down_proj, expert_ids, route_weight,
):
    anywhere = pl.BlockSpec(memory_space=pl.ANY)
    return pl.pallas_call(
        kernel,
        out_shape=pltpu.VMEM((R, COLS), BF16),
        in_specs=[anywhere] * 12,
        out_specs=pl.BlockSpec(memory_space=pltpu.VMEM),
        scratch_shapes=[
            pltpu.SMEM((R,), jnp.int32),
            pltpu.VMEM((R, COLS), BF16),
            pltpu.VMEM((1, COLS), F32),
            pltpu.VMEM((R, 8), jnp.int32),
            pltpu.VMEM((R, 8), F32),
            pltpu.VMEM((R, HQ * HD), BF16),
            pltpu.VMEM((R, 128, KVH * HD), BF16),
            pltpu.VMEM((R, 128, KVH * HD), BF16),
            pltpu.VMEM((HQ * HD // CTX, D), BF16),
            pltpu.VMEM((E_LOC, COLS, 2 * FFH), BF16),
            pltpu.VMEM((E_LOC, FFH, COLS), BF16),
            pltpu.VMEM((CTX, 5, R, 128), BF16),
            pltpu.VMEM((CTX, 5, R, 128), BF16),
            pltpu.VMEM((CTX, 16, 128), BF16),
            pltpu.VMEM((CTX, 16, 128), BF16),
            pltpu.VMEM((FFN, 16, 128), BF16),
            pltpu.VMEM((FFN, R, 128), F32),
            pltpu.VMEM((2, SIDE, R, 128), F32),
            pltpu.VMEM((GROUPS, 6, SLOTS, FFH), BF16),
            pltpu.VMEM((GROUPS, SLOTS, FFH), BF16),
            pltpu.VMEM((GROUPS, SLOTS, FFH), F32),
            pltpu.VMEM((GROUPS, 2, SLOTS, FFH), F32),
            pltpu.VMEM((GROUPS, 5, SLOTS, FFH), BF16),
            pltpu.VMEM((GROUPS, SIDE, 2 * SLOTS, QUARTER), BF16),
            pltpu.VMEM((GROUPS, SIDE, 2 * SLOTS, QUARTER), BF16),
            pltpu.VMEM((SIDE, SIDE, GROUPS, SLOTS, QUARTER), BF16),
            pltpu.VMEM((FFN, R, COLS), BF16),
            pltpu.VMEM((FFN, R, COLS), BF16),
            pltpu.VMEM((128, 128), BF16),
            pltpu.VMEM((128, 128), BF16),
            pltpu.VMEM((E_LOC, SLOTS, COLS), BF16),
            pltpu.VMEM((E_LOC, SLOTS, COLS), BF16),
            pltpu.VMEM((PER, SLOTS, COLS), F32),
            pltpu.SemaphoreType.DMA((6,)),
            pltpu.SemaphoreType.DMA((2, 2)),
            pltpu.SemaphoreType.DMA((4,)),
            pltpu.SemaphoreType.DMA((3, E_LOC)),
            pltpu.SemaphoreType.DMA((14,)),
            pltpu.SemaphoreType.DMA((14,)),
            pltpu.SemaphoreType.DMA((SIDE,)),
        ],
        compiler_params=pltpu.CompilerParams(
            collective_id=0, has_side_effects=True, vmem_limit_bytes=56 * 2**20
        ),
        cost_estimate=pl.CostEstimate(
            flops=1_000_000_000, bytes_accessed=26_000_000, transcendentals=100_000
        ),
    )(
        lengths, residual, norm_gain.reshape(1, COLS), expert_ids, route_weight,
        queries, key_cache, value_cache, o_weight, gate_proj, up_proj, down_proj,
    )


def solution(mesh):
    placed = (
        P("ffn", None),
        P("ffn", "ctx", None),
        P("ffn", "ctx", None),
        P("ffn"),
        P("ffn", "ctx"),
        P("ctx", None),
        P("ctx"),
        P("ffn", "ctx", None),
        P("ffn", "ctx", None),
        P("ffn", None, "ctx"),
        P("ffn", None),
        P("ffn", None),
    )
    return jax.shard_map(
        local, mesh=mesh, in_specs=placed, out_specs=P("ffn", "ctx"), check_vma=False
    )
```

```python
import jax
import jax.numpy as jnp
from jax import lax
from jax.experimental import pallas as pl
from jax.experimental.pallas import tpu as pltpu
from jax.sharding import PartitionSpec as P

D = 4096
HQ = 64
KVH = 4
HD = 128
FFH = 1536
MOST = 2
CTX = 16
SIDE = 4
FFN = 8
R = 8
E_LOC = 8
SLOTS = FFN * MOST
GROUPS = 2
PER = E_LOC // GROUPS
QUARTER = FFH // SIDE
COLS = D // CTX
LOGICAL = pl.DeviceIdType.LOGICAL
F32 = jnp.float32
BF16 = jnp.bfloat16


FAR_FIRST = sorted(
    ((dx, dz) for dx in range(SIDE) for dz in range(SIDE) if (dx, dz) != (0, 0)),
    key=lambda d: -(min(d[0], SIDE - d[0]) + min(d[1], SIDE - d[1])),
)
FFN_FIRST = (4, 5, 3, 2, 6, 7, 1)
OTHERS = (2, 1, 3)
BLOCKS = (2, 1, 3, 0)


def kernel(
    len_hbm, res_hbm, gain_hbm, ids_hbm, route_hbm,
    q_hbm, k_hbm, v_hbm, o_hbm, g_hbm, u_hbm, d_hbm,
    out,
    lengths, residual, gain, ids, route,
    q_v, k_v, v_v, o_v, gu_v, d_v,
    send_a, recv_a, send_b, recv_b, recv_c, recv_r, recv_s,
    send_1, passing, behind, own_1, recv_1, send_2, recv_2, recv_e, send_f,
    pick, weigh, rows, results, partly,
    in_sem, kv_sem, o_sem, w_sem, send_sem, recv_sem, line_recv,
):
    cx = lax.axis_index("ctx")
    fx = lax.axis_index("ffn")
    sx = cx // SIDE
    sz = lax.rem(cx, SIDE)

    way = 1 - 2 * lax.rem(fx, 2)
    turn_x = [lax.rem(sx + SIDE + way * step, SIDE) for step in range(SIDE)]
    turn_z = [lax.rem(sz + SIDE + way * step, SIDE) for step in range(SIDE)]
    number_x = [x * (SIDE * FFN) for x in turn_x]
    number_z = [z * FFN + fx for z in turn_z]
    number_f = [cx * FFN + lax.rem(fx + step, FFN) for step in range(FFN)]

    def every_ffn(visit):
        for step in FFN_FIRST:
            visit(number_f[step])

    def place(g):
        return (sx, sz) if g == 0 else (sz, sx)

    def turn(g, step):
        return turn_x[step] if g == 0 else turn_z[step]

    def first_line(g, step):
        return number_x[step] + number_z[0] if g == 0 else number_x[0] + number_z[step]

    def second_line(g, step):
        return first_line(1 - g, step)

    def settle(ref, sem):
        pltpu.make_async_copy(ref, ref, sem).wait()

    def push(src, dst, phase, to, recv=None):
        pltpu.make_async_remote_copy(
            src_ref=src, dst_ref=dst, send_sem=send_sem.at[phase],
            recv_sem=recv_sem.at[phase] if recv is None else recv,
            device_id=to, device_id_type=LOGICAL,
        ).start()

    with jax.named_scope("entry"):
        barrier = pltpu.get_barrier_semaphore()

        def greet(to):
            pl.semaphore_signal(barrier, inc=1, device_id=to, device_id_type=LOGICAL)

        pairs = [
            (q_hbm, q_v), (len_hbm, lengths),
            (ids_hbm, ids), (route_hbm, route), (res_hbm, residual), (gain_hbm, gain),
        ]
        first = [pltpu.make_async_copy(src, dst, in_sem.at[n]) for n, (src, dst) in enumerate(pairs)]
        for copy in first[:4]:
            copy.start()
        kv_copies = []
        for m, (src, dst) in enumerate(((k_hbm, k_v), (v_hbm, v_v))):
            for n in range(2):
                span = pl.ds(n * (R // 2), R // 2)
                kv_copies.append(
                    pltpu.make_async_copy(src.at[span], dst.at[span], kv_sem.at[m, n])
                )
        for copy in kv_copies:
            copy.start()
        for copy in first[4:]:
            copy.start()
        for dx, dz in FAR_FIRST:
            greet(number_x[dx] + number_z[dz])
        every_ffn(greet)
        o_copies = [
            pltpu.make_async_copy(
                o_hbm.at[pl.ds(n * 128, 128)], o_v.at[pl.ds(n * 128, 128)], o_sem.at[n]
            )
            for n in range(4)
        ]


        def fetch(step):
            for g in range(GROUPS):
                e = g * PER + turn(g, step)
                pltpu.make_async_copy(g_hbm.at[e], gu_v.at[e, :, 0:FFH], w_sem.at[0, e]).start()
                pltpu.make_async_copy(u_hbm.at[e], gu_v.at[e, :, FFH:], w_sem.at[1, e]).start()

        def fetch_down(e, carry):
            pltpu.make_async_copy(d_hbm.at[e], d_v.at[e], w_sem.at[2, e]).start()
            return carry


        lane8 = lax.broadcasted_iota(jnp.int32, (R, 128), 1)
        sub8 = lax.broadcasted_iota(jnp.int32, (R, 128), 0)
        filled = jnp.zeros((R, 128), jnp.int32)
        row_r = lax.broadcasted_iota(jnp.int32, (128, 128), 0) & 7
        lane_full = lax.broadcasted_iota(jnp.int32, (1, 4, R, 128), 3)
        head4 = lax.broadcasted_iota(jnp.int32, (1, 4, R, 128), 1)
        first[2].wait()
        first[3].wait()
        table = jnp.zeros((R, 128), F32)
        ids_f = ids[...].astype(F32)
        route_f = route[...]
        for k in range(8):
            table = jnp.where(lane8 == k, ids_f[:, k : k + 1], table)
            table = jnp.where(lane8 == 8 + k, route_f[:, k : k + 1], table)
        recv_r[fx] = table
        first[1].wait()
        for r in range(R):
            filled = jnp.where(sub8 == r, lengths[r], filled)
        usable = ((cx * 128 + lane8) < filled)[None]
        first[0].wait()

        def weigh_up(k):
            part = q_v[:, k * 16 * HD : (k + 1) * 16 * HD].astype(F32)
            queries = jnp.concatenate(
                [part[:, g * HD : (g + 1) * HD] for g in range(16)], axis=0
            ).astype(BF16)
            every = lax.dot_general(
                queries, k_v[:, :, k * HD : (k + 1) * HD].reshape(R * 128, HD),
                (((1,), (1,)), ((), ())), preferred_element_type=F32,
            )
            scores = every[:, 0:128]
            for r in range(1, R):
                scores = jnp.where(row_r == r, every[:, r * 128 : (r + 1) * 128], scores)
            scores = (scores * HD ** (-0.5)).reshape(16, R, 128)
            peak = jnp.max(jnp.where(usable, scores, -1e30), axis=-1, keepdims=True)
            peak = peak.astype(BF16).astype(F32)
            probs = jnp.where(usable, jnp.exp(scores - peak), 0.0)
            probs = probs.astype(BF16).astype(F32)
            total = jnp.sum(probs, axis=-1, keepdims=True)
            peak4 = jnp.broadcast_to(peak, (16, R, 128)).reshape(4, 4, R, 128)
            total4 = jnp.broadcast_to(total, (16, R, 128)).reshape(4, 4, R, 128)
            high = total4.astype(BF16).astype(F32)
            marks = jnp.sum(
                jnp.where(lane_full == head4, peak4, 0.0)
                + jnp.where(lane_full == head4 + 4, high, 0.0)
                + jnp.where(lane_full == head4 + 8, total4 - high, 0.0),
                axis=1,
            )
            send_a[k * 4 : (k + 1) * 4, 4] = marks.astype(BF16)
            return probs.reshape(128, 128)

        def sum_up(k, flat):
            spread = jnp.concatenate(
                [jnp.where(row_r == r, flat, 0.0).astype(BF16) for r in range(R)], axis=1
            )
            values = v_v[:, :, k * HD : (k + 1) * HD].reshape(R * 128, HD)
            numerator = jnp.dot(spread, values, preferred_element_type=F32)
            send_a[k * 4 : (k + 1) * 4, 0:4] = numerator.reshape(4, 4, R, HD).astype(BF16)

    with jax.named_scope("attention"):
        kv_copies[0].wait()
        kv_copies[1].wait()
        flats = [weigh_up(k) for k in range(KVH)]
        kv_copies[2].wait()
        kv_copies[3].wait()
        for copy in o_copies:
            copy.start()
        for k in range(KVH):
            sum_up(k, flats[k])

    with jax.named_scope("attention_sends"):
        pl.semaphore_wait(barrier, CTX - 1 + FFN - 1)
        for step in BLOCKS:
            for z in OTHERS + ((0,) if step else ()):
                to = turn_x[step] * SIDE + turn_z[z]
                push(send_a.at[to], recv_a.at[cx], 0, number_x[step] + number_z[z])
        every_ffn(lambda to: push(recv_r.at[fx], recv_r.at[fx], 1, to))
        recv_a[cx] = send_a[cx]
        fetch(2)
        fetch(1)

    with jax.named_scope("routing"):
        settle(recv_r.at[pl.ds(0, FFN - 1)], recv_sem.at[1])
        tables = recv_r[...].reshape(FFN * R, 128)
        lane = lax.broadcasted_iota(jnp.int32, (FFN * R, 128), 1)
        token = lax.broadcasted_iota(jnp.int32, (FFN * R, 128), 0)
        expert = (fx * E_LOC + (lane >> 4)).astype(F32)
        chosen = jnp.zeros((FFN * R, 128), F32)
        weight = jnp.zeros((FFN * R, 128), F32)
        for k in range(8):
            hit = tables[:, k : k + 1] == expert
            chosen = jnp.where(hit, 1.0, chosen)
            weight = jnp.where(hit, tables[:, 8 + k : 9 + k], weight)
        row = lax.broadcasted_iota(jnp.int32, (64, 64), 0)
        col = lax.broadcasted_iota(jnp.int32, (64, 64), 1)
        before = jnp.where((col < row) & ((col >> 3) == (row >> 3)), 1.0, 0.0).astype(BF16)
        rank = jnp.dot(before, chosen.astype(BF16), preferred_element_type=F32)
        here = (
            (chosen > 0.5)
            & (rank == (lane & 1).astype(F32))
            & ((token >> 3) == ((lane & 15) >> 1))
        )
        here_f = jnp.where(here, 1.0, 0.0)
        padded = jnp.concatenate([here_f, jnp.zeros((64, 128), F32)], axis=0)
        pick[...] = jnp.transpose(padded).astype(BF16)
        weight = jnp.where(here, weight, 0.0)
        high = weight.astype(BF16)
        weigh[0:64] = high
        weigh[64:128] = (weight - high.astype(F32)).astype(BF16)

    with jax.named_scope("attention_wait"):
        settle(recv_a.at[pl.ds(0, CTX - 1)], recv_sem.at[0])

    with jax.named_scope("attention_combine"):
        got = recv_a[...].astype(F32)
        marks = got[:, 4]
        factor = jnp.exp(marks - jnp.max(marks, axis=0, keepdims=True))
        share = pltpu.roll(marks, 124, 2) + pltpu.roll(marks, 120, 2)
        below = jnp.sum(factor * share, axis=0)
        heads = []
        for h in range(4):
            top = jnp.zeros((R, HD), F32)
            for c in range(CTX):
                top = top + factor[c, :, h : h + 1] * got[c, h]
            heads.append(top / below[:, h : h + 1])
        attended = jnp.concatenate(heads, axis=1).astype(BF16)

        for copy in o_copies:
            copy.wait()

    with jax.named_scope("projection"):
        projected = jnp.dot(attended, o_v[...], preferred_element_type=F32)
        for c in range(CTX):
            ahead, rest = projected[:, c * 256 : c * 256 + 128], projected[:, c * 256 + 128 : c * 256 + 256]
            send_b[c] = jnp.concatenate([ahead, rest], axis=0).astype(BF16)
        for step in BLOCKS:
            for z in OTHERS + ((0,) if step else ()):
                to = turn_x[step] * SIDE + turn_z[z]
                push(send_b.at[to], recv_b.at[cx], 2, number_x[step] + number_z[z])
        recv_b[cx] = send_b[cx]
        fetch(3)
        fetch(0)

        def weights_here(e, carry):
            pltpu.make_async_copy(g_hbm.at[e], gu_v.at[e, :, 0:FFH], w_sem.at[0, e]).wait()
            pltpu.make_async_copy(u_hbm.at[e], gu_v.at[e, :, FFH:], w_sem.at[1, e]).wait()
            return carry

        first[4].wait()
        first[5].wait()
        res = residual[...].astype(F32)
        res = jnp.concatenate([res[:, 0:128], res[:, 128:256]], axis=0)

    with jax.named_scope("projection_wait"):
        settle(recv_b.at[pl.ds(0, CTX - 1)], recv_sem.at[2])

    with jax.named_scope("hidden_sends"):
        hidden = res + jnp.sum(recv_b[...].astype(F32), axis=0)
        recv_c[fx] = hidden.astype(BF16)
        every_ffn(lambda to: push(recv_c.at[fx], recv_c.at[fx], 3, to))
        lax.fori_loop(0, E_LOC, fetch_down, 0)
        lax.fori_loop(0, E_LOC, weights_here, 0)

    with jax.named_scope("hidden_wait"):
        settle(recv_c.at[pl.ds(0, FFN - 1)], recv_sem.at[3])

    with jax.named_scope("rows"):
        tokens = recv_c[...].astype(F32)
        left = tokens[:, 0:8, :].reshape(64, 128)
        right = tokens[:, 8:16, :].reshape(64, 128)
        gained = jnp.concatenate([left * gain[:, 0:128], right * gain[:, 128:256]], axis=1)
        gained = jnp.concatenate([gained, jnp.zeros((64, 256), F32)], axis=0).astype(BF16)
        rows[...] = (
            jnp.dot(pick[...], gained, preferred_element_type=F32)
            .astype(BF16)
            .reshape(E_LOC, SLOTS, COLS)
        )

        def share_squares():
            squares = jnp.sum(left * left + right * right, axis=1, keepdims=True).reshape(FFN, R, 1)
            squares = jnp.broadcast_to(squares, (FFN, R, 128))
            block = lax.broadcasted_iota(jnp.int32, (FFN, R, 128), 0)
            lanes = lax.broadcasted_iota(jnp.int32, (FFN, R, 128), 2)
            recv_s[0, sx] = jnp.sum(jnp.where(lanes == block, squares, 0.0), axis=0)
            for step in OTHERS:
                push(recv_s.at[0, sx], recv_s.at[0, sx], 6, first_line(0, step))

        def gate_up(g, step):
            e = g * PER + turn(g, step)
            both = jnp.dot(rows[e], gu_v[e], preferred_element_type=F32)
            return both[:, 0:FFH], both[:, FFH:]

        def half_of(g, step, span):
            e = g * PER + turn(g, step)
            return jnp.dot(rows[e], gu_v[e, :, span], preferred_element_type=F32).astype(BF16)

    with jax.named_scope("gate_up"):
        for g in range(GROUPS):
            send_1[g, 5] = half_of(g, 2, slice(FFH, 2 * FFH))
        for g in range(GROUPS):
            push(send_1.at[g, 5], passing.at[g], 9 + g, first_line(g, 3))
        for g in range(GROUPS):
            send_1[g, 4] = half_of(g, 2, slice(0, FFH))
        for g in range(GROUPS):
            push(send_1.at[g, 4], recv_1.at[g, 4], 4 + g, first_line(g, 2))
        for g in range(GROUPS):
            gate, upward = gate_up(g, 1)
            send_1[g, 0] = gate.astype(BF16)
            send_1[g, 1] = upward.astype(BF16)
            gate, behind[g] = gate_up(g, 3)
            send_1[g, 2] = gate.astype(BF16)
        for g in range(GROUPS):
            push(send_1.at[g, pl.ds(0, 2)], recv_1.at[g, pl.ds(0, 2)], 4 + g, first_line(g, 1))
            push(send_1.at[g, 2], recv_1.at[g, 2], 4 + g, first_line(g, 3))
        share_squares()
        for g in range(GROUPS):
            settle(passing.at[g], recv_sem.at[9 + g])
            send_1[g, 3] = (behind[g] + passing[g].astype(F32)).astype(BF16)
            push(send_1.at[g, 3], recv_1.at[g, 3], 4 + g, first_line(g, 3))
        for g in range(GROUPS):
            own_1[g, 0], own_1[g, 1] = gate_up(g, 0)

    with jax.named_scope("square_sums"):
        settle(recv_s.at[0, pl.ds(0, SIDE - 1)], recv_sem.at[6])
        recv_s[1, sz] = jnp.sum(recv_s[0], axis=0)
        for step in OTHERS:
            push(recv_s.at[1, sz], recv_s.at[1, sz], 12, second_line(0, step))

    with jax.named_scope("first_sums"):
        for g in range(GROUPS):
            after = place(g)[1]
            settle(recv_1.at[g], recv_sem.at[4 + g])
            gate = own_1[g, 0]
            upward = own_1[g, 1]
            for c in (0, 2, 4):
                gate = gate + recv_1[g, c].astype(F32)
            for c in (1, 3):
                upward = upward + recv_1[g, c].astype(F32)
            for n in range(SIDE):
                span = slice(n * QUARTER, (n + 1) * QUARTER)
                send_2[g, n, 0:SLOTS] = gate[:, span].astype(BF16)
                send_2[g, n, SLOTS:] = upward[:, span].astype(BF16)
            for step in OTHERS:
                to = turn(1 - g, step)
                push(send_2.at[g, to], recv_2.at[g, after], 7 + g, second_line(g, step))
            recv_2[g, after] = send_2[g, after]

    with jax.named_scope("scales"):
        settle(recv_s.at[1, pl.ds(0, SIDE - 1)], recv_sem.at[12])
        scale = lax.rsqrt(jnp.sum(recv_s[1], axis=0) * (1.0 / D) + 1e-06)
        scale = jnp.concatenate(
            [jnp.broadcast_to(scale[:, b : b + 1], (R, 128)) for b in range(FFN)]
            + [jnp.zeros((64, 128), F32)],
            axis=0,
        )
        high = scale.astype(BF16)
        split = jnp.concatenate([high, (scale - high.astype(F32)).astype(BF16)], axis=1)
        owned = [
            pick[pl.ds(pl.multiple_of((g * PER + place(g)[0]) * SLOTS, SLOTS), SLOTS), :]
            for g in range(GROUPS)
        ]
        scales = jnp.dot(jnp.concatenate(owned, axis=0), split, preferred_element_type=F32)
        scales = scales[:, 0:128] + scales[:, 128:256]
        own_scales = [
            jnp.concatenate([scales[g * SLOTS : (g + 1) * SLOTS]] * (QUARTER // 128), axis=1)
            for g in range(GROUPS)
        ]

    with jax.named_scope("inner"):
        for g in range(GROUPS):
            settle(recv_2.at[g, pl.ds(0, SIDE - 1)], recv_sem.at[7 + g])
            both = recv_2[g, 0].astype(F32)
            for c in range(1, SIDE):
                both = both + recv_2[g, c].astype(F32)
            gate = both[0:SLOTS] * own_scales[g]
            upward = both[SLOTS:] * own_scales[g]
            inner = gate / (1.0 + jnp.exp(-gate)) * upward
            recv_e[sx, sz, g] = inner.astype(BF16)

    with jax.named_scope("inner_sends"):
        for dx, dz in FAR_FIRST:
            push(
                recv_e.at[sx, sz], recv_e.at[sx, sz], 13, number_x[dx] + number_z[dz], line_recv.at[sx]
            )

        def down_here(e, carry):
            pltpu.make_async_copy(d_hbm.at[e], d_v.at[e], w_sem.at[2, e]).wait()
            return carry

        lax.fori_loop(0, E_LOC, down_here, 0)

    with jax.named_scope("down"):
        for step in (0, 1, 3, 2):
            x = turn_x[step]
            settle(recv_e.at[0, pl.ds(0, SIDE if step else SIDE - 1)], line_recv.at[x])
            inner = jnp.concatenate([recv_e[x, q, 0] for q in range(SIDE)], axis=1)
            results[x] = jnp.dot(inner, d_v[x], preferred_element_type=F32).astype(BF16)
            span = pl.ds(pl.multiple_of(x * QUARTER, QUARTER), QUARTER)
            for n in range(PER):
                term = jnp.dot(recv_e[x, n, 1], d_v[PER + n, span, :], preferred_element_type=F32)
                if step:
                    term = term + partly[n]
                if step != 2:
                    partly[n] = term
                else:
                    results[PER + n] = term.astype(BF16)

    with jax.named_scope("mix"):
        found = results[...].reshape(E_LOC * SLOTS, COLS)
        mixed = jnp.dot(weigh[...], found, preferred_element_type=F32)
        mixed = mixed[0:64] + mixed[64:128]
        for b in range(FFN):
            piece = mixed[b * R : (b + 1) * R]
            send_f[b] = piece.astype(BF16)
        for step in FFN_FIRST:
            push(send_f.at[lax.rem(fx + step, FFN)], out.at[fx], 11, number_f[step])
        kept = pltpu.make_async_copy(send_f.at[fx], out.at[fx], o_sem.at[0])
        kept.start()

    with jax.named_scope("last_wait"):
        settle(send_a.at[pl.ds(0, CTX - 1)], send_sem.at[0])
        settle(recv_r.at[pl.ds(0, FFN - 1)], send_sem.at[1])
        settle(send_b.at[pl.ds(0, CTX - 1)], send_sem.at[2])
        settle(recv_c.at[pl.ds(0, FFN - 1)], send_sem.at[3])
        settle(recv_s.at[0, pl.ds(0, SIDE - 1)], send_sem.at[6])
        settle(recv_s.at[1, pl.ds(0, SIDE - 1)], send_sem.at[12])
        for g in range(GROUPS):
            settle(recv_1.at[g], send_sem.at[4 + g])
            settle(passing.at[g], send_sem.at[9 + g])
            settle(send_2.at[g, pl.ds(0, SIDE - 1)], send_sem.at[7 + g])
        settle(recv_e.at[pl.ds(0, SIDE - 1)], send_sem.at[13])
        settle(recv_e.at[0, pl.ds(0, SIDE - 1)], send_sem.at[13])
        settle(send_f.at[pl.ds(0, FFN - 1)], send_sem.at[11])

        kept.wait()
        settle(out.at[pl.ds(0, FFN - 1)], recv_sem.at[11])


def local(
    queries, key_cache, value_cache, lengths, residual, o_weight, norm_gain,
    gate_proj, up_proj, down_proj, expert_ids, route_weight,
):
    anywhere = pl.BlockSpec(memory_space=pl.ANY)
    parts = pl.pallas_call(
        kernel,
        out_shape=pltpu.VMEM((FFN, R, COLS), BF16),
        in_specs=[anywhere] * 12,
        out_specs=pl.BlockSpec(memory_space=pltpu.VMEM),
        scratch_shapes=[
            pltpu.SMEM((R,), jnp.int32),
            pltpu.VMEM((R, COLS), BF16),
            pltpu.VMEM((1, COLS), F32),
            pltpu.VMEM((R, 8), jnp.int32),
            pltpu.VMEM((R, 8), F32),
            pltpu.VMEM((R, HQ * HD), BF16),
            pltpu.VMEM((R, 128, KVH * HD), BF16),
            pltpu.VMEM((R, 128, KVH * HD), BF16),
            pltpu.VMEM((HQ * HD // CTX, D), BF16),
            pltpu.VMEM((E_LOC, COLS, 2 * FFH), BF16),
            pltpu.VMEM((E_LOC, FFH, COLS), BF16),
            pltpu.VMEM((CTX, 5, R, 128), BF16),
            pltpu.VMEM((CTX, 5, R, 128), BF16),
            pltpu.VMEM((CTX, 16, 128), BF16),
            pltpu.VMEM((CTX, 16, 128), BF16),
            pltpu.VMEM((FFN, 16, 128), BF16),
            pltpu.VMEM((FFN, R, 128), F32),
            pltpu.VMEM((2, SIDE, R, 128), F32),
            pltpu.VMEM((GROUPS, 6, SLOTS, FFH), BF16),
            pltpu.VMEM((GROUPS, SLOTS, FFH), BF16),
            pltpu.VMEM((GROUPS, SLOTS, FFH), F32),
            pltpu.VMEM((GROUPS, 2, SLOTS, FFH), F32),
            pltpu.VMEM((GROUPS, 5, SLOTS, FFH), BF16),
            pltpu.VMEM((GROUPS, SIDE, 2 * SLOTS, QUARTER), BF16),
            pltpu.VMEM((GROUPS, SIDE, 2 * SLOTS, QUARTER), BF16),
            pltpu.VMEM((SIDE, SIDE, GROUPS, SLOTS, QUARTER), BF16),
            pltpu.VMEM((FFN, R, COLS), BF16),
            pltpu.VMEM((128, 128), BF16),
            pltpu.VMEM((128, 128), BF16),
            pltpu.VMEM((E_LOC, SLOTS, COLS), BF16),
            pltpu.VMEM((E_LOC, SLOTS, COLS), BF16),
            pltpu.VMEM((PER, SLOTS, COLS), F32),
            pltpu.SemaphoreType.DMA((6,)),
            pltpu.SemaphoreType.DMA((2, 2)),
            pltpu.SemaphoreType.DMA((4,)),
            pltpu.SemaphoreType.DMA((3, E_LOC)),
            pltpu.SemaphoreType.DMA((14,)),
            pltpu.SemaphoreType.DMA((14,)),
            pltpu.SemaphoreType.DMA((SIDE,)),
        ],
        compiler_params=pltpu.CompilerParams(
            collective_id=0, has_side_effects=True, vmem_limit_bytes=56 * 2**20
        ),
        cost_estimate=pl.CostEstimate(
            flops=1_000_000_000, bytes_accessed=26_000_000, transcendentals=100_000
        ),
    )(
        lengths, residual, norm_gain.reshape(1, COLS), expert_ids, route_weight,
        queries, key_cache, value_cache, o_weight, gate_proj, up_proj, down_proj,
    )
    return jnp.sum(parts.astype(F32), axis=0).astype(BF16)


def solution(mesh):
    placed = (
        P("ffn", None),
        P("ffn", "ctx", None),
        P("ffn", "ctx", None),
        P("ffn"),
        P("ffn", "ctx"),
        P("ctx", None),
        P("ctx"),
        P("ffn", "ctx", None),
        P("ffn", "ctx", None),
        P("ffn", None, "ctx"),
        P("ffn", None),
        P("ffn", None),
    )
    return jax.shard_map(
        local, mesh=mesh, in_specs=placed, out_specs=P("ffn", "ctx"), check_vma=False
    )
```

```python
import jax
import jax.numpy as jnp
from jax import lax
from jax.experimental import pallas as pl
from jax.experimental.pallas import tpu as pltpu
from jax.sharding import PartitionSpec as P

D = 4096
HQ = 64
KVH = 4
HD = 128
FFH = 1536
MOST = 2
CTX = 16
SIDE = 4
FFN = 8
R = 8
E_LOC = 8
SLOTS = FFN * MOST
GROUPS = 2
PER = E_LOC // GROUPS
QUARTER = FFH // SIDE
COLS = D // CTX
LOGICAL = pl.DeviceIdType.LOGICAL
F32 = jnp.float32
BF16 = jnp.bfloat16


FAR_FIRST = sorted(
    ((dx, dz) for dx in range(SIDE) for dz in range(SIDE) if (dx, dz) != (0, 0)),
    key=lambda d: -(min(d[0], SIDE - d[0]) + min(d[1], SIDE - d[1])),
)
FFN_FIRST = (4, 5, 3, 2, 6, 7, 1)
OTHERS = (2, 1, 3)
BLOCKS = (2, 1, 3, 0)


def kernel(
    len_hbm, res_hbm, gain_hbm, ids_hbm, route_hbm,
    q_hbm, k_hbm, v_hbm, o_hbm, g_hbm, u_hbm, d_hbm,
    out,
    lengths, residual, gain, ids, route,
    q_v, k_v, v_v, o_v, gu_v, d_v,
    send_a, recv_a, send_b, recv_b, recv_c, recv_r, recv_s,
    send_1, passing, behind, own_1, recv_1, send_2, recv_2, recv_e, send_f,
    pick, weigh, rows, results, partly,
    in_sem, kv_sem, o_sem, w_sem, send_sem, recv_sem, line_recv,
):
    cx = lax.axis_index("ctx")
    fx = lax.axis_index("ffn")
    sx = cx // SIDE
    sz = lax.rem(cx, SIDE)

    way = 1 - 2 * lax.rem(fx, 2)
    turn_x = [lax.rem(sx + SIDE + way * step, SIDE) for step in range(SIDE)]
    turn_z = [lax.rem(sz + SIDE + way * step, SIDE) for step in range(SIDE)]
    number_x = [x * (SIDE * FFN) for x in turn_x]
    number_z = [z * FFN + fx for z in turn_z]
    number_f = [cx * FFN + lax.rem(fx + step, FFN) for step in range(FFN)]

    def every_ffn(visit):
        for step in FFN_FIRST:
            visit(number_f[step])

    def place(g):
        return (sx, sz) if g == 0 else (sz, sx)

    def turn(g, step):
        return turn_x[step] if g == 0 else turn_z[step]

    def first_line(g, step):
        return number_x[step] + number_z[0] if g == 0 else number_x[0] + number_z[step]

    def second_line(g, step):
        return first_line(1 - g, step)

    def settle(ref, sem):
        pltpu.make_async_copy(ref, ref, sem).wait()

    def push(src, dst, phase, to, recv=None):
        pltpu.make_async_remote_copy(
            src_ref=src, dst_ref=dst, send_sem=send_sem.at[phase],
            recv_sem=recv_sem.at[phase] if recv is None else recv,
            device_id=to, device_id_type=LOGICAL,
        ).start()

    with jax.named_scope("entry"):
        barrier = pltpu.get_barrier_semaphore()

        def greet(to):
            pl.semaphore_signal(barrier, inc=1, device_id=to, device_id_type=LOGICAL)

        pairs = [
            (q_hbm, q_v), (len_hbm, lengths),
            (ids_hbm, ids), (route_hbm, route), (res_hbm, residual), (gain_hbm, gain),
        ]
        first = [pltpu.make_async_copy(src, dst, in_sem.at[n]) for n, (src, dst) in enumerate(pairs)]
        first[0].start()
        kv_copies = []
        for m, (src, dst) in enumerate(((k_hbm, k_v), (v_hbm, v_v))):
            for n in range(2):
                span = pl.ds(n * (R // 2), R // 2)
                kv_copies.append(
                    pltpu.make_async_copy(src.at[span], dst.at[span], kv_sem.at[m, n])
                )
        for copy in kv_copies:
            copy.start()
        for dx, dz in FAR_FIRST:
            greet(number_x[dx] + number_z[dz])
        every_ffn(greet)
        for copy in first[1:]:
            copy.start()
        o_copies = [
            pltpu.make_async_copy(
                o_hbm.at[pl.ds(n * 128, 128)], o_v.at[pl.ds(n * 128, 128)], o_sem.at[n]
            )
            for n in range(4)
        ]


        def fetch(step):
            for g in range(GROUPS):
                e = g * PER + turn(g, step)
                pltpu.make_async_copy(g_hbm.at[e], gu_v.at[e, :, 0:FFH], w_sem.at[0, e]).start()
                pltpu.make_async_copy(u_hbm.at[e], gu_v.at[e, :, FFH:], w_sem.at[1, e]).start()

        def fetch_down(e, carry):
            pltpu.make_async_copy(d_hbm.at[e], d_v.at[e], w_sem.at[2, e]).start()
            return carry


        lane8 = lax.broadcasted_iota(jnp.int32, (R, 128), 1)
        sub8 = lax.broadcasted_iota(jnp.int32, (R, 128), 0)
        filled = jnp.zeros((R, 128), jnp.int32)
        row_r = lax.broadcasted_iota(jnp.int32, (128, 128), 0) & 7
        lane_full = lax.broadcasted_iota(jnp.int32, (1, 4, R, 128), 3)
        head4 = lax.broadcasted_iota(jnp.int32, (1, 4, R, 128), 1)
        first[1].wait()
        for r in range(R):
            filled = jnp.where(sub8 == r, lengths[r], filled)
        usable = ((cx * 128 + lane8) < filled)[None]
        first[0].wait()

        def weigh_up(k):
            part = q_v[:, k * 16 * HD : (k + 1) * 16 * HD].astype(F32)
            queries = jnp.concatenate(
                [part[:, g * HD : (g + 1) * HD] for g in range(16)], axis=0
            ).astype(BF16)
            every = lax.dot_general(
                queries, k_v[:, :, k * HD : (k + 1) * HD].reshape(R * 128, HD),
                (((1,), (1,)), ((), ())), preferred_element_type=F32,
            )
            scores = every[:, 0:128]
            for r in range(1, R):
                scores = jnp.where(row_r == r, every[:, r * 128 : (r + 1) * 128], scores)
            scores = (scores * HD ** (-0.5)).reshape(16, R, 128)
            peak = jnp.max(jnp.where(usable, scores, -1e30), axis=-1, keepdims=True)
            peak = peak.astype(BF16).astype(F32)
            probs = jnp.where(usable, jnp.exp(scores - peak), 0.0)
            probs = probs.astype(BF16).astype(F32)
            total = jnp.sum(probs, axis=-1, keepdims=True)
            peak4 = jnp.broadcast_to(peak, (16, R, 128)).reshape(4, 4, R, 128)
            total4 = jnp.broadcast_to(total, (16, R, 128)).reshape(4, 4, R, 128)
            high = total4.astype(BF16).astype(F32)
            marks = jnp.sum(
                jnp.where(lane_full == head4, peak4, 0.0)
                + jnp.where(lane_full == head4 + 4, high, 0.0)
                + jnp.where(lane_full == head4 + 8, total4 - high, 0.0),
                axis=1,
            )
            send_a[k * 4 : (k + 1) * 4, 4] = marks.astype(BF16)
            return probs.reshape(128, 128)

        def sum_up(k, flat):
            spread = jnp.concatenate(
                [jnp.where(row_r == r, flat, 0.0).astype(BF16) for r in range(R)], axis=1
            )
            values = v_v[:, :, k * HD : (k + 1) * HD].reshape(R * 128, HD)
            numerator = jnp.dot(spread, values, preferred_element_type=F32)
            send_a[k * 4 : (k + 1) * 4, 0:4] = numerator.reshape(4, 4, R, HD).astype(BF16)

    with jax.named_scope("attention"):
        kv_copies[0].wait()
        kv_copies[1].wait()
        flats = [weigh_up(k) for k in range(KVH)]
        first[2].wait()
        first[3].wait()
        table = jnp.zeros((R, 128), F32)
        ids_f = ids[...].astype(F32)
        route_f = route[...]
        for k in range(8):
            table = jnp.where(lane8 == k, ids_f[:, k : k + 1], table)
            table = jnp.where(lane8 == 8 + k, route_f[:, k : k + 1], table)
        recv_r[fx] = table
        kv_copies[2].wait()
        kv_copies[3].wait()
        for copy in o_copies:
            copy.start()
        for k in range(KVH):
            sum_up(k, flats[k])

    with jax.named_scope("attention_sends"):
        pl.semaphore_wait(barrier, CTX - 1 + FFN - 1)
        for step in BLOCKS:
            for z in OTHERS + ((0,) if step else ()):
                to = turn_x[step] * SIDE + turn_z[z]
                push(send_a.at[to], recv_a.at[cx], 0, number_x[step] + number_z[z])
        every_ffn(lambda to: push(recv_r.at[fx], recv_r.at[fx], 1, to))
        recv_a[cx] = send_a[cx]
        fetch(2)
        fetch(1)

    with jax.named_scope("routing"):
        settle(recv_r.at[pl.ds(0, FFN - 1)], recv_sem.at[1])
        tables = recv_r[...].reshape(FFN * R, 128)
        lane = lax.broadcasted_iota(jnp.int32, (FFN * R, 128), 1)
        token = lax.broadcasted_iota(jnp.int32, (FFN * R, 128), 0)
        expert = (fx * E_LOC + (lane >> 4)).astype(F32)
        chosen = jnp.zeros((FFN * R, 128), F32)
        weight = jnp.zeros((FFN * R, 128), F32)
        for k in range(8):
            hit = tables[:, k : k + 1] == expert
            chosen = jnp.where(hit, 1.0, chosen)
            weight = jnp.where(hit, tables[:, 8 + k : 9 + k], weight)
        row = lax.broadcasted_iota(jnp.int32, (64, 64), 0)
        col = lax.broadcasted_iota(jnp.int32, (64, 64), 1)
        before = jnp.where((col < row) & ((col >> 3) == (row >> 3)), 1.0, 0.0).astype(BF16)
        rank = jnp.dot(before, chosen.astype(BF16), preferred_element_type=F32)
        here = (
            (chosen > 0.5)
            & (rank == (lane & 1).astype(F32))
            & ((token >> 3) == ((lane & 15) >> 1))
        )
        here_f = jnp.where(here, 1.0, 0.0)
        padded = jnp.concatenate([here_f, jnp.zeros((64, 128), F32)], axis=0)
        pick[...] = jnp.transpose(padded).astype(BF16)
        weight = jnp.where(here, weight, 0.0)
        high = weight.astype(BF16)
        weigh[0:64] = high
        weigh[64:128] = (weight - high.astype(F32)).astype(BF16)

    with jax.named_scope("attention_wait"):
        settle(recv_a.at[pl.ds(0, CTX - 1)], recv_sem.at[0])

    with jax.named_scope("attention_combine"):
        got = recv_a[...].astype(F32)
        marks = got[:, 4]
        factor = jnp.exp(marks - jnp.max(marks, axis=0, keepdims=True))
        share = pltpu.roll(marks, 124, 2) + pltpu.roll(marks, 120, 2)
        below = jnp.sum(factor * share, axis=0)
        heads = []
        for h in range(4):
            top = jnp.zeros((R, HD), F32)
            for c in range(CTX):
                top = top + factor[c, :, h : h + 1] * got[c, h]
            heads.append(top / below[:, h : h + 1])
        attended = jnp.concatenate(heads, axis=1).astype(BF16)

        for copy in o_copies:
            copy.wait()

    with jax.named_scope("projection"):
        projected = jnp.dot(attended, o_v[...], preferred_element_type=F32)
        for c in range(CTX):
            ahead, rest = projected[:, c * 256 : c * 256 + 128], projected[:, c * 256 + 128 : c * 256 + 256]
            send_b[c] = jnp.concatenate([ahead, rest], axis=0).astype(BF16)
        for step in BLOCKS:
            for z in OTHERS + ((0,) if step else ()):
                to = turn_x[step] * SIDE + turn_z[z]
                push(send_b.at[to], recv_b.at[cx], 2, number_x[step] + number_z[z])
        recv_b[cx] = send_b[cx]
        fetch(3)
        fetch(0)

        def weights_here(e, carry):
            pltpu.make_async_copy(g_hbm.at[e], gu_v.at[e, :, 0:FFH], w_sem.at[0, e]).wait()
            pltpu.make_async_copy(u_hbm.at[e], gu_v.at[e, :, FFH:], w_sem.at[1, e]).wait()
            return carry

        first[4].wait()
        first[5].wait()
        res = residual[...].astype(F32)
        res = jnp.concatenate([res[:, 0:128], res[:, 128:256]], axis=0)

    with jax.named_scope("projection_wait"):
        settle(recv_b.at[pl.ds(0, CTX - 1)], recv_sem.at[2])

    with jax.named_scope("hidden_sends"):
        hidden = res + jnp.sum(recv_b[...].astype(F32), axis=0)
        recv_c[fx] = hidden.astype(BF16)
        every_ffn(lambda to: push(recv_c.at[fx], recv_c.at[fx], 3, to))
        lax.fori_loop(0, E_LOC, fetch_down, 0)
        lax.fori_loop(0, E_LOC, weights_here, 0)

    with jax.named_scope("hidden_wait"):
        settle(recv_c.at[pl.ds(0, FFN - 1)], recv_sem.at[3])

    with jax.named_scope("rows"):
        tokens = recv_c[...].astype(F32)
        left = tokens[:, 0:8, :].reshape(64, 128)
        right = tokens[:, 8:16, :].reshape(64, 128)
        gained = jnp.concatenate([left * gain[:, 0:128], right * gain[:, 128:256]], axis=1)
        gained = jnp.concatenate([gained, jnp.zeros((64, 256), F32)], axis=0).astype(BF16)
        rows[...] = (
            jnp.dot(pick[...], gained, preferred_element_type=F32)
            .astype(BF16)
            .reshape(E_LOC, SLOTS, COLS)
        )

        def share_squares():
            squares = jnp.sum(left * left + right * right, axis=1, keepdims=True).reshape(FFN, R, 1)
            squares = jnp.broadcast_to(squares, (FFN, R, 128))
            block = lax.broadcasted_iota(jnp.int32, (FFN, R, 128), 0)
            lanes = lax.broadcasted_iota(jnp.int32, (FFN, R, 128), 2)
            recv_s[0, sx] = jnp.sum(jnp.where(lanes == block, squares, 0.0), axis=0)
            for step in OTHERS:
                push(recv_s.at[0, sx], recv_s.at[0, sx], 6, first_line(0, step))

        def gate_up(g, step):
            e = g * PER + turn(g, step)
            both = jnp.dot(rows[e], gu_v[e], preferred_element_type=F32)
            return both[:, 0:FFH], both[:, FFH:]

    with jax.named_scope("gate_up"):
        for g in range(GROUPS):
            gate, upward = gate_up(g, 2)
            send_1[g, 4] = gate.astype(BF16)
            send_1[g, 5] = upward.astype(BF16)
        for g in range(GROUPS):
            push(send_1.at[g, 5], passing.at[g], 9 + g, first_line(g, 3))
            push(send_1.at[g, 4], recv_1.at[g, 4], 4 + g, first_line(g, 2))
        for g in range(GROUPS):
            gate, upward = gate_up(g, 1)
            send_1[g, 0] = gate.astype(BF16)
            send_1[g, 1] = upward.astype(BF16)
            gate, behind[g] = gate_up(g, 3)
            send_1[g, 2] = gate.astype(BF16)
        for g in range(GROUPS):
            push(send_1.at[g, pl.ds(0, 2)], recv_1.at[g, pl.ds(0, 2)], 4 + g, first_line(g, 1))
            push(send_1.at[g, 2], recv_1.at[g, 2], 4 + g, first_line(g, 3))
        for g in range(GROUPS):
            own_1[g, 0], own_1[g, 1] = gate_up(g, 0)
        share_squares()
        for g in range(GROUPS):
            settle(passing.at[g], recv_sem.at[9 + g])
            send_1[g, 3] = (behind[g] + passing[g].astype(F32)).astype(BF16)
            push(send_1.at[g, 3], recv_1.at[g, 3], 4 + g, first_line(g, 3))

    with jax.named_scope("square_sums"):
        settle(recv_s.at[0, pl.ds(0, SIDE - 1)], recv_sem.at[6])
        recv_s[1, sz] = jnp.sum(recv_s[0], axis=0)
        for step in OTHERS:
            push(recv_s.at[1, sz], recv_s.at[1, sz], 12, second_line(0, step))

    with jax.named_scope("first_sums"):
        for g in range(GROUPS):
            after = place(g)[1]
            settle(recv_1.at[g], recv_sem.at[4 + g])
            gate = own_1[g, 0]
            upward = own_1[g, 1]
            for c in (0, 2, 4):
                gate = gate + recv_1[g, c].astype(F32)
            for c in (1, 3):
                upward = upward + recv_1[g, c].astype(F32)
            for n in range(SIDE):
                span = slice(n * QUARTER, (n + 1) * QUARTER)
                send_2[g, n, 0:SLOTS] = gate[:, span].astype(BF16)
                send_2[g, n, SLOTS:] = upward[:, span].astype(BF16)
            for step in OTHERS:
                to = turn(1 - g, step)
                push(send_2.at[g, to], recv_2.at[g, after], 7 + g, second_line(g, step))
            recv_2[g, after] = send_2[g, after]

    with jax.named_scope("scales"):
        settle(recv_s.at[1, pl.ds(0, SIDE - 1)], recv_sem.at[12])
        scale = lax.rsqrt(jnp.sum(recv_s[1], axis=0) * (1.0 / D) + 1e-06)
        scale = jnp.concatenate(
            [jnp.broadcast_to(scale[:, b : b + 1], (R, 128)) for b in range(FFN)]
            + [jnp.zeros((64, 128), F32)],
            axis=0,
        )
        high = scale.astype(BF16)
        split = jnp.concatenate([high, (scale - high.astype(F32)).astype(BF16)], axis=1)
        owned = [
            pick[pl.ds(pl.multiple_of((g * PER + place(g)[0]) * SLOTS, SLOTS), SLOTS), :]
            for g in range(GROUPS)
        ]
        scales = jnp.dot(jnp.concatenate(owned, axis=0), split, preferred_element_type=F32)
        scales = scales[:, 0:128] + scales[:, 128:256]
        own_scales = [
            jnp.concatenate([scales[g * SLOTS : (g + 1) * SLOTS]] * (QUARTER // 128), axis=1)
            for g in range(GROUPS)
        ]

    with jax.named_scope("inner"):
        for g in range(GROUPS):
            settle(recv_2.at[g, pl.ds(0, SIDE - 1)], recv_sem.at[7 + g])
            both = recv_2[g, 0].astype(F32)
            for c in range(1, SIDE):
                both = both + recv_2[g, c].astype(F32)
            gate = both[0:SLOTS] * own_scales[g]
            upward = both[SLOTS:] * own_scales[g]
            inner = gate / (1.0 + jnp.exp(-gate)) * upward
            recv_e[sx, sz, g] = inner.astype(BF16)

    with jax.named_scope("inner_sends"):
        for dx, dz in FAR_FIRST:
            push(
                recv_e.at[sx, sz], recv_e.at[sx, sz], 13, number_x[dx] + number_z[dz], line_recv.at[sx]
            )

        def down_here(e, carry):
            pltpu.make_async_copy(d_hbm.at[e], d_v.at[e], w_sem.at[2, e]).wait()
            return carry

        lax.fori_loop(0, E_LOC, down_here, 0)

    with jax.named_scope("down"):
        for step in (0, 1, 3, 2):
            x = turn_x[step]
            settle(recv_e.at[0, pl.ds(0, SIDE if step else SIDE - 1)], line_recv.at[x])
            inner = jnp.concatenate([recv_e[x, q, 0] for q in range(SIDE)], axis=1)
            results[x] = jnp.dot(inner, d_v[x], preferred_element_type=F32).astype(BF16)
            span = pl.ds(pl.multiple_of(x * QUARTER, QUARTER), QUARTER)
            for n in range(PER):
                term = jnp.dot(recv_e[x, n, 1], d_v[PER + n, span, :], preferred_element_type=F32)
                if step:
                    term = term + partly[n]
                if step != 2:
                    partly[n] = term
                else:
                    results[PER + n] = term.astype(BF16)

    with jax.named_scope("mix"):
        found = results[...].reshape(E_LOC * SLOTS, COLS)
        mixed = jnp.dot(weigh[...], found, preferred_element_type=F32)
        mixed = mixed[0:64] + mixed[64:128]
        for b in range(FFN):
            piece = mixed[b * R : (b + 1) * R]
            send_f[b] = piece.astype(BF16)
        for step in FFN_FIRST:
            push(send_f.at[lax.rem(fx + step, FFN)], out.at[fx], 11, number_f[step])
        kept = pltpu.make_async_copy(send_f.at[fx], out.at[fx], o_sem.at[0])
        kept.start()

    with jax.named_scope("last_wait"):
        settle(send_a.at[pl.ds(0, CTX - 1)], send_sem.at[0])
        settle(recv_r.at[pl.ds(0, FFN - 1)], send_sem.at[1])
        settle(send_b.at[pl.ds(0, CTX - 1)], send_sem.at[2])
        settle(recv_c.at[pl.ds(0, FFN - 1)], send_sem.at[3])
        settle(recv_s.at[0, pl.ds(0, SIDE - 1)], send_sem.at[6])
        settle(recv_s.at[1, pl.ds(0, SIDE - 1)], send_sem.at[12])
        for g in range(GROUPS):
            settle(recv_1.at[g], send_sem.at[4 + g])
            settle(passing.at[g], send_sem.at[9 + g])
            settle(send_2.at[g, pl.ds(0, SIDE - 1)], send_sem.at[7 + g])
        settle(recv_e.at[pl.ds(0, SIDE - 1)], send_sem.at[13])
        settle(recv_e.at[0, pl.ds(0, SIDE - 1)], send_sem.at[13])
        settle(send_f.at[pl.ds(0, FFN - 1)], send_sem.at[11])

        kept.wait()
        settle(out.at[pl.ds(0, FFN - 1)], recv_sem.at[11])


def local(
    queries, key_cache, value_cache, lengths, residual, o_weight, norm_gain,
    gate_proj, up_proj, down_proj, expert_ids, route_weight,
):
    anywhere = pl.BlockSpec(memory_space=pl.ANY)
    parts = pl.pallas_call(
        kernel,
        out_shape=pltpu.VMEM((FFN, R, COLS), BF16),
        in_specs=[anywhere] * 12,
        out_specs=pl.BlockSpec(memory_space=pltpu.VMEM),
        scratch_shapes=[
            pltpu.SMEM((R,), jnp.int32),
            pltpu.VMEM((R, COLS), BF16),
            pltpu.VMEM((1, COLS), F32),
            pltpu.VMEM((R, 8), jnp.int32),
            pltpu.VMEM((R, 8), F32),
            pltpu.VMEM((R, HQ * HD), BF16),
            pltpu.VMEM((R, 128, KVH * HD), BF16),
            pltpu.VMEM((R, 128, KVH * HD), BF16),
            pltpu.VMEM((HQ * HD // CTX, D), BF16),
            pltpu.VMEM((E_LOC, COLS, 2 * FFH), BF16),
            pltpu.VMEM((E_LOC, FFH, COLS), BF16),
            pltpu.VMEM((CTX, 5, R, 128), BF16),
            pltpu.VMEM((CTX, 5, R, 128), BF16),
            pltpu.VMEM((CTX, 16, 128), BF16),
            pltpu.VMEM((CTX, 16, 128), BF16),
            pltpu.VMEM((FFN, 16, 128), BF16),
            pltpu.VMEM((FFN, R, 128), F32),
            pltpu.VMEM((2, SIDE, R, 128), F32),
            pltpu.VMEM((GROUPS, 6, SLOTS, FFH), BF16),
            pltpu.VMEM((GROUPS, SLOTS, FFH), BF16),
            pltpu.VMEM((GROUPS, SLOTS, FFH), F32),
            pltpu.VMEM((GROUPS, 2, SLOTS, FFH), F32),
            pltpu.VMEM((GROUPS, 5, SLOTS, FFH), BF16),
            pltpu.VMEM((GROUPS, SIDE, 2 * SLOTS, QUARTER), BF16),
            pltpu.VMEM((GROUPS, SIDE, 2 * SLOTS, QUARTER), BF16),
            pltpu.VMEM((SIDE, SIDE, GROUPS, SLOTS, QUARTER), BF16),
            pltpu.VMEM((FFN, R, COLS), BF16),
            pltpu.VMEM((128, 128), BF16),
            pltpu.VMEM((128, 128), BF16),
            pltpu.VMEM((E_LOC, SLOTS, COLS), BF16),
            pltpu.VMEM((E_LOC, SLOTS, COLS), BF16),
            pltpu.VMEM((PER, SLOTS, COLS), F32),
            pltpu.SemaphoreType.DMA((6,)),
            pltpu.SemaphoreType.DMA((2, 2)),
            pltpu.SemaphoreType.DMA((4,)),
            pltpu.SemaphoreType.DMA((3, E_LOC)),
            pltpu.SemaphoreType.DMA((14,)),
            pltpu.SemaphoreType.DMA((14,)),
            pltpu.SemaphoreType.DMA((SIDE,)),
        ],
        compiler_params=pltpu.CompilerParams(
            collective_id=0, has_side_effects=True, vmem_limit_bytes=56 * 2**20
        ),
        cost_estimate=pl.CostEstimate(
            flops=1_000_000_000, bytes_accessed=26_000_000, transcendentals=100_000
        ),
    )(
        lengths, residual, norm_gain.reshape(1, COLS), expert_ids, route_weight,
        queries, key_cache, value_cache, o_weight, gate_proj, up_proj, down_proj,
    )
    return jnp.sum(parts.astype(F32), axis=0).astype(BF16)


def solution(mesh):
    placed = (
        P("ffn", None),
        P("ffn", "ctx", None),
        P("ffn", "ctx", None),
        P("ffn"),
        P("ffn", "ctx"),
        P("ctx", None),
        P("ctx"),
        P("ffn", "ctx", None),
        P("ffn", "ctx", None),
        P("ffn", None, "ctx"),
        P("ffn", None),
        P("ffn", None),
    )
    return jax.shard_map(
        local, mesh=mesh, in_specs=placed, out_specs=P("ffn", "ctx"), check_vma=False
    )
```

```python
import jax
import jax.numpy as jnp
from jax import lax
from jax.experimental import pallas as pl
from jax.experimental.pallas import tpu as pltpu
from jax.sharding import PartitionSpec as P

D = 4096
HQ = 64
KVH = 4
HD = 128
FFH = 1536
MOST = 2
CTX = 16
SIDE = 4
FFN = 8
R = 8
E_LOC = 8
SLOTS = FFN * MOST
GROUPS = 2
PER = E_LOC // GROUPS
QUARTER = FFH // SIDE
COLS = D // CTX
LOGICAL = pl.DeviceIdType.LOGICAL
F32 = jnp.float32
BF16 = jnp.bfloat16


FAR_FIRST = sorted(
    ((dx, dz) for dx in range(SIDE) for dz in range(SIDE) if (dx, dz) != (0, 0)),
    key=lambda d: -(min(d[0], SIDE - d[0]) + min(d[1], SIDE - d[1])),
)
FFN_FIRST = (4, 5, 3, 2, 6, 7, 1)
OTHERS = (2, 1, 3)
BLOCKS = (2, 1, 3, 0)


def kernel(
    len_hbm, res_hbm, gain_hbm, ids_hbm, route_hbm,
    q_hbm, k_hbm, v_hbm, o_hbm, g_hbm, u_hbm, d_hbm,
    out,
    lengths, residual, gain, ids, route,
    q_v, k_v, v_v, o_v, gu_v, d_v,
    send_a, recv_a, send_b, recv_b, recv_c, recv_r, recv_s,
    send_1, passing, behind, ahead, own_1, recv_1, send_2, recv_2, recv_e, send_f,
    pick, weigh, rows, results, partly,
    in_sem, kv_sem, o_sem, w_sem, send_sem, recv_sem, line_recv,
):
    cx = lax.axis_index("ctx")
    fx = lax.axis_index("ffn")
    sx = cx // SIDE
    sz = lax.rem(cx, SIDE)

    way = 1 - 2 * lax.rem(fx, 2)
    turn_x = [lax.rem(sx + SIDE + way * step, SIDE) for step in range(SIDE)]
    turn_z = [lax.rem(sz + SIDE + way * step, SIDE) for step in range(SIDE)]
    number_x = [x * (SIDE * FFN) for x in turn_x]
    number_z = [z * FFN + fx for z in turn_z]
    number_f = [cx * FFN + lax.rem(fx + step, FFN) for step in range(FFN)]

    def every_ffn(visit):
        for step in FFN_FIRST:
            visit(number_f[step])

    def place(g):
        return (sx, sz) if g == 0 else (sz, sx)

    def turn(g, step):
        return turn_x[step] if g == 0 else turn_z[step]

    def first_line(g, step):
        return number_x[step] + number_z[0] if g == 0 else number_x[0] + number_z[step]

    def second_line(g, step):
        return first_line(1 - g, step)

    def settle(ref, sem):
        pltpu.make_async_copy(ref, ref, sem).wait()

    def push(src, dst, phase, to, recv=None):
        pltpu.make_async_remote_copy(
            src_ref=src, dst_ref=dst, send_sem=send_sem.at[phase],
            recv_sem=recv_sem.at[phase] if recv is None else recv,
            device_id=to, device_id_type=LOGICAL,
        ).start()

    with jax.named_scope("entry"):
        barrier = pltpu.get_barrier_semaphore()

        def greet(to):
            pl.semaphore_signal(barrier, inc=1, device_id=to, device_id_type=LOGICAL)

        pairs = [
            (q_hbm, q_v), (len_hbm, lengths),
            (ids_hbm, ids), (route_hbm, route), (res_hbm, residual), (gain_hbm, gain),
        ]
        first = [pltpu.make_async_copy(src, dst, in_sem.at[n]) for n, (src, dst) in enumerate(pairs)]
        for copy in first[:4]:
            copy.start()
        kv_copies = []
        for m, (src, dst) in enumerate(((k_hbm, k_v), (v_hbm, v_v))):
            for n in range(2):
                span = pl.ds(n * (R // 2), R // 2)
                kv_copies.append(
                    pltpu.make_async_copy(src.at[span], dst.at[span], kv_sem.at[m, n])
                )
        for copy in kv_copies:
            copy.start()
        for copy in first[4:]:
            copy.start()
        for dx, dz in FAR_FIRST:
            greet(number_x[dx] + number_z[dz])
        every_ffn(greet)
        o_copies = [
            pltpu.make_async_copy(
                o_hbm.at[pl.ds(n * 128, 128)], o_v.at[pl.ds(n * 128, 128)], o_sem.at[n]
            )
            for n in range(4)
        ]


        def fetch(step):
            for g in range(GROUPS):
                e = g * PER + turn(g, step)
                pltpu.make_async_copy(g_hbm.at[e], gu_v.at[e, :, 0:FFH], w_sem.at[0, e]).start()
                pltpu.make_async_copy(u_hbm.at[e], gu_v.at[e, :, FFH:], w_sem.at[1, e]).start()

        def fetch_down(e, carry):
            pltpu.make_async_copy(d_hbm.at[e], d_v.at[e], w_sem.at[2, e]).start()
            return carry


        lane8 = lax.broadcasted_iota(jnp.int32, (R, 128), 1)
        sub8 = lax.broadcasted_iota(jnp.int32, (R, 128), 0)
        filled = jnp.zeros((R, 128), jnp.int32)
        row_r = lax.broadcasted_iota(jnp.int32, (128, 128), 0) & 7
        lane_full = lax.broadcasted_iota(jnp.int32, (1, 4, R, 128), 3)
        head4 = lax.broadcasted_iota(jnp.int32, (1, 4, R, 128), 1)
        first[2].wait()
        first[3].wait()
        table = jnp.zeros((R, 128), F32)
        ids_f = ids[...].astype(F32)
        route_f = route[...]
        for k in range(8):
            table = jnp.where(lane8 == k, ids_f[:, k : k + 1], table)
            table = jnp.where(lane8 == 8 + k, route_f[:, k : k + 1], table)
        recv_r[fx] = table
        first[1].wait()
        for r in range(R):
            filled = jnp.where(sub8 == r, lengths[r], filled)
        usable = ((cx * 128 + lane8) < filled)[None]
        first[0].wait()

        def weigh_up(k):
            part = q_v[:, k * 16 * HD : (k + 1) * 16 * HD].astype(F32)
            queries = jnp.concatenate(
                [part[:, g * HD : (g + 1) * HD] for g in range(16)], axis=0
            ).astype(BF16)
            every = lax.dot_general(
                queries, k_v[:, :, k * HD : (k + 1) * HD].reshape(R * 128, HD),
                (((1,), (1,)), ((), ())), preferred_element_type=F32,
            )
            scores = every[:, 0:128]
            for r in range(1, R):
                scores = jnp.where(row_r == r, every[:, r * 128 : (r + 1) * 128], scores)
            scores = (scores * HD ** (-0.5)).reshape(16, R, 128)
            peak = jnp.max(jnp.where(usable, scores, -1e30), axis=-1, keepdims=True)
            peak = peak.astype(BF16).astype(F32)
            probs = jnp.where(usable, jnp.exp(scores - peak), 0.0)
            probs = probs.astype(BF16).astype(F32)
            total = jnp.sum(probs, axis=-1, keepdims=True)
            peak4 = jnp.broadcast_to(peak, (16, R, 128)).reshape(4, 4, R, 128)
            total4 = jnp.broadcast_to(total, (16, R, 128)).reshape(4, 4, R, 128)
            high = total4.astype(BF16).astype(F32)
            marks = jnp.sum(
                jnp.where(lane_full == head4, peak4, 0.0)
                + jnp.where(lane_full == head4 + 4, high, 0.0)
                + jnp.where(lane_full == head4 + 8, total4 - high, 0.0),
                axis=1,
            )
            send_a[k * 4 : (k + 1) * 4, 4] = marks.astype(BF16)
            return probs.reshape(128, 128)

        def sum_up(k, flat):
            spread = jnp.concatenate(
                [jnp.where(row_r == r, flat, 0.0).astype(BF16) for r in range(R)], axis=1
            )
            values = v_v[:, :, k * HD : (k + 1) * HD].reshape(R * 128, HD)
            numerator = jnp.dot(spread, values, preferred_element_type=F32)
            send_a[k * 4 : (k + 1) * 4, 0:4] = numerator.reshape(4, 4, R, HD).astype(BF16)

    with jax.named_scope("attention"):
        kv_copies[0].wait()
        kv_copies[1].wait()
        flats = [weigh_up(k) for k in range(KVH)]
        kv_copies[2].wait()
        kv_copies[3].wait()
        for copy in o_copies:
            copy.start()
        for k in range(KVH):
            sum_up(k, flats[k])

    with jax.named_scope("attention_sends"):
        pl.semaphore_wait(barrier, CTX - 1 + FFN - 1)
        for step in BLOCKS:
            for z in OTHERS + ((0,) if step else ()):
                to = turn_x[step] * SIDE + turn_z[z]
                push(send_a.at[to], recv_a.at[cx], 0, number_x[step] + number_z[z])
        every_ffn(lambda to: push(recv_r.at[fx], recv_r.at[fx], 1, to))
        recv_a[cx] = send_a[cx]
        fetch(2)
        fetch(1)

    with jax.named_scope("routing"):
        settle(recv_r.at[pl.ds(0, FFN - 1)], recv_sem.at[1])
        tables = recv_r[...].reshape(FFN * R, 128)
        lane = lax.broadcasted_iota(jnp.int32, (FFN * R, 128), 1)
        token = lax.broadcasted_iota(jnp.int32, (FFN * R, 128), 0)
        expert = (fx * E_LOC + (lane >> 4)).astype(F32)
        chosen = jnp.zeros((FFN * R, 128), F32)
        weight = jnp.zeros((FFN * R, 128), F32)
        for k in range(8):
            hit = tables[:, k : k + 1] == expert
            chosen = jnp.where(hit, 1.0, chosen)
            weight = jnp.where(hit, tables[:, 8 + k : 9 + k], weight)
        row = lax.broadcasted_iota(jnp.int32, (64, 64), 0)
        col = lax.broadcasted_iota(jnp.int32, (64, 64), 1)
        before = jnp.where((col < row) & ((col >> 3) == (row >> 3)), 1.0, 0.0).astype(BF16)
        rank = jnp.dot(before, chosen.astype(BF16), preferred_element_type=F32)
        here = (
            (chosen > 0.5)
            & (rank == (lane & 1).astype(F32))
            & ((token >> 3) == ((lane & 15) >> 1))
        )
        here_f = jnp.where(here, 1.0, 0.0)
        padded = jnp.concatenate([here_f, jnp.zeros((64, 128), F32)], axis=0)
        pick[...] = jnp.transpose(padded).astype(BF16)
        weight = jnp.where(here, weight, 0.0)
        high = weight.astype(BF16)
        weigh[0:64] = high
        weigh[64:128] = (weight - high.astype(F32)).astype(BF16)

    with jax.named_scope("attention_wait"):
        settle(recv_a.at[pl.ds(0, CTX - 1)], recv_sem.at[0])

    with jax.named_scope("attention_combine"):
        got = recv_a[...].astype(F32)
        marks = got[:, 4]
        factor = jnp.exp(marks - jnp.max(marks, axis=0, keepdims=True))
        share = pltpu.roll(marks, 124, 2) + pltpu.roll(marks, 120, 2)
        below = jnp.sum(factor * share, axis=0)
        heads = []
        for h in range(4):
            top = jnp.zeros((R, HD), F32)
            for c in range(CTX):
                top = top + factor[c, :, h : h + 1] * got[c, h]
            heads.append(top / below[:, h : h + 1])
        attended = jnp.concatenate(heads, axis=1).astype(BF16)

        for copy in o_copies:
            copy.wait()

    with jax.named_scope("projection"):
        projected = jnp.dot(attended, o_v[...], preferred_element_type=F32)
        for c in range(CTX):
            first_half, rest = projected[:, c * 256 : c * 256 + 128], projected[:, c * 256 + 128 : c * 256 + 256]
            send_b[c] = jnp.concatenate([first_half, rest], axis=0).astype(BF16)
        for step in BLOCKS:
            for z in OTHERS + ((0,) if step else ()):
                to = turn_x[step] * SIDE + turn_z[z]
                push(send_b.at[to], recv_b.at[cx], 2, number_x[step] + number_z[z])
        recv_b[cx] = send_b[cx]
        fetch(3)
        fetch(0)

        def weights_here(e, carry):
            pltpu.make_async_copy(g_hbm.at[e], gu_v.at[e, :, 0:FFH], w_sem.at[0, e]).wait()
            pltpu.make_async_copy(u_hbm.at[e], gu_v.at[e, :, FFH:], w_sem.at[1, e]).wait()
            return carry

        first[4].wait()
        first[5].wait()
        res = residual[...].astype(F32)
        res = jnp.concatenate([res[:, 0:128], res[:, 128:256]], axis=0)

    with jax.named_scope("projection_wait"):
        settle(recv_b.at[pl.ds(0, CTX - 1)], recv_sem.at[2])

    with jax.named_scope("hidden_sends"):
        hidden = res + jnp.sum(recv_b[...].astype(F32), axis=0)
        recv_c[fx] = hidden.astype(BF16)
        every_ffn(lambda to: push(recv_c.at[fx], recv_c.at[fx], 3, to))
        lax.fori_loop(0, E_LOC, fetch_down, 0)
        lax.fori_loop(0, E_LOC, weights_here, 0)

    with jax.named_scope("hidden_wait"):
        settle(recv_c.at[pl.ds(0, FFN - 1)], recv_sem.at[3])

    with jax.named_scope("rows"):
        tokens = recv_c[...].astype(F32)
        left = tokens[:, 0:8, :].reshape(64, 128)
        right = tokens[:, 8:16, :].reshape(64, 128)
        gained = jnp.concatenate([left * gain[:, 0:128], right * gain[:, 128:256]], axis=1)
        gained = jnp.concatenate([gained, jnp.zeros((64, 256), F32)], axis=0).astype(BF16)
        rows[...] = (
            jnp.dot(pick[...], gained, preferred_element_type=F32)
            .astype(BF16)
            .reshape(E_LOC, SLOTS, COLS)
        )

        def share_squares():
            squares = jnp.sum(left * left + right * right, axis=1, keepdims=True).reshape(FFN, R, 1)
            squares = jnp.broadcast_to(squares, (FFN, R, 128))
            block = lax.broadcasted_iota(jnp.int32, (FFN, R, 128), 0)
            lanes = lax.broadcasted_iota(jnp.int32, (FFN, R, 128), 2)
            recv_s[0, sx] = jnp.sum(jnp.where(lanes == block, squares, 0.0), axis=0)
            for step in OTHERS:
                push(recv_s.at[0, sx], recv_s.at[0, sx], 6, first_line(0, step))

        def gate_up(g, step):
            e = g * PER + turn(g, step)
            both = jnp.dot(rows[e], gu_v[e], preferred_element_type=F32)
            return both[:, 0:FFH], both[:, FFH:]

    with jax.named_scope("gate_up"):
        for g in range(GROUPS):
            gate, upward = gate_up(g, 2)
            send_1[g, 4] = gate.astype(BF16)
            send_1[g, 5] = upward.astype(BF16)
        for g in range(GROUPS):
            push(send_1.at[g, 5], passing.at[g, 0], 9 + g, first_line(g, 3))
            push(send_1.at[g, 4], passing.at[g, 1], 9 + g, first_line(g, 1))
        for g in range(GROUPS):
            ahead[g], upward = gate_up(g, 1)
            send_1[g, 1] = upward.astype(BF16)
            gate, behind[g] = gate_up(g, 3)
            send_1[g, 2] = gate.astype(BF16)
        for g in range(GROUPS):
            push(send_1.at[g, 1], recv_1.at[g, 1], 4 + g, first_line(g, 1))
            push(send_1.at[g, 2], recv_1.at[g, 2], 4 + g, first_line(g, 3))
        for g in range(GROUPS):
            own_1[g, 0], own_1[g, 1] = gate_up(g, 0)
        share_squares()
        for g in range(GROUPS):
            settle(passing.at[g], recv_sem.at[9 + g])
            send_1[g, 3] = (behind[g] + passing[g, 0].astype(F32)).astype(BF16)
            send_1[g, 0] = (ahead[g] + passing[g, 1].astype(F32)).astype(BF16)
            push(send_1.at[g, 3], recv_1.at[g, 3], 4 + g, first_line(g, 3))
            push(send_1.at[g, 0], recv_1.at[g, 0], 4 + g, first_line(g, 1))

    with jax.named_scope("square_sums"):
        settle(recv_s.at[0, pl.ds(0, SIDE - 1)], recv_sem.at[6])
        recv_s[1, sz] = jnp.sum(recv_s[0], axis=0)
        for step in OTHERS:
            push(recv_s.at[1, sz], recv_s.at[1, sz], 12, second_line(0, step))

    with jax.named_scope("first_sums"):
        for g in range(GROUPS):
            after = place(g)[1]
            settle(recv_1.at[g], recv_sem.at[4 + g])
            gate = own_1[g, 0]
            upward = own_1[g, 1]
            for c in (0, 2):
                gate = gate + recv_1[g, c].astype(F32)
            for c in (1, 3):
                upward = upward + recv_1[g, c].astype(F32)
            for n in range(SIDE):
                span = slice(n * QUARTER, (n + 1) * QUARTER)
                send_2[g, n, 0:SLOTS] = gate[:, span].astype(BF16)
                send_2[g, n, SLOTS:] = upward[:, span].astype(BF16)
            for step in OTHERS:
                to = turn(1 - g, step)
                push(send_2.at[g, to], recv_2.at[g, after], 7 + g, second_line(g, step))
            recv_2[g, after] = send_2[g, after]

    with jax.named_scope("scales"):
        settle(recv_s.at[1, pl.ds(0, SIDE - 1)], recv_sem.at[12])
        scale = lax.rsqrt(jnp.sum(recv_s[1], axis=0) * (1.0 / D) + 1e-06)
        scale = jnp.concatenate(
            [jnp.broadcast_to(scale[:, b : b + 1], (R, 128)) for b in range(FFN)]
            + [jnp.zeros((64, 128), F32)],
            axis=0,
        )
        high = scale.astype(BF16)
        split = jnp.concatenate([high, (scale - high.astype(F32)).astype(BF16)], axis=1)
        owned = [
            pick[pl.ds(pl.multiple_of((g * PER + place(g)[0]) * SLOTS, SLOTS), SLOTS), :]
            for g in range(GROUPS)
        ]
        scales = jnp.dot(jnp.concatenate(owned, axis=0), split, preferred_element_type=F32)
        scales = scales[:, 0:128] + scales[:, 128:256]
        own_scales = [
            jnp.concatenate([scales[g * SLOTS : (g + 1) * SLOTS]] * (QUARTER // 128), axis=1)
            for g in range(GROUPS)
        ]

    with jax.named_scope("inner"):
        for g in range(GROUPS):
            settle(recv_2.at[g, pl.ds(0, SIDE - 1)], recv_sem.at[7 + g])
            both = recv_2[g, 0].astype(F32)
            for c in range(1, SIDE):
                both = both + recv_2[g, c].astype(F32)
            gate = both[0:SLOTS] * own_scales[g]
            upward = both[SLOTS:] * own_scales[g]
            inner = gate / (1.0 + jnp.exp(-gate)) * upward
            recv_e[sx, sz, g] = inner.astype(BF16)

    with jax.named_scope("inner_sends"):
        for dx, dz in FAR_FIRST:
            push(
                recv_e.at[sx, sz], recv_e.at[sx, sz], 13, number_x[dx] + number_z[dz], line_recv.at[sx]
            )

        def down_here(e, carry):
            pltpu.make_async_copy(d_hbm.at[e], d_v.at[e], w_sem.at[2, e]).wait()
            return carry

        lax.fori_loop(0, E_LOC, down_here, 0)

    with jax.named_scope("down"):
        for step in (0, 1, 3, 2):
            x = turn_x[step]
            settle(recv_e.at[0, pl.ds(0, SIDE if step else SIDE - 1)], line_recv.at[x])
            inner = jnp.concatenate([recv_e[x, q, 0] for q in range(SIDE)], axis=1)
            results[x] = jnp.dot(inner, d_v[x], preferred_element_type=F32).astype(BF16)
            span = pl.ds(pl.multiple_of(x * QUARTER, QUARTER), QUARTER)
            for n in range(PER):
                term = jnp.dot(recv_e[x, n, 1], d_v[PER + n, span, :], preferred_element_type=F32)
                if step:
                    term = term + partly[n]
                if step != 2:
                    partly[n] = term
                else:
                    results[PER + n] = term.astype(BF16)

    with jax.named_scope("mix"):
        found = results[...].reshape(E_LOC * SLOTS, COLS)
        mixed = jnp.dot(weigh[...], found, preferred_element_type=F32)
        mixed = mixed[0:64] + mixed[64:128]
        for b in range(FFN):
            piece = mixed[b * R : (b + 1) * R]
            send_f[b] = piece.astype(BF16)
        for step in FFN_FIRST:
            push(send_f.at[lax.rem(fx + step, FFN)], out.at[fx], 11, number_f[step])
        kept = pltpu.make_async_copy(send_f.at[fx], out.at[fx], o_sem.at[0])
        kept.start()

    with jax.named_scope("last_wait"):
        settle(send_a.at[pl.ds(0, CTX - 1)], send_sem.at[0])
        settle(recv_r.at[pl.ds(0, FFN - 1)], send_sem.at[1])
        settle(send_b.at[pl.ds(0, CTX - 1)], send_sem.at[2])
        settle(recv_c.at[pl.ds(0, FFN - 1)], send_sem.at[3])
        settle(recv_s.at[0, pl.ds(0, SIDE - 1)], send_sem.at[6])
        settle(recv_s.at[1, pl.ds(0, SIDE - 1)], send_sem.at[12])
        for g in range(GROUPS):
            settle(recv_1.at[g], send_sem.at[4 + g])
            settle(passing.at[g], send_sem.at[9 + g])
            settle(send_2.at[g, pl.ds(0, SIDE - 1)], send_sem.at[7 + g])
        settle(recv_e.at[pl.ds(0, SIDE - 1)], send_sem.at[13])
        settle(recv_e.at[0, pl.ds(0, SIDE - 1)], send_sem.at[13])
        settle(send_f.at[pl.ds(0, FFN - 1)], send_sem.at[11])

        kept.wait()
        settle(out.at[pl.ds(0, FFN - 1)], recv_sem.at[11])


def local(
    queries, key_cache, value_cache, lengths, residual, o_weight, norm_gain,
    gate_proj, up_proj, down_proj, expert_ids, route_weight,
):
    anywhere = pl.BlockSpec(memory_space=pl.ANY)
    parts = pl.pallas_call(
        kernel,
        out_shape=pltpu.VMEM((FFN, R, COLS), BF16),
        in_specs=[anywhere] * 12,
        out_specs=pl.BlockSpec(memory_space=pltpu.VMEM),
        scratch_shapes=[
            pltpu.SMEM((R,), jnp.int32),
            pltpu.VMEM((R, COLS), BF16),
            pltpu.VMEM((1, COLS), F32),
            pltpu.VMEM((R, 8), jnp.int32),
            pltpu.VMEM((R, 8), F32),
            pltpu.VMEM((R, HQ * HD), BF16),
            pltpu.VMEM((R, 128, KVH * HD), BF16),
            pltpu.VMEM((R, 128, KVH * HD), BF16),
            pltpu.VMEM((HQ * HD // CTX, D), BF16),
            pltpu.VMEM((E_LOC, COLS, 2 * FFH), BF16),
            pltpu.VMEM((E_LOC, FFH, COLS), BF16),
            pltpu.VMEM((CTX, 5, R, 128), BF16),
            pltpu.VMEM((CTX, 5, R, 128), BF16),
            pltpu.VMEM((CTX, 16, 128), BF16),
            pltpu.VMEM((CTX, 16, 128), BF16),
            pltpu.VMEM((FFN, 16, 128), BF16),
            pltpu.VMEM((FFN, R, 128), F32),
            pltpu.VMEM((2, SIDE, R, 128), F32),
            pltpu.VMEM((GROUPS, 6, SLOTS, FFH), BF16),
            pltpu.VMEM((GROUPS, 2, SLOTS, FFH), BF16),
            pltpu.VMEM((GROUPS, SLOTS, FFH), F32),
            pltpu.VMEM((GROUPS, SLOTS, FFH), F32),
            pltpu.VMEM((GROUPS, 2, SLOTS, FFH), F32),
            pltpu.VMEM((GROUPS, 4, SLOTS, FFH), BF16),
            pltpu.VMEM((GROUPS, SIDE, 2 * SLOTS, QUARTER), BF16),
            pltpu.VMEM((GROUPS, SIDE, 2 * SLOTS, QUARTER), BF16),
            pltpu.VMEM((SIDE, SIDE, GROUPS, SLOTS, QUARTER), BF16),
            pltpu.VMEM((FFN, R, COLS), BF16),
            pltpu.VMEM((128, 128), BF16),
            pltpu.VMEM((128, 128), BF16),
            pltpu.VMEM((E_LOC, SLOTS, COLS), BF16),
            pltpu.VMEM((E_LOC, SLOTS, COLS), BF16),
            pltpu.VMEM((PER, SLOTS, COLS), F32),
            pltpu.SemaphoreType.DMA((6,)),
            pltpu.SemaphoreType.DMA((2, 2)),
            pltpu.SemaphoreType.DMA((4,)),
            pltpu.SemaphoreType.DMA((3, E_LOC)),
            pltpu.SemaphoreType.DMA((14,)),
            pltpu.SemaphoreType.DMA((14,)),
            pltpu.SemaphoreType.DMA((SIDE,)),
        ],
        compiler_params=pltpu.CompilerParams(
            collective_id=0, has_side_effects=True, vmem_limit_bytes=56 * 2**20
        ),
        cost_estimate=pl.CostEstimate(
            flops=1_000_000_000, bytes_accessed=26_000_000, transcendentals=100_000
        ),
    )(
        lengths, residual, norm_gain.reshape(1, COLS), expert_ids, route_weight,
        queries, key_cache, value_cache, o_weight, gate_proj, up_proj, down_proj,
    )
    return jnp.sum(parts.astype(F32), axis=0).astype(BF16)


def solution(mesh):
    placed = (
        P("ffn", None),
        P("ffn", "ctx", None),
        P("ffn", "ctx", None),
        P("ffn"),
        P("ffn", "ctx"),
        P("ctx", None),
        P("ctx"),
        P("ffn", "ctx", None),
        P("ffn", "ctx", None),
        P("ffn", None, "ctx"),
        P("ffn", None),
        P("ffn", None),
    )
    return jax.shard_map(
        local, mesh=mesh, in_specs=placed, out_specs=P("ffn", "ctx"), check_vma=False
    )
```
